32 devices in a mesh: pair: 2 (over x), row: 4 (over y, core), col: 4 (over z).
Axes of the slice: x: 2, y: 2, z: 4, core: 2. Of those that a mesh axis runs over, the one named last changes fastest.
Arguments:
- queries: bfloat16 [4, 8, 8, 32, 2304], P('pair', None, 'row', 'col'), may hold values from -5 to 5
- key_states: bfloat16 [4, 8, 8, 32, 2304], P('pair', None, 'row', 'col'), may hold values from -5 to 5
- value_states: bfloat16 [4, 8, 8, 32, 2304], P('pair', None, 'row', 'col'), may hold values from -6 to 6
- tile_mask: int32 [2, 4, 4, 9], P('pair', 'row', 'col'), may hold values 0 or 1
- frame_reach: int32 [18], replicated, may hold values from 0 to 7
- out_weight: bfloat16 [2, 2304, 3072], P(None, 'pair'), may hold values from -0.125 to 0.125
Outputs:
- attended: bfloat16 [4, 8, 8, 32, 3072], P('pair', None, 'row', 'col')
The draws below stay inside these ranges and needn't reach their ends.
All inputs are finite; a program needn't handle non-finite values. No bound on the sum of `tile_mask` on one device may be relied on, other than what follows from the above.
Results may differ from the reference program's by a relative error of at most 0.0095.
Values may be sent and summed in bfloat16 or wider, within the bound.
No kernel may reach another device: no remote copies, remote signals or barrier semaphores. Data moves between devices by JAX's collectives and lax.ppermute only.
A program may use at most 256 MiB of HBM per device.

```python
import jax
import jax.numpy as jnp
from jax import lax

D = 3072
HEADS = 18
HEAD_DIM = 128
FRAMES = 8
ROWS_DEV = 2
COLS_DEV = 8
HD = 2304
CLIPS = 2
STREAMS = 4
TILE_ROWS = 4
TILE_COLS = 4
FRAME_H = 8
FRAME_W = 32


def draw_queries(key, part):
    key = jax.random.fold_in(key, 5)
    full_shape = (STREAMS, FRAMES, FRAME_H, FRAME_W, HEADS, HEAD_DIM)
    result = jnp.clip(jax.random.normal(key, full_shape, jnp.float32), -5.0, 5.0)
    return result.reshape(STREAMS, FRAMES, FRAME_H, FRAME_W, HEADS * HEAD_DIM).astype(jnp.bfloat16)


def draw_key_states(key, part):
    key = jax.random.fold_in(key, 9)
    full_shape = (STREAMS, FRAMES, FRAME_H, FRAME_W, HEADS, HEAD_DIM)
    result = jnp.clip(jax.random.normal(key, full_shape, jnp.float32), -5.0, 5.0)
    return result.reshape(STREAMS, FRAMES, FRAME_H, FRAME_W, HEADS * HEAD_DIM).astype(jnp.bfloat16)


def place_ends(entries, key, smallest, top_value):
    index_at = [jax.random.randint(jax.random.fold_in(key, axis), (), 0, length) for axis, length in enumerate(entries.shape)]
    widest = entries.shape.index(max(entries.shape))
    next_to = index_at[:widest] + [(index_at[widest] + 1) % entries.shape[widest]] + index_at[widest + 1:]
    return entries.at[tuple(index_at)].set(smallest).at[tuple(next_to)].set(top_value)


def levels(own_key, extent, cuts, smallest, largest):
    def one(position, blocks):
        draws = jax.random.uniform(jax.random.fold_in(jax.random.fold_in(own_key, 6), position), (blocks,), jnp.float32, smallest / len(cuts), largest / len(cuts))
        return jnp.repeat(jnp.exp(draws), extent[position] // blocks).reshape((-1,) + (1,) * (len(extent) - position - 1))

    level = one(*cuts[0])
    for cut in cuts[1:]:
        level = level * one(*cut)
    return level


def bell_draw(key, extent, scale, bound, pieces=(), kind=jnp.bfloat16):
    values = scale * jax.random.normal(key, extent, jnp.float32)
    if pieces:
        values = values * levels(key, extent, pieces, -0.22, 0.18)
    return jnp.clip(values, -bound, bound).astype(kind)


def setup_inputs(seed: int = 0) -> dict:
    keys = jax.random.split(jax.random.key(seed), 7)
    return {
        "queries": draw_queries(jax.random.fold_in(keys[6], 71), 0),
        "key_states": draw_key_states(jax.random.fold_in(keys[6], 71), 0),
        "value_states": bell_draw(keys[2], (STREAMS, FRAMES, FRAME_H, FRAME_W, HD), 1.0, 6.0, ((0, 2), (2, 4), (3, 4))),
        "tile_mask": place_ends((jax.random.randint(keys[3], (CLIPS, TILE_ROWS, TILE_COLS, 9), 0, 2) < 1).astype(jnp.int32), jax.random.fold_in(keys[3], 1), 0, 1),
        "frame_reach": place_ends(jax.random.randint(keys[4], (HEADS,), 0, FRAMES), jax.random.fold_in(keys[4], 1), 0, FRAMES - 1).astype(jnp.int32),
        "out_weight": bell_draw(keys[5], (2, HD, D), HD ** -0.5, 0.125, ((1, 2),)),
    }


def softmax_rows(scores):
    row_max = jnp.max(scores, axis=-1, keepdims=True)
    weights = jnp.exp(scores - row_max)
    row_total = jnp.sum(weights, axis=-1, keepdims=True)
    return (weights / row_total).astype(jnp.bfloat16)


def window_attend(query_rows, key_rows, value_rows, tile_ok, frame_reach):
    S, F, R, C, width = query_rows.shape
    head_count = frame_reach.shape[0]
    head_size = width // head_count
    query_heads = query_rows.astype(jnp.float32).reshape(S, F * R * C, head_count, head_size)
    key_heads = key_rows.astype(jnp.float32).reshape(S, -1, head_count, head_size)
    value_heads = value_rows.astype(jnp.float32).reshape(S, -1, head_count, head_size)
    scores = jnp.einsum("sqhd,skhd->shqk", query_heads, key_heads) * (head_size ** -0.5)
    frames = jnp.arange(F, dtype=jnp.int32)
    frame_gap = jnp.abs(frames[:, None] - frames[None, :])
    close = frame_gap[None, :, :] <= frame_reach[:, None, None]
    allowed = close[:, :, None, :, None, None, None, None] & tile_ok[None, None, None, None, :, None, :, None]
    allowed = jnp.broadcast_to(allowed, (head_count, F, R * C, F, 3, R, 3, C)).reshape(head_count, F * R * C, -1)
    scores = jnp.where(allowed[None], scores, -1e30)
    weights_bf = softmax_rows(scores)
    result = jnp.einsum("shqk,skhd->sqhd", weights_bf.astype(jnp.float32), value_heads)
    return result.reshape(S, F, R, C, width)


def axial_attend(query_rows, key_rows, value_rows, head_count):
    S, F, R, C, width = query_rows.shape
    head_size = width // head_count
    query_heads = query_rows.astype(jnp.float32).reshape(S, F, R, C, head_count, head_size)
    key_heads = key_rows.astype(jnp.float32).reshape(S, F, R, -1, head_count, head_size)
    value_heads = value_rows.astype(jnp.float32).reshape(S, F, R, -1, head_count, head_size)
    scores = jnp.einsum("sfrchd,sfrwhd->sfrhcw", query_heads, key_heads) * (head_size ** -0.5)
    weights_bf = softmax_rows(scores)
    result = jnp.einsum("sfrhcw,sfrwhd->sfrchd", weights_bf.astype(jnp.float32), value_heads)
    return result.reshape(S, F, R, C, width)


def stream_output(query_clip, key_clip, value_clip, clip_mask, frame_reach, model_weight, tile_rows, tile_cols):
    F, H, W, width = query_clip.shape
    R = H // tile_rows
    C = W // tile_cols
    margins = ((0, 0), (R, R), (C, C), (0, 0))
    key_padded = jnp.pad(key_clip, margins)
    value_padded = jnp.pad(value_clip, margins)
    offsets = jnp.arange(3, dtype=jnp.int32) - 1
    center = (offsets[:, None] == 0) & (offsets[None, :] == 0)
    anchor = jnp.zeros((), jnp.int32)

    def one_tile(tile_index):
        i = (tile_index // tile_cols).astype(jnp.int32)
        j = (tile_index % tile_cols).astype(jnp.int32)
        query_tile = lax.dynamic_slice(query_clip, (anchor, i * R, j * C, anchor), (F, R, C, width))
        key_tile = lax.dynamic_slice(key_padded, (anchor, i * R, j * C, anchor), (F, 3 * R, 3 * C, width))
        value_tile = lax.dynamic_slice(value_padded, (anchor, i * R, j * C, anchor), (F, 3 * R, 3 * C, width))
        listed = lax.dynamic_slice(clip_mask, (i, j, anchor), (1, 1, 9)).reshape(3, 3) > 0
        row_inside = (i + offsets >= 0) & (i + offsets < tile_rows)
        col_inside = (j + offsets >= 0) & (j + offsets < tile_cols)
        tile_ok = (listed | center) & row_inside[:, None] & col_inside[None, :]
        result = window_attend(query_tile[None], key_tile.reshape(1, F, 3, R, 3, C, width),
                               value_tile.reshape(1, F, 3, R, 3, C, width), tile_ok, frame_reach)
        return result[0]

    tile_outs = lax.map(one_tile, jnp.arange(tile_rows * tile_cols, dtype=jnp.int32))
    window_out = tile_outs.reshape(tile_rows, tile_cols, F, R, C, width).transpose(2, 0, 3, 1, 4, 5).reshape(F, H, W, width)
    axial_out = axial_attend(query_clip[None], key_clip[None], value_clip[None], frame_reach.shape[0])[0]
    combined = (window_out + axial_out).astype(jnp.bfloat16).reshape(-1, width)
    projected = jnp.dot(combined, model_weight, preferred_element_type=jnp.float32)
    return projected.astype(jnp.bfloat16).reshape(F, H, W, -1)


def reference(queries, key_states, value_states, tile_mask, frame_reach, out_weight):
    tile_rows = FRAME_H // ROWS_DEV
    tile_cols = FRAME_W // COLS_DEV
    outputs = []
    for stream in range(STREAMS):
        outputs.append(stream_output(queries[stream], key_states[stream], value_states[stream],
                                     tile_mask[stream // 2], frame_reach, out_weight[stream % 2],
                                     tile_rows, tile_cols))
    return jnp.stack(outputs)
```

```python
import functools
import math

import jax
import jax.numpy as jnp
from jax import lax
from jax.experimental import pallas as pl
from jax.experimental.pallas import tpu as pltpu
from jax.sharding import PartitionSpec as P

NEG = -1e30
VMEM_LIMIT = 48 * 1024 * 1024


def dot_nt(a, b):
    return lax.dot_general(a, b, (((1,), (1,)), ((), ())), preferred_element_type=jnp.float32)


def dot_nn(a, b):
    return lax.dot_general(a, b, (((1,), (0,)), ((), ())), preferred_element_type=jnp.float32)


def token_grids(tokens, group):
    q = lax.broadcasted_iota(jnp.int32, (tokens, tokens), 0)
    k = lax.broadcasted_iota(jnp.int32, (tokens, tokens), 1)
    return jnp.abs(q // group - k // group)


def edge_kernel(flags, q_ref, left_ref, right_ref, far_ref, out_ref, *, heads, cols_tile):
    tokens = q_ref.shape[0]
    d = 128
    scale = d ** (-0.5)

    @pl.when(flags[0] > 0)
    def _():
        use_right = flags[1] > 0
        same = token_grids(tokens, cols_tile) == 0
        lane = lax.broadcasted_iota(jnp.int32, (tokens, d), 1)
        stats = jnp.zeros((tokens, d), jnp.float32)
        for n in range(heads):
            cut = slice(n * d, (n + 1) * d)
            q = q_ref[:, cut]
            near_k = jnp.where(use_right, right_ref[0, :, cut], left_ref[0, :, cut])
            near_v = jnp.where(use_right, right_ref[1, :, cut], left_ref[1, :, cut])
            s0 = jnp.where(same, dot_nt(q, near_k) * scale, NEG)
            s1 = jnp.where(same, dot_nt(q, far_ref[0, :, cut]) * scale, NEG)
            top = jnp.max(jnp.maximum(s0, s1), axis=1, keepdims=True)
            e0 = jnp.exp(s0 - top)
            e1 = jnp.exp(s1 - top)
            total = jnp.sum(e0 + e1, axis=1, keepdims=True)
            o = dot_nn(e0.astype(jnp.bfloat16), near_v) + dot_nn(
                e1.astype(jnp.bfloat16), far_ref[1, :, cut]
            )
            out_ref[:, cut] = (o / total).astype(jnp.bfloat16)
            lse = top + jnp.log(total)
            high = lse.astype(jnp.bfloat16).astype(jnp.float32)
            mid = (lse - high).astype(jnp.bfloat16).astype(jnp.float32)
            low = lse - high - mid
            stats = jnp.where(lane == 3 * n, high, stats)
            stats = jnp.where(lane == 3 * n + 1, mid, stats)
            stats = jnp.where(lane == 3 * n + 2, low, stats)
        out_ref[:, heads * d:] = stats.astype(jnp.bfloat16)


def main_kernel(flags, reach, q_ref, *refs, heads, cols_tile, frame_tokens):
    tiles = refs[:10]
    remote_ref, stats_ref, out_ref = refs[10:]
    tokens = q_ref.shape[0]
    d = 128
    scale = d ** (-0.5)
    step = pl.program_id(0)
    frame_gap = token_grids(tokens, frame_tokens)
    row_gap = token_grids(tokens, cols_tile)
    lane = lax.broadcasted_iota(jnp.int32, (tokens, d), 1)
    stats = stats_ref[...].astype(jnp.float32)
    for n in range(heads):
        cut = slice(n * d, (n + 1) * d)
        head = step * heads + n
        q = q_ref[:, cut]
        keys = jnp.concatenate([t[0, :, cut] for t in tiles], axis=0)
        values = jnp.concatenate([t[1, :, cut] for t in tiles], axis=0)
        scores = dot_nt(q, keys) * scale
        raw = [scores[:, t * tokens:(t + 1) * tokens] for t in range(10)]
        masked = []
        for t in range(9):
            limit = jnp.where(flags[t] > 0, reach[head], -1)
            masked.append(jnp.where(frame_gap <= limit, raw[t], NEG))
        top = functools.reduce(jnp.maximum, masked)
        top = jnp.max(top, axis=1, keepdims=True)
        weights = [jnp.exp(m - top) for m in masked]
        total = jnp.sum(functools.reduce(jnp.add, weights), axis=1, keepdims=True)
        probs = jnp.concatenate([w.astype(jnp.bfloat16) for w in weights], axis=1)
        window = dot_nn(probs, values[:9 * tokens]) / total

        row_tiles = [(3, flags[9]), (4, None), (5, flags[10]), (9, flags[11])]
        row_masked = []
        for t, valid in row_tiles:
            limit = 0 if valid is None else jnp.where(valid > 0, 0, -1)
            row_masked.append(jnp.where(row_gap <= limit, raw[t], NEG))
        row_top = jnp.max(functools.reduce(jnp.maximum, row_masked), axis=1, keepdims=True)
        row_weights = [jnp.exp(m - row_top) for m in row_masked]
        row_total = jnp.sum(functools.reduce(jnp.add, row_weights), axis=1, keepdims=True)
        row_probs = jnp.concatenate([w.astype(jnp.bfloat16) for w in row_weights], axis=1)
        row_values = jnp.concatenate([values[3 * tokens:6 * tokens], values[9 * tokens:]], axis=0)
        row = dot_nn(row_probs, row_values)

        mine = (lane >= 3 * head) & (lane < 3 * head + 3)
        lse = jnp.sum(jnp.where(mine, stats, 0.0), axis=1, keepdims=True)
        lse = jnp.where(flags[12] > 0, lse, NEG)
        both = jnp.maximum(row_top, lse)
        here = jnp.exp(row_top - both)
        there = jnp.exp(lse - both)
        whole = here * row_total + there
        axial = row * (here / whole) + remote_ref[:, cut].astype(jnp.float32) * (there / whole)
        out_ref[:, cut] = (window + axial).astype(jnp.bfloat16)


def edge_attend(flags, q, left, right, far, half, stream, cols_tile):
    tokens, width = far.shape[1:]
    heads = width // 128
    kv_spec = pl.BlockSpec((2, None, tokens, width), lambda g: (0, stream, 0, 0))
    return pl.pallas_call(
        functools.partial(edge_kernel, heads=heads, cols_tile=cols_tile),
        out_shape=jax.ShapeDtypeStruct((tokens, width + 128), jnp.bfloat16),
        grid=(1,),
        in_specs=[
            pl.BlockSpec(memory_space=pltpu.SMEM),
            pl.BlockSpec((None, None, tokens, width), lambda g: (half, stream, 0, 0)),
            kv_spec,
            kv_spec,
            pl.BlockSpec((2, tokens, width), lambda g: (0, 0, 0)),
        ],
        out_specs=pl.BlockSpec((tokens, width + 128), lambda g: (0, 0)),
        compiler_params=pltpu.CompilerParams(vmem_limit_bytes=VMEM_LIMIT),
        cost_estimate=pl.CostEstimate(
            flops=8 * tokens * tokens * width,
            bytes_accessed=16 * tokens * width,
            transcendentals=2 * tokens * tokens * heads,
        ),
        name="edge_rows",
    )(flags, q, left, right, far)


def main_attend(flags, reach, q, tiles, far, remote, half, stream, cols_tile, frame_tokens, block_heads=3):
    tokens, width = far.shape[1:]
    heads = width // 128
    lanes = block_heads * 128
    kv_spec = pl.BlockSpec((2, None, tokens, lanes), lambda g: (0, stream, 0, g))
    smem = pl.BlockSpec(memory_space=pltpu.SMEM)
    return pl.pallas_call(
        functools.partial(
            main_kernel, heads=block_heads, cols_tile=cols_tile, frame_tokens=frame_tokens
        ),
        out_shape=jax.ShapeDtypeStruct((tokens, width), jnp.bfloat16),
        grid=(heads // block_heads,),
        in_specs=[
            smem,
            smem,
            pl.BlockSpec((None, None, tokens, lanes), lambda g: (half, stream, 0, g)),
        ]
        + [kv_spec] * 9
        + [
            pl.BlockSpec((2, tokens, lanes), lambda g: (0, 0, g)),
            pl.BlockSpec((tokens, lanes), lambda g: (0, g)),
            pl.BlockSpec((tokens, 128), lambda g: (0, heads)),
        ],
        out_specs=pl.BlockSpec((tokens, lanes), lambda g: (0, g)),
        compiler_params=pltpu.CompilerParams(vmem_limit_bytes=VMEM_LIMIT),
        cost_estimate=pl.CostEstimate(
            flops=46 * tokens * tokens * width,
            bytes_accessed=46 * tokens * width,
            transcendentals=13 * tokens * tokens * heads,
        ),
        name="tile_rows",
    )(flags, reach, q, *tiles, far, remote, remote)


def per_device(queries, key_states, value_states, tile_mask, frame_reach, out_weight):
    S, F, R, C, width = queries.shape
    tokens = F * R * C
    half = width // 2
    pair = lax.axis_index("pair")
    rows, cols = lax.axis_size("row"), lax.axis_size("col")
    row, col = lax.axis_index("row"), lax.axis_index("col")
    last = cols - 1
    up = [(i, i + 1) for i in range(rows - 1)]
    down = [(i + 1, i) for i in range(rows - 1)]
    right = [(i, i + 1) for i in range(cols - 1)]
    left = [(i + 1, i) for i in range(cols - 1)]
    swap = [(0, 1), (1, 0)]
    inward = [(0, 1), (last, last - 1)]
    outward = [(1, 0), (last - 1, last)]
    middle = [(1, 2), (2, 1)]

    flat = [a.reshape(S, tokens, width) for a in (queries, key_states, value_states)]
    first = pair == 0

    def halves(value):
        low, high = value[:, :, :half], value[:, :, half:]
        return jnp.where(first, high, low), jnp.where(first, low, high)

    q_halves, k_halves, v_halves = [halves(a) for a in flat]
    kv = [jnp.stack([k, v]) for k, v in zip(k_halves, v_halves)]
    q = jnp.stack(q_halves)

    offsets = jnp.arange(3, dtype=jnp.int32) - 1
    row_inside = (row + offsets >= 0) & (row + offsets < rows)
    col_inside = (col + offsets >= 0) & (col + offsets < cols)
    listed = tile_mask.reshape(3, 3) > 0
    center = (offsets[:, None] == 0) & (offsets[None, :] == 0)
    tile_ok = (listed | center) & row_inside[:, None] & col_inside[None, :]
    inner = (col > 0) & (col < last)
    flags = jnp.concatenate(
        [tile_ok.reshape(9), jnp.stack([col > 0, col < last, inner, ~inner])]
    ).astype(jnp.int32)
    edge_flags = jnp.stack([inner, col == 1]).astype(jnp.int32)
    heads_half = half // 128
    reach_low, reach_high = frame_reach[:heads_half], frame_reach[heads_half:]
    reach = [jnp.where(first, reach_high, reach_low), jnp.where(first, reach_low, reach_high)]

    edge_q = lax.ppermute(q, "col", inward)
    combined = [[None] * S for _ in range(2)]
    for h in range(2):
        own = kv[h]
        from_left = lax.ppermute(own, "col", right)
        from_right = lax.ppermute(own, "col", left)
        strip = (from_left, own, from_right)
        above = [lax.ppermute(x, "row", up) for x in strip]
        below = [lax.ppermute(x, "row", down) for x in strip]
        tiles = above + list(strip) + below
        for s in range(S):
            passed = jnp.where(col == 1, from_left[:, s], from_right[:, s])
            far = lax.ppermute(passed, "col", middle)
            partial = edge_attend(edge_flags, edge_q, from_left, from_right, far, h, s, C)
            remote = lax.ppermute(partial, "col", outward)
            combined[h][s] = main_attend(
                flags, reach[h], q, tiles, far, remote, h, s, C, R * C
            )
    outs = []
    for s in range(S):
        theirs = lax.ppermute(combined[0][s], "pair", swap)
        product = dot_nn(theirs, out_weight[s]).astype(jnp.bfloat16)
        mine = lax.ppermute(product, "pair", swap)
        outs.append(
            (dot_nn(combined[1][s], out_weight[s]) + mine.astype(jnp.float32)).astype(jnp.bfloat16)
        )
    return jnp.stack(outs).reshape(S, F, R, C, out_weight.shape[2])


def solution(mesh):
    return jax.shard_map(
        per_device,
        mesh=mesh,
        in_specs=(
            P("pair", None, "row", "col", None),
            P("pair", None, "row", "col", None),
            P("pair", None, "row", "col", None),
            P("pair", "row", "col", None),
            P(),
            P(None, "pair", None),
        ),
        out_specs=P("pair", None, "row", "col", None),
        check_vma=False,
    )
```

```python
import functools
import math

import jax
import jax.numpy as jnp
from jax import lax
from jax.experimental import pallas as pl
from jax.experimental.pallas import tpu as pltpu
from jax.sharding import PartitionSpec as P

NEG = -1e30
VMEM_LIMIT = 24 * 1024 * 1024
HEAD = 128
TO_LOG2 = HEAD ** (-0.5) * math.log2(math.e)
ANY = pl.BlockSpec(memory_space=pl.ANY)
SMEM = pl.BlockSpec(memory_space=pltpu.SMEM)


def dot_nt(a, b):
    return lax.dot_general(a, b, (((1,), (1,)), ((), ())), preferred_element_type=jnp.float32)


def dot_nn(a, b):
    return lax.dot_general(a, b, (((1,), (0,)), ((), ())), preferred_element_type=jnp.float32)


def group_gap(tokens, group):
    q = lax.broadcasted_iota(jnp.int32, (tokens, tokens), 0)
    k = lax.broadcasted_iota(jnp.int32, (tokens, tokens), 1)
    return jnp.abs(q // group - k // group)


def with_ones(values):
    return jnp.concatenate([values, jnp.ones_like(values)], axis=1)


def softmax_sums(scores, values):
    top = jnp.max(functools.reduce(jnp.maximum, scores), axis=1, keepdims=True)
    weights = [jnp.exp2((s - top) * TO_LOG2).astype(jnp.bfloat16) for s in scores]
    sums = dot_nn(jnp.concatenate(weights, axis=1), with_ones(jnp.concatenate(values, axis=0)))
    return top * TO_LOG2, sums[:, :HEAD], sums[:, HEAD:]


def edge_kernel(place, q_ref, near_ref, far_ref, out_ref, *, heads, cols_tile, cols):
    tokens = q_ref.shape[0]

    @pl.when((place[2] > 0) & (place[2] < cols - 1))
    def _():
        bias = jnp.where(group_gap(tokens, cols_tile) == 0, 0.0, NEG)
        lane = lax.broadcasted_iota(jnp.int32, (tokens, HEAD), 1)
        stats = jnp.zeros((tokens, HEAD), jnp.float32)
        for n in range(heads):
            cut = slice(n * HEAD, (n + 1) * HEAD)
            q = q_ref[:, cut]
            scores = [dot_nt(q, t[0, :, cut]) + bias for t in (near_ref, far_ref)]
            top, total, weight = softmax_sums(scores, [near_ref[1, :, cut], far_ref[1, :, cut]])
            out_ref[:, cut] = (total / weight).astype(jnp.bfloat16)
            lse = top + jnp.log2(weight)
            high = lse.astype(jnp.bfloat16).astype(jnp.float32)
            mid = (lse - high).astype(jnp.bfloat16).astype(jnp.float32)
            low = lse - high - mid
            stats = jnp.where(lane == 3 * n, high, stats)
            stats = jnp.where(lane == 3 * n + 1, mid, stats)
            stats = jnp.where(lane == 3 * n + 2, low, stats)
        out_ref[:, heads * HEAD:] = stats.astype(jnp.bfloat16)


def fill_bias(bias_ref, frame_tokens, cols_tile):
    tokens = bias_ref.shape[1]
    frames = tokens // frame_tokens
    gap = group_gap(tokens, frame_tokens)
    for reach in range(frames):
        bias_ref[reach] = jnp.where(gap <= reach, 0.0, NEG)
    bias_ref[frames] = jnp.full((tokens, tokens), NEG, jnp.float32)
    bias_ref[frames + 1] = jnp.where(group_gap(tokens, cols_tile) == 0, 0.0, NEG)


def combined_heads(place, mask, reach, q_ref, tiles, remote_ref, stats_ref, bias_ref, heads, half, grid):
    tokens = q_ref.shape[0]
    none = bias_ref.shape[0] - 2
    step = pl.program_id(0)
    rows, cols = grid
    row, col = place[1], place[2]
    row_sign, col_sign = 1 - 2 * (row % 2), 1 - 2 * (col % 2)
    row_steps, col_steps = (row_sign, 0, -row_sign), (0, col_sign, -col_sign)
    listed = []
    for a in row_steps:
        for b in col_steps:
            inside = (row + a >= 0) & (row + a < rows) & (col + b >= 0) & (col + b < cols)
            listed.append(inside & ((mask[3 * (a + 1) + b + 1] > 0) | ((a == 0) & (b == 0))))
    inner = (col > 0) & (col < cols - 1)
    first_head = (half + (1 - 2 * half) * (1 - place[0])) * heads * pl.num_programs(0)
    lane = lax.broadcasted_iota(jnp.int32, (tokens, HEAD), 1)
    stats = stats_ref[...].astype(jnp.float32)
    results = []
    for n in range(heads):
        cut = slice(n * HEAD, (n + 1) * HEAD)
        head = step * heads + n
        limit = reach[first_head + head]
        q = q_ref[:, cut]
        scores = dot_nt(q, jnp.concatenate([t[0, :, cut] for t in tiles], axis=0))
        raw = [scores[:, t * tokens:(t + 1) * tokens] for t in range(10)]
        values = [t[1, :, cut] for t in tiles]
        window = [raw[t] + bias_ref[jnp.where(listed[t], limit, none)] for t in range(9)]
        _, window_total, window_weight = softmax_sums(window, values[:9])
        row_bias = bias_ref[none + 1]
        outer_bias = bias_ref[jnp.where(inner, none + 1, none)]
        row_scores = [raw[3] + row_bias, raw[4] + row_bias, raw[5] + outer_bias, raw[9] + outer_bias]
        row_top, row_total, row_weight = softmax_sums(row_scores, values[3:6] + values[9:])
        mine = (lane >= 3 * head) & (lane < 3 * head + 3)
        lse = jnp.sum(jnp.where(mine, stats, 0.0), axis=1, keepdims=True)
        lse = jnp.where(inner, NEG, lse)
        both = jnp.maximum(row_top, lse)
        here = jnp.exp2(row_top - both)
        there = jnp.exp2(lse - both)
        whole = here * row_weight + there
        axial = (row_total * here + remote_ref[:, cut].astype(jnp.float32) * there) / whole
        results.append((window_total / window_weight + axial).astype(jnp.bfloat16))
    return jnp.concatenate(results, axis=1)


def first_kernel(place, mask, reach, q_ref, *refs, cols_tile, frame_tokens, **sizes):
    tiles = refs[:10]
    remote_ref, stats_ref, out_ref, bias_ref = refs[10:]

    @pl.when(pl.program_id(0) == 0)
    def _():
        fill_bias(bias_ref, frame_tokens, cols_tile)

    out_ref[...] = combined_heads(
        place, mask, reach, q_ref, tiles, remote_ref, stats_ref, bias_ref, **sizes
    )


def add_product(total_ref, rows, weight_ref, lanes=512):
    for start in range(0, total_ref.shape[1], lanes):
        cut = slice(start, start + lanes)
        total_ref[:, cut] += dot_nn(rows, weight_ref[:, cut])


def second_kernel(place, mask, reach, q_ref, *refs, cols_tile, frame_tokens, **sizes):
    tiles = refs[:10]
    remote_ref, stats_ref, weight_ref, other_ref = refs[10:14]
    out_ref, bias_ref, total_ref = refs[-3:]

    @pl.when(pl.program_id(0) == 0)
    def _():
        fill_bias(bias_ref, frame_tokens, cols_tile)
        total_ref[...] = other_ref[...].astype(jnp.float32)

    rows = combined_heads(
        place, mask, reach, q_ref, tiles, remote_ref, stats_ref, bias_ref, **sizes
    )
    add_product(total_ref, rows, weight_ref)

    @pl.when(pl.program_id(0) == pl.num_programs(0) - 1)
    def _():
        out_ref[...] = total_ref[...].astype(jnp.bfloat16)


def product_kernel(rows_ref, weight_ref, out_ref, total_ref):
    @pl.when(pl.program_id(0) == 0)
    def _():
        total_ref[...] = jnp.zeros_like(total_ref)

    add_product(total_ref, rows_ref[...], weight_ref)

    @pl.when(pl.program_id(0) == pl.num_programs(0) - 1)
    def _():
        out_ref[...] = total_ref[...].astype(jnp.bfloat16)


def params():
    return pltpu.CompilerParams(vmem_limit_bytes=VMEM_LIMIT)


def side(half, place):
    return half + (1 - 2 * half) * (1 - place[0])


def pack(place, keys, values, half, *earlier):
    S, tokens, width = keys.shape
    spec = pl.BlockSpec((None, tokens, width // 2), lambda s, p: (s, 0, side(half, p)))

    def kernel(place, k_ref, v_ref, *refs):
        refs[-1][0] = k_ref[...]
        refs[-1][1] = v_ref[...]

    return pl.pallas_call(
        kernel,
        out_shape=jax.ShapeDtypeStruct((S, 2, tokens, width // 2), keys.dtype),
        grid_spec=pltpu.PrefetchScalarGridSpec(
            num_scalar_prefetch=1,
            grid=(S,),
            in_specs=[spec, spec, *[ANY] * len(earlier)],
            out_specs=pl.BlockSpec((None, 2, tokens, width // 2), lambda s, p: (s, 0, 0, 0)),
        ),
        compiler_params=params(),
        cost_estimate=pl.CostEstimate(
            flops=0, bytes_accessed=4 * S * tokens * width, transcendentals=0
        ),
        name="pack",
    )(place, keys, values, *earlier)


def edge_attend(place, q, near, far, half, stream, cols_tile, cols):
    tokens, width = far.shape[1:]
    heads = width // HEAD
    return pl.pallas_call(
        functools.partial(edge_kernel, heads=heads, cols_tile=cols_tile, cols=cols),
        out_shape=jax.ShapeDtypeStruct((tokens, width + HEAD), jnp.bfloat16),
        grid_spec=pltpu.PrefetchScalarGridSpec(
            num_scalar_prefetch=1,
            grid=(1,),
            in_specs=[
                pl.BlockSpec((None, tokens, width), lambda g, p: (stream, 0, side(half, p))),
                pl.BlockSpec((None, 2, tokens, width), lambda g, p: (stream, 0, 0, 0)),
                pl.BlockSpec((2, tokens, width), lambda g, p: (0, 0, 0)),
            ],
            out_specs=pl.BlockSpec((tokens, width + HEAD), lambda g, p: (0, 0)),
        ),
        compiler_params=params(),
        cost_estimate=pl.CostEstimate(
            flops=8 * tokens * tokens * width,
            bytes_accessed=14 * tokens * width,
            transcendentals=2 * tokens * tokens * heads,
        ),
        name="edge_rows",
    )(place, q, near, far)


def main_attend(place, mask, reach, q, tiles, far, remote, half, stream, cols_tile, frame_tokens, grid,
                project=None, block=3):
    tokens, width = far.shape[1:]
    heads = width // HEAD
    lanes = block * HEAD
    steps = heads // block
    sizes = dict(heads=block, half=half, grid=grid, cols_tile=cols_tile, frame_tokens=frame_tokens)
    in_specs = [
        SMEM,
        SMEM,
        pl.BlockSpec((None, tokens, lanes), lambda g, p: (stream, 0, side(half, p) * steps + g)),
        *[pl.BlockSpec((None, 2, tokens, lanes), lambda g, p: (stream, 0, 0, g))] * 9,
        pl.BlockSpec((2, tokens, lanes), lambda g, p: (0, 0, g)),
        pl.BlockSpec((tokens, lanes), lambda g, p: (0, g)),
        pl.BlockSpec((tokens, HEAD), lambda g, p: (0, heads)),
    ]
    args = [place, mask, reach, q, *tiles, far, remote, remote]
    scratch = [pltpu.VMEM((tokens // frame_tokens + 2, tokens, tokens), jnp.float32)]
    flops, moved = 46 * tokens * tokens * width, 46 * tokens * width
    exps = 13 * tokens * tokens * heads
    if project is None:
        return pl.pallas_call(
            functools.partial(first_kernel, **sizes),
            out_shape=jax.ShapeDtypeStruct((tokens, width), jnp.bfloat16),
            grid_spec=pltpu.PrefetchScalarGridSpec(
                num_scalar_prefetch=1,
                grid=(steps,),
                in_specs=in_specs,
                out_specs=pl.BlockSpec((tokens, lanes), lambda g, p: (0, g)),
                scratch_shapes=scratch,
            ),
            compiler_params=params(),
            cost_estimate=pl.CostEstimate(
                flops=flops, bytes_accessed=moved, transcendentals=exps
            ),
            name="first_rows",
        )(*args)
    weight, other, output = project
    model = weight.shape[2]
    earlier = [] if output is None else [output]
    return pl.pallas_call(
        functools.partial(second_kernel, **sizes),
        out_shape=jax.ShapeDtypeStruct((q.shape[0], tokens, model), jnp.bfloat16),
        grid_spec=pltpu.PrefetchScalarGridSpec(
            num_scalar_prefetch=1,
            grid=(steps,),
            in_specs=[
                *in_specs,
                pl.BlockSpec((None, lanes, model), lambda g, p: (stream, g, 0)),
                pl.BlockSpec((tokens, model), lambda g, p: (0, 0)),
                *[ANY] * len(earlier),
            ],
            out_specs=pl.BlockSpec((None, tokens, model), lambda g, p: (stream, 0, 0)),
            scratch_shapes=[*scratch, pltpu.VMEM((tokens, model), jnp.float32)],
        ),
        input_output_aliases={len(args) + 2: 0} if earlier else {},
        compiler_params=params(),
        cost_estimate=pl.CostEstimate(
            flops=flops + 2 * tokens * width * model,
            bytes_accessed=moved + 2 * width * model,
            transcendentals=exps,
        ),
        name="second_rows",
    )(*args, weight, other, *earlier)


def product(rows, weight, stream, block=3):
    tokens, width = rows.shape
    model = weight.shape[2]
    lanes = block * HEAD
    return pl.pallas_call(
        product_kernel,
        out_shape=jax.ShapeDtypeStruct((tokens, model), jnp.bfloat16),
        grid=(width // lanes,),
        in_specs=[
            pl.BlockSpec((tokens, lanes), lambda g: (0, g)),
            pl.BlockSpec((None, lanes, model), lambda g: (stream, g, 0)),
        ],
        out_specs=pl.BlockSpec((tokens, model), lambda g: (0, 0)),
        scratch_shapes=[pltpu.VMEM((tokens, model), jnp.float32)],
        compiler_params=params(),
        cost_estimate=pl.CostEstimate(
            flops=2 * tokens * width * model, bytes_accessed=2 * width * model, transcendentals=0
        ),
        name="product",
    )(rows, weight)


def swaps(size, start):
    pairs = [(i, i + 1) for i in range(start, size - 1, 2)]
    return pairs + [(j, i) for i, j in pairs]


def per_device(queries, key_states, value_states, tile_mask, frame_reach, out_weight):
    S, F, R, C, width = queries.shape
    tokens = F * R * C
    model = out_weight.shape[2]
    rows, cols = lax.axis_size("row"), lax.axis_size("col")
    inward = [(0, 1), (cols - 1, cols - 2)]
    outward = [(j, i) for i, j in inward]
    place = jnp.stack([lax.axis_index(a) for a in ("pair", "row", "col")]).astype(jnp.int32)
    q, k, v = [a.reshape(S, tokens, width) for a in (queries, key_states, value_states)]
    mask = tile_mask.reshape(9)

    output, near = None, None
    others = []
    for h in range(2):
        own = pack(place, k, v, h, *([] if h == 0 else [near]))
        near = lax.ppermute(own, "col", swaps(cols, 0))
        other = lax.ppermute(own, "col", swaps(cols, 1))
        if h == 0:
            edge_q = lax.ppermute(q, "col", inward)
        strip = (own, near, other)
        above = [lax.ppermute(x, "row", swaps(rows, 0)) for x in strip]
        below = [lax.ppermute(x, "row", swaps(rows, 1)) for x in strip]
        tiles = above + list(strip) + below
        for s in range(S):
            far = lax.ppermute(near[s], "col", swaps(cols, 1))
            partial = edge_attend(place, edge_q, other, far, h, s, C, cols)
            remote = lax.ppermute(partial, "col", outward)
            args = (place, mask, frame_reach, q, tiles, far, remote, h, s, C, R * C, (rows, cols))
            if h == 0:
                theirs = lax.ppermute(main_attend(*args), "pair", swaps(2, 0))
                others.append(lax.ppermute(product(theirs, out_weight, s), "pair", swaps(2, 0)))
            else:
                output = main_attend(*args, project=(out_weight, others[s], output))
    return output.reshape(S, F, R, C, model)


def solution(mesh):
    return jax.shard_map(
        per_device,
        mesh=mesh,
        in_specs=(
            P("pair", None, "row", "col", None),
            P("pair", None, "row", "col", None),
            P("pair", None, "row", "col", None),
            P("pair", "row", "col", None),
            P(),
            P(None, "pair", None),
        ),
        out_specs=P("pair", None, "row", "col", None),
        check_vma=False,
    )
```

```python
import functools
import math

import jax
import jax.numpy as jnp
from jax import lax
from jax.experimental import pallas as pl
from jax.experimental.pallas import tpu as pltpu
from jax.sharding import PartitionSpec as P

NEG = -1e30
VMEM_LIMIT = 24 * 1024 * 1024
HEAD = 128
TO_LOG2 = HEAD ** (-0.5) * math.log2(math.e)
ANY = pl.BlockSpec(memory_space=pl.ANY)
SMEM = pl.BlockSpec(memory_space=pltpu.SMEM)


def dot_nn(a, b):
    return lax.dot_general(a, b, (((1,), (0,)), ((), ())), preferred_element_type=jnp.float32)


def group_gap(tokens, group):
    q = lax.broadcasted_iota(jnp.int32, (tokens, tokens), 0)
    k = lax.broadcasted_iota(jnp.int32, (tokens, tokens), 1)
    return jnp.abs(q // group - k // group)


def with_ones(values):
    return jnp.concatenate([values, jnp.ones_like(values)], axis=1)


def softmax_sums(scores, values):
    tops = [jnp.max(functools.reduce(jnp.maximum, tiles), axis=1, keepdims=True) for tiles in scores]
    weights = [
        jnp.concatenate(
            [jnp.exp2((s - top) * TO_LOG2).astype(jnp.bfloat16) for s in tiles], axis=1
        )
        for tiles, top in zip(scores, tops)
    ]
    sums = [
        dot_nn(w, with_ones(jnp.concatenate(tiles, axis=0))) for w, tiles in zip(weights, values)
    ]
    return [top * TO_LOG2 for top in tops], [x[:, :HEAD] for x in sums], [x[:, HEAD:] for x in sums]


def edge_kernel(place, q_ref, near_ref, far_ref, out_ref, *, heads, cols_tile, cols):
    tokens = q_ref.shape[0]

    @pl.when((place[2] > 0) & (place[2] < cols - 1))
    def _():
        bias = jnp.where(group_gap(tokens, cols_tile) == 0, 0.0, NEG)
        lane = lax.broadcasted_iota(jnp.int32, (tokens, HEAD), 1)
        cuts = [slice(n * HEAD, (n + 1) * HEAD) for n in range(heads)]
        tiles = (near_ref, far_ref)
        scores = [[dot_nn(q_ref[:, c], t[0, :, c]) + bias for t in tiles] for c in cuts]
        values = [[t[1, :, c] for t in tiles] for c in cuts]
        tops, totals, weights = softmax_sums(scores, values)
        stats = jnp.zeros((tokens, HEAD), jnp.float32)
        for n in range(heads):
            lse = tops[n] + jnp.log2(weights[n])
            high = lse.astype(jnp.bfloat16).astype(jnp.float32)
            mid = (lse - high).astype(jnp.bfloat16).astype(jnp.float32)
            low = lse - high - mid
            stats = jnp.where(lane == 3 * n, high, stats)
            stats = jnp.where(lane == 3 * n + 1, mid, stats)
            stats = jnp.where(lane == 3 * n + 2, low, stats)
        out_ref[:, :heads * HEAD] = jnp.concatenate(
            [(t / w).astype(jnp.bfloat16) for t, w in zip(totals, weights)], axis=1
        )
        out_ref[:, heads * HEAD:] = stats.astype(jnp.bfloat16)


def fill_bias(bias_ref, frame_tokens, cols_tile):
    tokens = bias_ref.shape[1]
    frames = tokens // frame_tokens
    gap = group_gap(tokens, frame_tokens)
    for reach in range(frames):
        bias_ref[reach] = jnp.where(gap <= reach, 0.0, NEG)
    bias_ref[frames] = jnp.full((tokens, tokens), NEG, jnp.float32)
    bias_ref[frames + 1] = jnp.where(group_gap(tokens, cols_tile) == 0, 0.0, NEG)


def combined_heads(place, mask, reach, q_ref, tiles, remote_ref, stats_ref, bias_ref, heads, half, grid):
    tokens = q_ref.shape[0]
    none = bias_ref.shape[0] - 2
    step = pl.program_id(0)
    rows, cols = grid
    row, col = place[1], place[2]
    row_sign, col_sign = 1 - 2 * (row % 2), 1 - 2 * (col % 2)
    row_steps, col_steps = (row_sign, 0, -row_sign), (0, col_sign, -col_sign)
    listed = []
    for a in row_steps:
        for b in col_steps:
            inside = (row + a >= 0) & (row + a < rows) & (col + b >= 0) & (col + b < cols)
            listed.append(inside & ((mask[3 * (a + 1) + b + 1] > 0) | ((a == 0) & (b == 0))))
    inner = (col > 0) & (col < cols - 1)
    first_head = (half + (1 - 2 * half) * (1 - place[0])) * heads * pl.num_programs(0)
    lane = lax.broadcasted_iota(jnp.int32, (tokens, HEAD), 1)
    stats = stats_ref[...].astype(jnp.float32)
    cuts = [slice(n * HEAD, (n + 1) * HEAD) for n in range(heads)]
    raw = []
    for c in cuts:
        scores = dot_nn(q_ref[:, c], jnp.concatenate([t[0, :, c] for t in tiles], axis=1))
        raw.append([scores[:, t * tokens:(t + 1) * tokens] for t in range(10)])
    values = [[t[1, :, c] for t in tiles] for c in cuts]
    window, row_scores = [], []
    row_bias = bias_ref[none + 1]
    outer_bias = bias_ref[jnp.where(inner, none + 1, none)]
    for n in range(heads):
        limit = reach[first_head + step * heads + n]
        window.append(
            [raw[n][t] + bias_ref[jnp.where(listed[t], limit, none)] for t in range(9)]
        )
        row_scores.append(
            [raw[n][3] + row_bias, raw[n][4] + row_bias, raw[n][5] + outer_bias, raw[n][9] + outer_bias]
        )
    _, window_totals, window_weights = softmax_sums(window, [v[:9] for v in values])
    tops, totals, weights = softmax_sums(row_scores, [v[3:6] + v[9:] for v in values])
    results = []
    for n, c in enumerate(cuts):
        head = step * heads + n
        mine = (lane >= 3 * head) & (lane < 3 * head + 3)
        lse = jnp.sum(jnp.where(mine, stats, 0.0), axis=1, keepdims=True)
        lse = jnp.where(inner, NEG, lse)
        both = jnp.maximum(tops[n], lse)
        here = jnp.exp2(tops[n] - both)
        there = jnp.exp2(lse - both)
        whole = here * weights[n] + there
        axial = (totals[n] * here + remote_ref[:, c].astype(jnp.float32) * there) / whole
        results.append((window_totals[n] / window_weights[n] + axial).astype(jnp.bfloat16))
    return jnp.concatenate(results, axis=1)


def first_kernel(place, mask, reach, q_ref, *refs, cols_tile, frame_tokens, **sizes):
    tiles = refs[:10]
    remote_ref, stats_ref, out_ref, bias_ref = refs[10:]

    @pl.when(pl.program_id(0) == 0)
    def _():
        fill_bias(bias_ref, frame_tokens, cols_tile)

    out_ref[...] = combined_heads(
        place, mask, reach, q_ref, tiles, remote_ref, stats_ref, bias_ref, **sizes
    )


def add_product(total_ref, rows, weight_ref, lanes=512):
    for start in range(0, total_ref.shape[1], lanes):
        cut = slice(start, start + lanes)
        total_ref[:, cut] += dot_nn(rows, weight_ref[:, cut])


def second_kernel(place, mask, reach, q_ref, *refs, cols_tile, frame_tokens, **sizes):
    tiles = refs[:10]
    remote_ref, stats_ref, weight_ref, other_ref = refs[10:14]
    out_ref, bias_ref, total_ref = refs[-3:]

    @pl.when(pl.program_id(0) == 0)
    def _():
        fill_bias(bias_ref, frame_tokens, cols_tile)
        total_ref[...] = other_ref[...].astype(jnp.float32)

    rows = combined_heads(
        place, mask, reach, q_ref, tiles, remote_ref, stats_ref, bias_ref, **sizes
    )
    add_product(total_ref, rows, weight_ref)

    @pl.when(pl.program_id(0) == pl.num_programs(0) - 1)
    def _():
        out_ref[...] = total_ref[...].astype(jnp.bfloat16)


def product_kernel(rows_ref, weight_ref, out_ref, total_ref):
    @pl.when(pl.program_id(0) == 0)
    def _():
        total_ref[...] = jnp.zeros_like(total_ref)

    add_product(total_ref, rows_ref[...], weight_ref)

    @pl.when(pl.program_id(0) == pl.num_programs(0) - 1)
    def _():
        out_ref[...] = total_ref[...].astype(jnp.bfloat16)


def hbm(*values):
    return [pltpu.with_memory_space_constraint(v, pltpu.HBM) for v in values]


def params():
    return pltpu.CompilerParams(vmem_limit_bytes=VMEM_LIMIT)


def side(half, place):
    return half + (1 - 2 * half) * (1 - place[0])


def pack(place, keys, values, half, *earlier):
    S, tokens, width = keys.shape
    width //= 2

    def kernel(place, k_ref, v_ref, *refs):
        out_ref, rows, turned, sems = refs[-4:]
        start = pl.multiple_of(side(half, place) * width, HEAD)
        loads, moves = [], []
        for s in range(S):
            loads.append(
                pltpu.make_async_copy(k_ref.at[s, :, pl.ds(start, width)], rows.at[s], sems.at[0, s])
            )
            moves.append(
                pltpu.make_async_copy(
                    v_ref.at[s, :, pl.ds(start, width)], out_ref.at[s, 1], sems.at[1, s]
                )
            )
            moves.append(pltpu.make_async_copy(turned.at[s], out_ref.at[s, 0], sems.at[2, s]))
        for s in range(S):
            loads[s].start()
            moves[2 * s].start()
        for s in range(S):
            loads[s].wait()
            for n in range(width // HEAD):
                cut = slice(n * HEAD, (n + 1) * HEAD)
                turned[s, :, cut] = rows[s, :, cut].T
            moves[2 * s + 1].start()
        for move in moves:
            move.wait()

    return pl.pallas_call(
        kernel,
        out_shape=jax.ShapeDtypeStruct((S, 2, tokens, width), keys.dtype),
        in_specs=[SMEM, ANY, ANY, *[ANY] * len(earlier)],
        out_specs=ANY,
        scratch_shapes=[
            pltpu.VMEM((S, tokens, width), keys.dtype),
            pltpu.VMEM((S, tokens, width), keys.dtype),
            pltpu.SemaphoreType.DMA((3, S)),
        ],
        compiler_params=params(),
        cost_estimate=pl.CostEstimate(
            flops=0, bytes_accessed=8 * S * tokens * width, transcendentals=0
        ),
        name="pack",
    )(place, *hbm(keys, values), *earlier)


def pick(place, value, half):
    S, tokens, width = value.shape
    width //= 2

    def kernel(place, in_ref, out_ref, sem):
        start = pl.multiple_of(side(half, place) * width, HEAD)
        move = pltpu.make_async_copy(in_ref.at[:, :, pl.ds(start, width)], out_ref, sem)
        move.start()
        move.wait()

    return pl.pallas_call(
        kernel,
        out_shape=jax.ShapeDtypeStruct((S, tokens, width), value.dtype),
        in_specs=[SMEM, ANY],
        out_specs=ANY,
        scratch_shapes=[pltpu.SemaphoreType.DMA],
        compiler_params=params(),
        cost_estimate=pl.CostEstimate(
            flops=0, bytes_accessed=4 * S * tokens * width, transcendentals=0
        ),
        name="pick",
    )(place, *hbm(value))


def edge_attend(place, q, near, far, start, cols_tile, cols):
    count, _, tokens, width = far.shape
    heads = width // HEAD
    return pl.pallas_call(
        functools.partial(edge_kernel, heads=heads, cols_tile=cols_tile, cols=cols),
        out_shape=jax.ShapeDtypeStruct((count, tokens, width + HEAD), jnp.bfloat16),
        grid_spec=pltpu.PrefetchScalarGridSpec(
            num_scalar_prefetch=1,
            grid=(count,),
            in_specs=[
                pl.BlockSpec((None, tokens, width), lambda g, p: (start + g, 0, 0)),
                pl.BlockSpec((None, 2, tokens, width), lambda g, p: (start + g, 0, 0, 0)),
                pl.BlockSpec((None, 2, tokens, width), lambda g, p: (g, 0, 0, 0)),
            ],
            out_specs=pl.BlockSpec((None, tokens, width + HEAD), lambda g, p: (g, 0, 0)),
        ),
        compiler_params=params(),
        cost_estimate=pl.CostEstimate(
            flops=8 * count * tokens * tokens * width,
            bytes_accessed=14 * count * tokens * width,
            transcendentals=2 * count * tokens * tokens * heads,
        ),
        name="edge_rows",
    )(place, q, near, far)


def main_attend(place, mask, reach, q, tiles, far, remote, half, stream, cols_tile, frame_tokens, grid,
                project=None, block=3):
    tokens, width = far.shape[2:]
    at = stream if far.shape[0] > 1 else 0
    heads = width // HEAD
    lanes = block * HEAD
    steps = heads // block
    sizes = dict(heads=block, half=half, grid=grid, cols_tile=cols_tile, frame_tokens=frame_tokens)
    in_specs = [
        SMEM,
        SMEM,
        pl.BlockSpec((None, tokens, lanes), lambda g, p: (stream, 0, side(half, p) * steps + g)),
        *[pl.BlockSpec((None, None, 2, tokens, lanes), lambda g, p: (1 - p[1] % 2, stream, 0, 0, g))] * 3,
        *[pl.BlockSpec((None, 2, tokens, lanes), lambda g, p: (stream, 0, 0, g))] * 6,
        pl.BlockSpec((None, 2, tokens, lanes), lambda g, p: (at, 0, 0, g)),
        pl.BlockSpec((None, tokens, lanes), lambda g, p: (at, 0, g)),
        pl.BlockSpec((None, tokens, HEAD), lambda g, p: (at, 0, heads)),
    ]
    args = [place, mask, reach, *hbm(q), *tiles, far, remote, remote]
    scratch = [pltpu.VMEM((tokens // frame_tokens + 2, tokens, tokens), jnp.float32)]
    flops, moved = 46 * tokens * tokens * width, 46 * tokens * width
    exps = 13 * tokens * tokens * heads
    if project is None:
        return pl.pallas_call(
            functools.partial(first_kernel, **sizes),
            out_shape=jax.ShapeDtypeStruct((tokens, width), jnp.bfloat16),
            grid_spec=pltpu.PrefetchScalarGridSpec(
                num_scalar_prefetch=1,
                grid=(steps,),
                in_specs=in_specs,
                out_specs=pl.BlockSpec((tokens, lanes), lambda g, p: (0, g)),
                scratch_shapes=scratch,
            ),
            compiler_params=params(),
            cost_estimate=pl.CostEstimate(
                flops=flops, bytes_accessed=moved, transcendentals=exps
            ),
            name="first_rows",
        )(*args)
    weight, other, output = project
    model = weight.shape[2]
    earlier = [] if output is None else [output]
    return pl.pallas_call(
        functools.partial(second_kernel, **sizes),
        out_shape=jax.ShapeDtypeStruct((q.shape[0], tokens, model), jnp.bfloat16),
        grid_spec=pltpu.PrefetchScalarGridSpec(
            num_scalar_prefetch=1,
            grid=(steps,),
            in_specs=[
                *in_specs,
                pl.BlockSpec((None, lanes, model), lambda g, p: (stream, g, 0)),
                pl.BlockSpec((tokens, model), lambda g, p: (0, 0)),
                *[ANY] * len(earlier),
            ],
            out_specs=pl.BlockSpec((None, tokens, model), lambda g, p: (stream, 0, 0)),
            scratch_shapes=[*scratch, pltpu.VMEM((tokens, model), jnp.float32)],
        ),
        input_output_aliases={len(args) + 2: 0} if earlier else {},
        compiler_params=params(),
        cost_estimate=pl.CostEstimate(
            flops=flops + 2 * tokens * width * model,
            bytes_accessed=moved + 2 * width * model,
            transcendentals=exps,
        ),
        name="second_rows",
    )(*args, weight, other, *earlier)


def product(rows, weight, stream, block=3):
    tokens, width = rows.shape
    model = weight.shape[2]
    lanes = block * HEAD
    return pl.pallas_call(
        product_kernel,
        out_shape=jax.ShapeDtypeStruct((tokens, model), jnp.bfloat16),
        grid=(width // lanes,),
        in_specs=[
            pl.BlockSpec((tokens, lanes), lambda g: (0, g)),
            pl.BlockSpec((None, lanes, model), lambda g: (stream, g, 0)),
        ],
        out_specs=pl.BlockSpec((tokens, model), lambda g: (0, 0)),
        scratch_shapes=[pltpu.VMEM((tokens, model), jnp.float32)],
        compiler_params=params(),
        cost_estimate=pl.CostEstimate(
            flops=2 * tokens * width * model, bytes_accessed=2 * width * model, transcendentals=0
        ),
        name="product",
    )(rows, weight)


def swaps(size, start):
    pairs = [(i, i + 1) for i in range(start, size - 1, 2)]
    return pairs + [(j, i) for i, j in pairs]


def per_device(queries, key_states, value_states, tile_mask, frame_reach, out_weight):
    S, F, R, C, width = queries.shape
    tokens = F * R * C
    model = out_weight.shape[2]
    rows, cols = lax.axis_size("row"), lax.axis_size("col")
    inward = [(0, 1), (cols - 1, cols - 2)]
    outward = [(j, i) for i, j in inward]
    place = jnp.stack([lax.axis_index(a) for a in ("pair", "row", "col")]).astype(jnp.int32)
    q, k, v = [a.reshape(S, tokens, width) for a in (queries, key_states, value_states)]
    mask = tile_mask.reshape(9)

    sent = {}

    def tied(value, after):
        return lax.optimization_barrier((value, *[sent[n] for n in after]))[0] if after else value

    def send(name, value, axis, pairs, *after):
        sent[name] = lax.ppermute(tied(value, after), axis, pairs)

    col_pairs, col_others = swaps(cols, 0), swaps(cols, 1)
    row_pairs, row_others = swaps(rows, 0), swaps(rows, 1)
    own = [pack(place, k, v, h) for h in range(2)]
    picked = [pick(place, q, h) for h in range(2)]

    def gather(name, value, *after):
        groups = [[i, i + 1] for i in range(0, rows, 2)]
        sent[name] = lax.all_gather(tied(value, after), "row", axis_index_groups=groups)

    def edge(h, start, name, *after):
        sent[f"part{name}"] = edge_attend(
            place, tied(sent[f"q{h}"], after), sent[f"other{h}"], sent[f"far{name}"], start, C, cols
        )

    def main(h, s, name, *after, project=None):
        tiles = [
            *[sent[f"pair_{n}{h}"] for n in ("own", "near", "other")],
            own[h],
            sent[f"near{h}"],
            sent[f"other{h}"],
            *[sent[f"next_{n}{h}"] for n in ("own", "near", "other")],
        ]
        return main_attend(
            place, mask, frame_reach, tied(q, after), tiles, sent[f"far{name}"], sent[f"rest{name}"],
            h, s, C, R * C, (rows, cols), project=project,
        )

    pair_swap = swaps(2, 0)
    send("near0", own[0], "col", col_pairs)
    send("other0", own[0], "col", col_others)
    send("next_own0", own[0], "row", row_others)
    send("q0", picked[0], "col", inward)
    gather("pair_own0", own[0])
    second = ("near0", "other0", "next_own0")
    send("far00", sent["near0"][:1], "col", col_others, *second)
    send("far01", sent["near0"][1:], "col", col_others, *second)
    send("next_near0", sent["near0"], "row", row_others, *second)
    gather("pair_near0", sent["near0"], "pair_own0")
    edge(0, 0, "00")
    send("rest00", sent["part00"], "col", outward)
    send("near1", own[1], "col", col_pairs, "rest00")
    send("next_other0", sent["other0"], "row", row_others, "next_near0", "q0")
    send("other1", own[1], "col", col_others, "next_near0")
    gather("pair_other0", sent["other0"], "pair_near0")
    edge(0, 1, "01")
    send("rest01", sent["part01"], "col", outward)
    send("next_own1", own[1], "row", row_others, "next_other0", "far01")
    sent["rows0"] = main(0, 0, "00")
    send("theirs0", sent["rows0"], "pair", pair_swap)
    sent["product0"] = product(sent["theirs0"], out_weight, 0)
    send("back0", sent["product0"], "pair", pair_swap)
    gather("pair_own1", own[1], "pair_other0")
    send("q1", picked[1], "col", inward, "rest00")
    send("far10", sent["near1"][:1], "col", col_others, "next_own1")
    send("next_near1", sent["near1"], "row", row_others, "next_own1", "q1")
    sent["rows1"] = main(0, 1, "01", "rows0")
    send("theirs1", sent["rows1"], "pair", pair_swap)
    sent["product1"] = product(sent["theirs1"], out_weight, 1)
    send("back1", sent["product1"], "pair", pair_swap)
    send("far11", sent["near1"][1:], "col", col_others, "other1")
    gather("pair_near1", sent["near1"], "pair_own1")
    send("next_other1", sent["other1"], "row", row_others)
    gather("pair_other1", sent["other1"], "pair_near1")
    edge(1, 0, "10")
    send("rest10", sent["part10"], "col", outward)
    edge(1, 1, "11")
    send("rest11", sent["part11"], "col", outward)
    output = main(1, 0, "10", project=(out_weight, sent["back0"], None))
    output = main(1, 1, "11", project=(out_weight, sent["back1"], output))
    return output.reshape(S, F, R, C, model)


def solution(mesh):
    return jax.shard_map(
        per_device,
        mesh=mesh,
        in_specs=(
            P("pair", None, "row", "col", None),
            P("pair", None, "row", "col", None),
            P("pair", None, "row", "col", None),
            P("pair", "row", "col", None),
            P(),
            P(None, "pair", None),
        ),
        out_specs=P("pair", None, "row", "col", None),
        check_vma=False,
    )
```

```python
import functools
import math

import jax
import jax.numpy as jnp
from jax import lax
from jax.experimental import pallas as pl
from jax.experimental.pallas import tpu as pltpu
from jax.sharding import PartitionSpec as P

NEG = -1e30
VMEM_LIMIT = 24 * 1024 * 1024
HEAD = 128
TO_LOG2 = HEAD ** (-0.5) * math.log2(math.e)
ANY = pl.BlockSpec(memory_space=pl.ANY)
SMEM = pl.BlockSpec(memory_space=pltpu.SMEM)


def dot_nn(a, b):
    return lax.dot_general(a, b, (((1,), (0,)), ((), ())), preferred_element_type=jnp.float32)


def group_gap(tokens, group):
    q = lax.broadcasted_iota(jnp.int32, (tokens, tokens), 0)
    k = lax.broadcasted_iota(jnp.int32, (tokens, tokens), 1)
    return jnp.abs(q // group - k // group)


def with_ones(values):
    return jnp.concatenate([values, jnp.ones_like(values)], axis=1)


def softmax_sums(scores, values):
    tops = [jnp.max(functools.reduce(jnp.maximum, tiles), axis=1, keepdims=True) for tiles in scores]
    weights = [
        jnp.concatenate(
            [jnp.exp2((s - top) * TO_LOG2).astype(jnp.bfloat16) for s in tiles], axis=1
        )
        for tiles, top in zip(scores, tops)
    ]
    sums = [
        dot_nn(w, with_ones(jnp.concatenate(tiles, axis=0))) for w, tiles in zip(weights, values)
    ]
    return [top * TO_LOG2 for top in tops], [x[:, :HEAD] for x in sums], [x[:, HEAD:] for x in sums]


def edge_kernel(place, q_ref, near_ref, far_ref, out_ref, *, heads, cols_tile, cols):
    tokens = q_ref.shape[0]

    @pl.when((place[2] > 0) & (place[2] < cols - 1))
    def _():
        bias = jnp.where(group_gap(tokens, cols_tile) == 0, 0.0, NEG)
        lane = lax.broadcasted_iota(jnp.int32, (tokens, HEAD), 1)
        cuts = [slice(n * HEAD, (n + 1) * HEAD) for n in range(heads)]
        tiles = (near_ref, far_ref)
        scores = [[dot_nn(q_ref[:, c], t[0, :, c]) + bias for t in tiles] for c in cuts]
        values = [[t[1, :, c] for t in tiles] for c in cuts]
        tops, totals, weights = softmax_sums(scores, values)
        stats = jnp.zeros((tokens, HEAD), jnp.float32)
        for n in range(heads):
            lse = tops[n] + jnp.log2(weights[n])
            high = lse.astype(jnp.bfloat16).astype(jnp.float32)
            mid = (lse - high).astype(jnp.bfloat16).astype(jnp.float32)
            low = lse - high - mid
            stats = jnp.where(lane == 3 * n, high, stats)
            stats = jnp.where(lane == 3 * n + 1, mid, stats)
            stats = jnp.where(lane == 3 * n + 2, low, stats)
        out_ref[:, :heads * HEAD] = jnp.concatenate(
            [(t / w).astype(jnp.bfloat16) for t, w in zip(totals, weights)], axis=1
        )
        out_ref[:, heads * HEAD:] = stats.astype(jnp.bfloat16)


def fill_bias(bias_ref, frame_tokens, cols_tile):
    tokens = bias_ref.shape[1]
    frames = tokens // frame_tokens
    gap = group_gap(tokens, frame_tokens)
    for reach in range(frames):
        bias_ref[reach] = jnp.where(gap <= reach, 0.0, NEG)
    bias_ref[frames] = jnp.full((tokens, tokens), NEG, jnp.float32)
    bias_ref[frames + 1] = jnp.where(group_gap(tokens, cols_tile) == 0, 0.0, NEG)


def rows_kernel(place, mask, reach, q_ref, *refs, heads, half, grid, cols_tile, frame_tokens):
    tiles = refs[:10]
    window_ref, row_ref, sums_ref, bias_ref = refs[10:]
    tokens = q_ref.shape[0]
    none = bias_ref.shape[0] - 2
    step = pl.program_id(0)

    @pl.when(step == 0)
    def _():
        fill_bias(bias_ref, frame_tokens, cols_tile)
        sums_ref[...] = jnp.zeros_like(sums_ref)

    rows, cols = grid
    row, col = place[1], place[2]
    row_sign, col_sign = 1 - 2 * (row % 2), 1 - 2 * (col % 2)
    row_steps, col_steps = (row_sign, 0, -row_sign), (0, col_sign, -col_sign)
    listed = []
    for a in row_steps:
        for b in col_steps:
            inside = (row + a >= 0) & (row + a < rows) & (col + b >= 0) & (col + b < cols)
            listed.append(inside & ((mask[3 * (a + 1) + b + 1] > 0) | ((a == 0) & (b == 0))))
    inner = (col > 0) & (col < cols - 1)
    first_head = side(half, place) * heads * pl.num_programs(0)
    cuts = [slice(n * HEAD, (n + 1) * HEAD) for n in range(heads)]
    raw = []
    for c in cuts:
        scores = dot_nn(q_ref[:, c], jnp.concatenate([t[0, :, c] for t in tiles], axis=1))
        raw.append([scores[:, t * tokens:(t + 1) * tokens] for t in range(10)])
    values = [[t[1, :, c] for t in tiles] for c in cuts]
    window, row_scores = [], []
    row_bias = bias_ref[none + 1]
    outer_bias = bias_ref[jnp.where(inner, none + 1, none)]
    for n in range(heads):
        limit = reach[first_head + step * heads + n]
        window.append(
            [raw[n][t] + bias_ref[jnp.where(listed[t], limit, none)] for t in range(9)]
        )
        row_scores.append(
            [raw[n][3] + row_bias, raw[n][4] + row_bias, raw[n][5] + outer_bias, raw[n][9] + outer_bias]
        )
    _, totals, weights = softmax_sums(window, [v[:9] for v in values])
    window_ref[...] = jnp.concatenate([t / w for t, w in zip(totals, weights)], axis=1)
    tops, totals, weights = softmax_sums(row_scores, [v[3:6] + v[9:] for v in values])
    row_ref[...] = jnp.concatenate([t / w for t, w in zip(totals, weights)], axis=1)
    lane = lax.broadcasted_iota(jnp.int32, (tokens, HEAD), 1)
    sums = sums_ref[...]
    for n in range(heads):
        sums = jnp.where(lane == step * heads + n, tops[n] + jnp.log2(weights[n]), sums)
    sums_ref[...] = sums


def merged(place, window, row, sums, rest, stats, cols, step, heads):
    inner = (place[2] > 0) & (place[2] < cols - 1)
    lane = lax.broadcasted_iota(jnp.int32, sums.shape, 1)
    results = []
    for n in range(heads):
        cut = slice(n * HEAD, (n + 1) * HEAD)
        head = step * heads + n
        near = jnp.sum(jnp.where(lane == head, sums, 0.0), axis=1, keepdims=True)
        mine = (lane >= 3 * head) & (lane < 3 * head + 3)
        far = jnp.sum(jnp.where(mine, stats, 0.0), axis=1, keepdims=True)
        far = jnp.where(inner, NEG, far)
        both = jnp.maximum(near, far)
        near, far = jnp.exp2(near - both), jnp.exp2(far - both)
        share = far / (near + far)
        axial = row[:, cut] * (1.0 - share) + rest[:, cut].astype(jnp.float32) * share
        results.append((window[:, cut] + axial).astype(jnp.bfloat16))
    return jnp.concatenate(results, axis=1)


def merge_kernel(place, window_ref, row_ref, sums_ref, rest_ref, stats_ref, out_ref, *, cols):
    out_ref[...] = merged(
        place, window_ref[...], row_ref[...], sums_ref[...], rest_ref[...],
        stats_ref[...].astype(jnp.float32), cols, 0, out_ref.shape[1] // HEAD,
    )


def add_product(total_ref, rows, weight_ref, lanes=512):
    for start in range(0, total_ref.shape[1], lanes):
        cut = slice(start, start + lanes)
        total_ref[:, cut] += dot_nn(rows, weight_ref[:, cut])


def project_kernel(place, window_ref, row_ref, sums_ref, rest_ref, stats_ref, weight_ref, other_ref, *refs, cols):
    out_ref, total_ref = refs[-2:]

    @pl.when(pl.program_id(0) == 0)
    def _():
        total_ref[...] = other_ref[...].astype(jnp.float32)

    rows = merged(
        place, window_ref[...], row_ref[...], sums_ref[...], rest_ref[...],
        stats_ref[...].astype(jnp.float32), cols, pl.program_id(0), window_ref.shape[1] // HEAD,
    )
    add_product(total_ref, rows, weight_ref)

    @pl.when(pl.program_id(0) == pl.num_programs(0) - 1)
    def _():
        out_ref[...] = total_ref[...].astype(jnp.bfloat16)


def product_kernel(rows_ref, weight_ref, out_ref, total_ref):
    @pl.when(pl.program_id(0) == 0)
    def _():
        total_ref[...] = jnp.zeros_like(total_ref)

    add_product(total_ref, rows_ref[...], weight_ref)

    @pl.when(pl.program_id(0) == pl.num_programs(0) - 1)
    def _():
        out_ref[...] = total_ref[...].astype(jnp.bfloat16)


def hbm(*values):
    return [pltpu.with_memory_space_constraint(v, pltpu.HBM) for v in values]


def params():
    return pltpu.CompilerParams(vmem_limit_bytes=VMEM_LIMIT)


def side(half, place):
    return half + (1 - 2 * half) * (1 - place[0])


def pack(place, keys, values, half):
    S, tokens, width = keys.shape
    width //= 2
    spec = pl.BlockSpec((None, tokens, width), lambda s, p: (s, 0, side(half, p)))

    def kernel(place, k_ref, v_ref, out_ref):
        for start in range(0, width, HEAD):
            cut = slice(start, start + HEAD)
            out_ref[0, :, cut] = k_ref[:, cut].T
        out_ref[1] = v_ref[...]

    return pl.pallas_call(
        kernel,
        out_shape=jax.ShapeDtypeStruct((S, 2, tokens, width), keys.dtype),
        grid_spec=pltpu.PrefetchScalarGridSpec(
            num_scalar_prefetch=1,
            grid=(S,),
            in_specs=[spec, spec],
            out_specs=pl.BlockSpec((None, 2, tokens, width), lambda s, p: (s, 0, 0, 0)),
        ),
        compiler_params=params(),
        cost_estimate=pl.CostEstimate(
            flops=0, bytes_accessed=8 * S * tokens * width, transcendentals=0
        ),
        name="pack",
    )(place, *hbm(keys, values))


def pick(place, value, half):
    S, tokens, width = value.shape
    width //= 2

    def kernel(place, in_ref, out_ref):
        out_ref[...] = in_ref[...]

    return pl.pallas_call(
        kernel,
        out_shape=jax.ShapeDtypeStruct((S, tokens, width), value.dtype),
        grid_spec=pltpu.PrefetchScalarGridSpec(
            num_scalar_prefetch=1,
            grid=(S,),
            in_specs=[pl.BlockSpec((None, tokens, width), lambda s, p: (s, 0, side(half, p)))],
            out_specs=pl.BlockSpec((None, tokens, width), lambda s, p: (s, 0, 0)),
        ),
        compiler_params=params(),
        cost_estimate=pl.CostEstimate(
            flops=0, bytes_accessed=4 * S * tokens * width, transcendentals=0
        ),
        name="pick",
    )(place, *hbm(value))


def edge_attend(place, q, near, far, start, cols_tile, cols):
    count, _, tokens, width = far.shape
    heads = width // HEAD
    return pl.pallas_call(
        functools.partial(edge_kernel, heads=heads, cols_tile=cols_tile, cols=cols),
        out_shape=jax.ShapeDtypeStruct((count, tokens, width + HEAD), jnp.bfloat16),
        grid_spec=pltpu.PrefetchScalarGridSpec(
            num_scalar_prefetch=1,
            grid=(count,),
            in_specs=[
                pl.BlockSpec((None, tokens, width), lambda g, p: (start + g, 0, 0)),
                pl.BlockSpec((None, 2, tokens, width), lambda g, p: (start + g, 0, 0, 0)),
                pl.BlockSpec((None, 2, tokens, width), lambda g, p: (g, 0, 0, 0)),
            ],
            out_specs=pl.BlockSpec((None, tokens, width + HEAD), lambda g, p: (g, 0, 0)),
        ),
        compiler_params=params(),
        cost_estimate=pl.CostEstimate(
            flops=8 * count * tokens * tokens * width,
            bytes_accessed=14 * count * tokens * width,
            transcendentals=2 * count * tokens * tokens * heads,
        ),
        name="edge_rows",
    )(place, q, near, far)


def rows_attend(place, mask, reach, q, tiles, sides, far, half, stream, cols_tile, frame_tokens, grid, block=3):
    tokens, width = far.shape[2:]
    at = stream if far.shape[0] > 1 else 0
    heads = width // HEAD
    lanes = block * HEAD
    steps = heads // block
    own = pl.BlockSpec((None, 2, tokens, lanes), lambda g, p: (stream, 0, 0, g))
    near = pl.BlockSpec((None, None, 2, tokens, lanes), lambda g, p: (0, stream, 0, 0, g))
    other = pl.BlockSpec((None, None, 2, tokens, lanes), lambda g, p: (1, stream, 0, 0, g))
    args = [x for tile, pair in zip(tiles, sides) for x in (tile, pair, pair)]
    kernel = functools.partial(
        rows_kernel, heads=block, half=half, grid=grid, cols_tile=cols_tile, frame_tokens=frame_tokens
    )
    return pl.pallas_call(
        kernel,
        out_shape=(
            jax.ShapeDtypeStruct((tokens, width), jnp.float32),
            jax.ShapeDtypeStruct((tokens, width), jnp.float32),
            jax.ShapeDtypeStruct((tokens, HEAD), jnp.float32),
        ),
        grid_spec=pltpu.PrefetchScalarGridSpec(
            num_scalar_prefetch=1,
            grid=(steps,),
            in_specs=[
                SMEM,
                SMEM,
                pl.BlockSpec((None, tokens, lanes), lambda g, p: (stream, 0, side(half, p) * steps + g)),
                *[own, near, other] * 3,
                pl.BlockSpec((None, 2, tokens, lanes), lambda g, p: (at, 0, 0, g)),
            ],
            out_specs=(
                pl.BlockSpec((tokens, lanes), lambda g, p: (0, g)),
                pl.BlockSpec((tokens, lanes), lambda g, p: (0, g)),
                pl.BlockSpec((tokens, HEAD), lambda g, p: (0, 0)),
            ),
            scratch_shapes=[
                pltpu.VMEM((tokens // frame_tokens + 2, tokens, tokens), jnp.float32)
            ],
        ),
        compiler_params=params(),
        cost_estimate=pl.CostEstimate(
            flops=46 * tokens * tokens * width,
            bytes_accessed=54 * tokens * width,
            transcendentals=13 * tokens * tokens * heads,
        ),
        name="rows",
    )(place, mask, reach, *hbm(q), *args, far)


def merge(place, parts, rest, stream, cols):
    tokens, width = parts[0].shape
    at = stream if rest.shape[0] > 1 else 0
    whole = pl.BlockSpec((tokens, width), lambda g, p: (0, 0))
    return pl.pallas_call(
        functools.partial(merge_kernel, cols=cols),
        out_shape=jax.ShapeDtypeStruct((tokens, width), jnp.bfloat16),
        grid_spec=pltpu.PrefetchScalarGridSpec(
            num_scalar_prefetch=1,
            grid=(1,),
            in_specs=[
                whole,
                whole,
                pl.BlockSpec((tokens, HEAD), lambda g, p: (0, 0)),
                pl.BlockSpec((None, tokens, width), lambda g, p: (at, 0, 0)),
                pl.BlockSpec((None, tokens, HEAD), lambda g, p: (at, 0, width // HEAD)),
            ],
            out_specs=whole,
        ),
        compiler_params=params(),
        cost_estimate=pl.CostEstimate(
            flops=8 * tokens * width, bytes_accessed=12 * tokens * width, transcendentals=0
        ),
        name="merge",
    )(place, *parts, rest, rest)


def project(place, parts, rest, weight, other, output, stream, cols, block=3):
    tokens, width = parts[0].shape
    at = stream if rest.shape[0] > 1 else 0
    lanes = block * HEAD
    streams, _, model = weight.shape
    earlier = [] if output is None else [output]
    cut = pl.BlockSpec((tokens, lanes), lambda g, p: (0, g))
    args = [place, *parts, rest, rest, weight, other]
    return pl.pallas_call(
        functools.partial(project_kernel, cols=cols),
        out_shape=jax.ShapeDtypeStruct((streams, tokens, model), jnp.bfloat16),
        grid_spec=pltpu.PrefetchScalarGridSpec(
            num_scalar_prefetch=1,
            grid=(width // lanes,),
            in_specs=[
                cut,
                cut,
                pl.BlockSpec((tokens, HEAD), lambda g, p: (0, 0)),
                pl.BlockSpec((None, tokens, lanes), lambda g, p: (at, 0, g)),
                pl.BlockSpec((None, tokens, HEAD), lambda g, p: (at, 0, width // HEAD)),
                pl.BlockSpec((None, lanes, model), lambda g, p: (stream, g, 0)),
                pl.BlockSpec((tokens, model), lambda g, p: (0, 0)),
                *[ANY] * len(earlier),
            ],
            out_specs=pl.BlockSpec((None, tokens, model), lambda g, p: (stream, 0, 0)),
            scratch_shapes=[pltpu.VMEM((tokens, model), jnp.float32)],
        ),
        input_output_aliases={len(args): 0} if earlier else {},
        compiler_params=params(),
        cost_estimate=pl.CostEstimate(
            flops=2 * tokens * width * model, bytes_accessed=2 * width * model, transcendentals=0
        ),
        name="project",
    )(*args, *earlier)


def product(rows, weight, stream, block=3):
    tokens, width = rows.shape
    model = weight.shape[2]
    lanes = block * HEAD
    return pl.pallas_call(
        product_kernel,
        out_shape=jax.ShapeDtypeStruct((tokens, model), jnp.bfloat16),
        grid=(width // lanes,),
        in_specs=[
            pl.BlockSpec((tokens, lanes), lambda g: (0, g)),
            pl.BlockSpec((None, lanes, model), lambda g: (stream, g, 0)),
        ],
        out_specs=pl.BlockSpec((tokens, model), lambda g: (0, 0)),
        scratch_shapes=[pltpu.VMEM((tokens, model), jnp.float32)],
        compiler_params=params(),
        cost_estimate=pl.CostEstimate(
            flops=2 * tokens * width * model, bytes_accessed=2 * width * model, transcendentals=0
        ),
        name="product",
    )(rows, weight)


def swaps(size, start):
    pairs = [(i, i + 1) for i in range(start, size - 1, 2)]
    return pairs + [(j, i) for i, j in pairs]


def per_device(queries, key_states, value_states, tile_mask, frame_reach, out_weight):
    S, F, R, C, width = queries.shape
    tokens = F * R * C
    model = out_weight.shape[2]
    rows, cols = lax.axis_size("row"), lax.axis_size("col")
    inward = [(0, 1), (cols - 1, cols - 2)]
    outward = [(j, i) for i, j in inward]
    place = jnp.stack([lax.axis_index(a) for a in ("pair", "row", "col")]).astype(jnp.int32)
    q, k, v = [a.reshape(S, tokens, width) for a in (queries, key_states, value_states)]
    mask = tile_mask.reshape(9)

    sent = {}

    def tied(value, after):
        return lax.optimization_barrier((value, *[sent[n] for n in after]))[0] if after else value

    def send(name, value, axis, pairs, *after):
        sent[name] = lax.ppermute(tied(value, after), axis, pairs)

    col_pairs, col_others = swaps(cols, 0), swaps(cols, 1)
    row_pairs, row_others = swaps(rows, 0), swaps(rows, 1)
    pair_swap = swaps(2, 0)
    own = [pack(place, k, v, h) for h in range(2)]
    picked = [pick(place, q, h) for h in range(2)]

    def edge(name, h, start, *after):
        sent[f"part{name}"] = edge_attend(
            place, tied(sent[f"q{h}"], after), sent[f"other{h}"], sent[f"far{name}"], start, C, cols
        )

    def rows_of(name, h, s, *after):
        tiles = [sent[f"pair_own{h}"], own[h], sent[f"next_own{h}"]]
        sides = [sent[f"pair_sides{h}"], sent[f"sides{h}"], sent[f"next_sides{h}"]]
        sent[f"rows{h}{s}"] = rows_attend(
            place, tied(mask, after), frame_reach, q, tiles, sides, sent[f"far{name}"], h, s, C, R * C, (rows, cols)
        )

    send("near0", own[0], "col", col_pairs)
    send("other0", own[0], "col", col_others)
    send("next_own0", own[0], "row", row_others)
    send("pair_own0", own[0], "row", row_pairs)
    send("q0", picked[0], "col", inward)
    send("far00", sent["near0"][:1], "col", col_others, "other0", "next_own0")
    send("far01", sent["near0"][1:], "col", col_others, "other0", "next_own0")
    sent["sides0"] = jnp.stack([sent["near0"], sent["other0"]])
    send("next_sides0", sent["sides0"], "row", row_others)
    send("pair_sides0", sent["sides0"], "row", row_pairs, "pair_own0")
    edge("00", 0, 0)
    send("rest00", sent["part00"], "col", outward)
    send("near1", own[1], "col", col_pairs, "rest00")
    send("other1", own[1], "col", col_others, "far00")
    edge("01", 0, 1)
    send("rest01", sent["part01"], "col", outward)
    rows_of("00", 0, 0)
    rows_of("01", 0, 1)
    sent["merged0"] = merge(tied(place, []), sent["rows00"], sent["rest00"], 0, cols)
    send("theirs0", sent["merged0"], "pair", pair_swap)
    sent["merged1"] = merge(tied(place, []), sent["rows01"], sent["rest01"], 1, cols)
    send("theirs1", sent["merged1"], "pair", pair_swap)
    send("next_own1", own[1], "row", row_others, "next_sides0")
    send("pair_own1", own[1], "row", row_pairs)
    send("q1", picked[1], "col", inward, "rest01")
    sent["product0"] = product(tied(sent["theirs0"], []), out_weight, 0)
    send("back0", sent["product0"], "pair", pair_swap)
    sent["product1"] = product(tied(sent["theirs1"], []), out_weight, 1)
    send("back1", sent["product1"], "pair", pair_swap)
    send("far10", sent["near1"][:1], "col", col_others, "far01")
    send("far11", sent["near1"][1:], "col", col_others, "other1")
    sent["sides1"] = jnp.stack([sent["near1"], sent["other1"]])
    send("next_sides1", sent["sides1"], "row", row_others)
    send("pair_sides1", sent["sides1"], "row", row_pairs)
    edge("10", 1, 0)
    send("rest10", sent["part10"], "col", outward)
    edge("11", 1, 1)
    send("rest11", sent["part11"], "col", outward)
    rows_of("10", 1, 0)
    rows_of("11", 1, 1)
    output = project(tied(place, []), sent["rows10"], sent["rest10"], out_weight, sent["back0"], None, 0, cols)
    output = project(place, sent["rows11"], sent["rest11"], out_weight, sent["back1"], output, 1, cols)
    return output.reshape(S, F, R, C, model)


def solution(mesh):
    return jax.shard_map(
        per_device,
        mesh=mesh,
        in_specs=(
            P("pair", None, "row", "col", None),
            P("pair", None, "row", "col", None),
            P("pair", None, "row", "col", None),
            P("pair", "row", "col", None),
            P(),
            P(None, "pair", None),
        ),
        out_specs=P("pair", None, "row", "col", None),
        check_vma=False,
    )
```

```python
import functools
import math

import jax
import jax.numpy as jnp
from jax import lax
from jax.experimental import pallas as pl
from jax.experimental.pallas import tpu as pltpu
from jax.sharding import PartitionSpec as P

NEG = -1e30
VMEM_LIMIT = 24 * 1024 * 1024
HEAD = 128
TO_LOG2 = HEAD ** (-0.5) * math.log2(math.e)
ANY = pl.BlockSpec(memory_space=pl.ANY)
SMEM = pl.BlockSpec(memory_space=pltpu.SMEM)


def dot_nn(a, b):
    return lax.dot_general(a, b, (((1,), (0,)), ((), ())), preferred_element_type=jnp.float32)


def group_gap(tokens, group):
    q = lax.broadcasted_iota(jnp.int32, (tokens, tokens), 0)
    k = lax.broadcasted_iota(jnp.int32, (tokens, tokens), 1)
    return jnp.abs(q // group - k // group)


def softmax_sums(scores, values):
    tops = [jnp.max(functools.reduce(jnp.maximum, tiles), axis=1, keepdims=True) for tiles in scores]
    weights = [
        [jnp.exp2((s - top) * TO_LOG2) for s in tiles] for tiles, top in zip(scores, tops)
    ]
    sums = [jnp.sum(functools.reduce(jnp.add, w), axis=1, keepdims=True) for w in weights]
    totals = [
        dot_nn(
            jnp.concatenate([x.astype(jnp.bfloat16) for x in w], axis=1),
            jnp.concatenate(tiles, axis=0),
        )
        for w, tiles in zip(weights, values)
    ]
    return [top * TO_LOG2 for top in tops], totals, sums


def place_pieces(stats, values, first):
    lane = lax.broadcasted_iota(jnp.int32, stats.shape, 1)
    for n, value in enumerate(values):
        at = 3 * (first + n)
        high = value.astype(jnp.bfloat16).astype(jnp.float32)
        mid = (value - high).astype(jnp.bfloat16).astype(jnp.float32)
        stats = jnp.where(lane == at, high, stats)
        stats = jnp.where(lane == at + 1, mid, stats)
        stats = jnp.where(lane == at + 2, value - high - mid, stats)
    return stats


def spread_pieces(stats, first, heads):
    lane = lax.broadcasted_iota(jnp.int32, (HEAD, heads * HEAD), 0)
    at = 3 * (first + lax.broadcasted_iota(jnp.int32, (HEAD, heads * HEAD), 1) // HEAD)
    pick_head = jnp.where((lane >= at) & (lane < at + 3), 1.0, 0.0).astype(jnp.bfloat16)
    return dot_nn(stats, pick_head)


def edge_kernel(place, q_ref, near_ref, far_ref, out_ref, *, heads, cols_tile, cols):
    tokens = q_ref.shape[0]

    @pl.when((place[2] > 0) & (place[2] < cols - 1))
    def _():
        bias = jnp.where(group_gap(tokens, cols_tile) == 0, 0.0, NEG)
        cuts = [slice(n * HEAD, (n + 1) * HEAD) for n in range(heads)]
        tiles = (near_ref, far_ref)
        scores = [[dot_nn(q_ref[:, c], t[0, :, c]) + bias for t in tiles] for c in cuts]
        values = [[t[1, :, c] for t in tiles] for c in cuts]
        tops, totals, weights = softmax_sums(scores, values)
        lse = [top + jnp.log2(w) for top, w in zip(tops, weights)]
        stats = place_pieces(jnp.zeros((tokens, HEAD), jnp.float32), lse, 0)
        out_ref[:, :heads * HEAD] = jnp.concatenate(
            [(t / w).astype(jnp.bfloat16) for t, w in zip(totals, weights)], axis=1
        )
        out_ref[:, heads * HEAD:] = stats.astype(jnp.bfloat16)


def fill_bias(bias_ref, frame_tokens, cols_tile):
    tokens = bias_ref.shape[1]
    frames = tokens // frame_tokens
    gap = group_gap(tokens, frame_tokens)
    for reach in range(frames):
        bias_ref[reach] = jnp.where(gap <= reach, 0.0, NEG)
    bias_ref[frames] = jnp.full((tokens, tokens), NEG, jnp.float32)
    bias_ref[frames + 1] = jnp.where(group_gap(tokens, cols_tile) == 0, 0.0, NEG)


def rows_kernel(place, mask, reach, q_ref, *refs, heads, half, grid, cols_tile, frame_tokens):
    tiles = refs[:10]
    window_ref, row_ref, sums_ref, bias_ref = refs[10:]
    tokens = q_ref.shape[0]
    none = bias_ref.shape[0] - 2
    step = pl.program_id(0)

    @pl.when(step == 0)
    def _():
        fill_bias(bias_ref, frame_tokens, cols_tile)
        sums_ref[...] = jnp.zeros_like(sums_ref)

    rows, cols = grid
    row, col = place[1], place[2]
    row_sign, col_sign = 1 - 2 * (row % 2), 1 - 2 * (col % 2)
    row_steps, col_steps = (row_sign, 0, -row_sign), (0, col_sign, -col_sign)
    listed = []
    for a in row_steps:
        for b in col_steps:
            inside = (row + a >= 0) & (row + a < rows) & (col + b >= 0) & (col + b < cols)
            listed.append(inside & ((mask[3 * (a + 1) + b + 1] > 0) | ((a == 0) & (b == 0))))
    inner = (col > 0) & (col < cols - 1)
    first_head = side(half, place) * heads * pl.num_programs(0)
    cuts = [slice(n * HEAD, (n + 1) * HEAD) for n in range(heads)]
    raw = []
    for c in cuts:
        scores = dot_nn(q_ref[:, c], jnp.concatenate([t[0, :, c] for t in tiles], axis=1))
        raw.append([scores[:, t * tokens:(t + 1) * tokens] for t in range(10)])
    values = [[t[1, :, c] for t in tiles] for c in cuts]
    window, row_scores = [], []
    row_bias = bias_ref[none + 1]
    outer_bias = bias_ref[jnp.where(inner, none + 1, none)]
    for n in range(heads):
        limit = reach[first_head + step * heads + n]
        window.append(
            [raw[n][t] + bias_ref[jnp.where(listed[t], limit, none)] for t in range(9)]
        )
        row_scores.append(
            [raw[n][3] + row_bias, raw[n][4] + row_bias, raw[n][5] + outer_bias, raw[n][9] + outer_bias]
        )
    _, totals, weights = softmax_sums(window, [v[:9] for v in values])
    window_ref[...] = jnp.concatenate([t / w for t, w in zip(totals, weights)], axis=1)
    tops, totals, weights = softmax_sums(row_scores, [v[3:6] + v[9:] for v in values])
    row_ref[...] = jnp.concatenate([t / w for t, w in zip(totals, weights)], axis=1)
    lse = [top + jnp.log2(w) for top, w in zip(tops, weights)]
    sums = place_pieces(sums_ref[...].astype(jnp.float32), lse, step * heads)
    sums_ref[...] = sums.astype(jnp.bfloat16)


def merged(place, window, row, sums, rest, stats, cols, first, heads):
    inner = (place[2] > 0) & (place[2] < cols - 1)
    near = spread_pieces(sums, first, heads)
    far = jnp.where(inner, NEG, spread_pieces(stats, first, heads))
    share = 1.0 / (1.0 + jnp.exp2(near - far))
    axial = row + (rest.astype(jnp.float32) - row) * share
    return (window + axial).astype(jnp.bfloat16)


def merge_kernel(place, window_ref, row_ref, sums_ref, rest_ref, stats_ref, out_ref, *, cols):
    out_ref[...] = merged(
        place, window_ref[...], row_ref[...], sums_ref[...], rest_ref[...], stats_ref[...], cols,
        0, out_ref.shape[1] // HEAD,
    )


def add_product(total_ref, rows, weight_ref, lanes=512):
    for start in range(0, total_ref.shape[1], lanes):
        cut = slice(start, start + lanes)
        total_ref[:, cut] += dot_nn(rows, weight_ref[:, cut])


def project_kernel(place, window_ref, row_ref, sums_ref, rest_ref, stats_ref, weight_ref, other_ref, *refs, cols):
    out_ref, total_ref = refs[-2:]

    @pl.when(pl.program_id(0) == 0)
    def _():
        total_ref[...] = other_ref[...].astype(jnp.float32)

    heads = window_ref.shape[1] // HEAD
    rows = merged(
        place, window_ref[...], row_ref[...], sums_ref[...], rest_ref[...], stats_ref[...], cols,
        pl.program_id(0) * heads, heads,
    )
    add_product(total_ref, rows, weight_ref)

    @pl.when(pl.program_id(0) == pl.num_programs(0) - 1)
    def _():
        out_ref[...] = total_ref[...].astype(jnp.bfloat16)


def product_kernel(rows_ref, weight_ref, out_ref, total_ref):
    @pl.when(pl.program_id(0) == 0)
    def _():
        total_ref[...] = jnp.zeros_like(total_ref)

    add_product(total_ref, rows_ref[...], weight_ref)

    @pl.when(pl.program_id(0) == pl.num_programs(0) - 1)
    def _():
        out_ref[...] = total_ref[...].astype(jnp.bfloat16)


def hbm(*values):
    return [pltpu.with_memory_space_constraint(v, pltpu.HBM) for v in values]


def params():
    return pltpu.CompilerParams(vmem_limit_bytes=VMEM_LIMIT)


def side(half, place):
    return half + (1 - 2 * half) * (1 - place[0])


def pack(place, keys, values, half):
    S, tokens, width = keys.shape
    width //= 2
    spec = pl.BlockSpec((None, tokens, width), lambda s, p: (s, 0, side(half, p)))

    def kernel(place, k_ref, v_ref, out_ref):
        for start in range(0, width, HEAD):
            cut = slice(start, start + HEAD)
            out_ref[0, :, cut] = k_ref[:, cut].T
        out_ref[1] = v_ref[...]

    return pl.pallas_call(
        kernel,
        out_shape=jax.ShapeDtypeStruct((S, 2, tokens, width), keys.dtype),
        grid_spec=pltpu.PrefetchScalarGridSpec(
            num_scalar_prefetch=1,
            grid=(S,),
            in_specs=[spec, spec],
            out_specs=pl.BlockSpec((None, 2, tokens, width), lambda s, p: (s, 0, 0, 0)),
        ),
        compiler_params=params(),
        cost_estimate=pl.CostEstimate(
            flops=0, bytes_accessed=8 * S * tokens * width, transcendentals=0
        ),
        name="pack",
    )(place, *hbm(keys, values))


def pick(place, value, half):
    S, tokens, width = value.shape
    width //= 2

    def kernel(place, in_ref, out_ref):
        out_ref[...] = in_ref[...]

    return pl.pallas_call(
        kernel,
        out_shape=jax.ShapeDtypeStruct((S, tokens, width), value.dtype),
        grid_spec=pltpu.PrefetchScalarGridSpec(
            num_scalar_prefetch=1,
            grid=(S,),
            in_specs=[pl.BlockSpec((None, tokens, width), lambda s, p: (s, 0, side(half, p)))],
            out_specs=pl.BlockSpec((None, tokens, width), lambda s, p: (s, 0, 0)),
        ),
        compiler_params=params(),
        cost_estimate=pl.CostEstimate(
            flops=0, bytes_accessed=4 * S * tokens * width, transcendentals=0
        ),
        name="pick",
    )(place, *hbm(value))


def edge_attend(place, q, near, far, start, cols_tile, cols):
    count, _, tokens, width = far.shape
    heads = width // HEAD
    return pl.pallas_call(
        functools.partial(edge_kernel, heads=heads, cols_tile=cols_tile, cols=cols),
        out_shape=jax.ShapeDtypeStruct((count, tokens, width + HEAD), jnp.bfloat16),
        grid_spec=pltpu.PrefetchScalarGridSpec(
            num_scalar_prefetch=1,
            grid=(count,),
            in_specs=[
                pl.BlockSpec((None, tokens, width), lambda g, p: (start + g, 0, 0)),
                pl.BlockSpec((None, 2, tokens, width), lambda g, p: (start + g, 0, 0, 0)),
                pl.BlockSpec((None, 2, tokens, width), lambda g, p: (g, 0, 0, 0)),
            ],
            out_specs=pl.BlockSpec((None, tokens, width + HEAD), lambda g, p: (g, 0, 0)),
        ),
        compiler_params=params(),
        cost_estimate=pl.CostEstimate(
            flops=8 * count * tokens * tokens * width,
            bytes_accessed=14 * count * tokens * width,
            transcendentals=2 * count * tokens * tokens * heads,
        ),
        name="edge_rows",
    )(place, q, near, far)


def rows_attend(place, mask, reach, q, tiles, sides, far, half, stream, cols_tile, frame_tokens, grid, block=3):
    tokens, width = far.shape[2:]
    at = stream if far.shape[0] > 1 else 0
    heads = width // HEAD
    lanes = block * HEAD
    steps = heads // block
    own = pl.BlockSpec((None, 2, tokens, lanes), lambda g, p: (stream, 0, 0, g))
    near = pl.BlockSpec((None, None, 2, tokens, lanes), lambda g, p: (0, stream, 0, 0, g))
    other = pl.BlockSpec((None, None, 2, tokens, lanes), lambda g, p: (1, stream, 0, 0, g))
    args = [x for tile, pair in zip(tiles, sides) for x in (tile, pair, pair)]
    kernel = functools.partial(
        rows_kernel, heads=block, half=half, grid=grid, cols_tile=cols_tile, frame_tokens=frame_tokens
    )
    return pl.pallas_call(
        kernel,
        out_shape=(
            jax.ShapeDtypeStruct((tokens, width), jnp.float32),
            jax.ShapeDtypeStruct((tokens, width), jnp.float32),
            jax.ShapeDtypeStruct((tokens, HEAD), jnp.bfloat16),
        ),
        grid_spec=pltpu.PrefetchScalarGridSpec(
            num_scalar_prefetch=1,
            grid=(steps,),
            in_specs=[
                SMEM,
                SMEM,
                pl.BlockSpec((None, tokens, lanes), lambda g, p: (stream, 0, side(half, p) * steps + g)),
                *[own, near, other] * 3,
                pl.BlockSpec((None, 2, tokens, lanes), lambda g, p: (at, 0, 0, g)),
            ],
            out_specs=(
                pl.BlockSpec((tokens, lanes), lambda g, p: (0, g)),
                pl.BlockSpec((tokens, lanes), lambda g, p: (0, g)),
                pl.BlockSpec((tokens, HEAD), lambda g, p: (0, 0)),
            ),
            scratch_shapes=[
                pltpu.VMEM((tokens // frame_tokens + 2, tokens, tokens), jnp.float32)
            ],
        ),
        compiler_params=params(),
        cost_estimate=pl.CostEstimate(
            flops=46 * tokens * tokens * width,
            bytes_accessed=54 * tokens * width,
            transcendentals=13 * tokens * tokens * heads,
        ),
        name="rows",
    )(place, mask, reach, *hbm(q), *args, far)


def merge(place, parts, rest, stream, cols):
    tokens, width = parts[0].shape
    at = stream if rest.shape[0] > 1 else 0
    whole = pl.BlockSpec((tokens, width), lambda g, p: (0, 0))
    return pl.pallas_call(
        functools.partial(merge_kernel, cols=cols),
        out_shape=jax.ShapeDtypeStruct((tokens, width), jnp.bfloat16),
        grid_spec=pltpu.PrefetchScalarGridSpec(
            num_scalar_prefetch=1,
            grid=(1,),
            in_specs=[
                whole,
                whole,
                pl.BlockSpec((tokens, HEAD), lambda g, p: (0, 0)),
                pl.BlockSpec((None, tokens, width), lambda g, p: (at, 0, 0)),
                pl.BlockSpec((None, tokens, HEAD), lambda g, p: (at, 0, width // HEAD)),
            ],
            out_specs=whole,
        ),
        compiler_params=params(),
        cost_estimate=pl.CostEstimate(
            flops=8 * tokens * width, bytes_accessed=12 * tokens * width, transcendentals=0
        ),
        name="merge",
    )(place, *parts, rest, rest)


def project(place, parts, rest, weight, other, output, stream, cols, block=3):
    tokens, width = parts[0].shape
    at = stream if rest.shape[0] > 1 else 0
    lanes = block * HEAD
    streams, _, model = weight.shape
    earlier = [] if output is None else [output]
    cut = pl.BlockSpec((tokens, lanes), lambda g, p: (0, g))
    args = [place, *parts, rest, rest, weight, other]
    return pl.pallas_call(
        functools.partial(project_kernel, cols=cols),
        out_shape=jax.ShapeDtypeStruct((streams, tokens, model), jnp.bfloat16),
        grid_spec=pltpu.PrefetchScalarGridSpec(
            num_scalar_prefetch=1,
            grid=(width // lanes,),
            in_specs=[
                cut,
                cut,
                pl.BlockSpec((tokens, HEAD), lambda g, p: (0, 0)),
                pl.BlockSpec((None, tokens, lanes), lambda g, p: (at, 0, g)),
                pl.BlockSpec((None, tokens, HEAD), lambda g, p: (at, 0, width // HEAD)),
                pl.BlockSpec((None, lanes, model), lambda g, p: (stream, g, 0)),
                pl.BlockSpec((tokens, model), lambda g, p: (0, 0)),
                *[ANY] * len(earlier),
            ],
            out_specs=pl.BlockSpec((None, tokens, model), lambda g, p: (stream, 0, 0)),
            scratch_shapes=[pltpu.VMEM((tokens, model), jnp.float32)],
        ),
        input_output_aliases={len(args): 0} if earlier else {},
        compiler_params=params(),
        cost_estimate=pl.CostEstimate(
            flops=2 * tokens * width * model, bytes_accessed=2 * width * model, transcendentals=0
        ),
        name="project",
    )(*args, *earlier)


def product(rows, weight, stream, block=3):
    tokens, width = rows.shape
    model = weight.shape[2]
    lanes = block * HEAD
    return pl.pallas_call(
        product_kernel,
        out_shape=jax.ShapeDtypeStruct((tokens, model), jnp.bfloat16),
        grid=(width // lanes,),
        in_specs=[
            pl.BlockSpec((tokens, lanes), lambda g: (0, g)),
            pl.BlockSpec((None, lanes, model), lambda g: (stream, g, 0)),
        ],
        out_specs=pl.BlockSpec((tokens, model), lambda g: (0, 0)),
        scratch_shapes=[pltpu.VMEM((tokens, model), jnp.float32)],
        compiler_params=params(),
        cost_estimate=pl.CostEstimate(
            flops=2 * tokens * width * model, bytes_accessed=2 * width * model, transcendentals=0
        ),
        name="product",
    )(rows, weight)


def swaps(size, start):
    pairs = [(i, i + 1) for i in range(start, size - 1, 2)]
    return pairs + [(j, i) for i, j in pairs]


def per_device(queries, key_states, value_states, tile_mask, frame_reach, out_weight):
    S, F, R, C, width = queries.shape
    tokens = F * R * C
    model = out_weight.shape[2]
    rows, cols = lax.axis_size("row"), lax.axis_size("col")
    inward = [(0, 1), (cols - 1, cols - 2)]
    outward = [(j, i) for i, j in inward]
    place = jnp.stack([lax.axis_index(a) for a in ("pair", "row", "col")]).astype(jnp.int32)
    q, k, v = [a.reshape(S, tokens, width) for a in (queries, key_states, value_states)]
    mask = tile_mask.reshape(9)

    sent = {}

    def tied(value, after):
        return lax.optimization_barrier((value, *[sent[n] for n in after]))[0] if after else value

    def send(name, value, axis, pairs, *after):
        sent[name] = lax.ppermute(tied(value, after), axis, pairs)

    col_pairs, col_others = swaps(cols, 0), swaps(cols, 1)
    row_pairs, row_others = swaps(rows, 0), swaps(rows, 1)
    pair_swap = swaps(2, 0)
    own = [pack(place, k, v, h) for h in range(2)]
    picked = [pick(place, q, h) for h in range(2)]

    def edge(name, h, start, *after):
        sent[f"part{name}"] = edge_attend(
            place, tied(sent[f"q{h}"], after), sent[f"other{h}"], sent[f"far{name}"], start, C, cols
        )

    def rows_of(name, h, s, *after):
        tiles = [sent[f"pair_own{h}"], own[h], sent[f"next_own{h}"]]
        sides = [sent[f"pair_sides{h}"], sent[f"sides{h}"], sent[f"next_sides{h}"]]
        sent[f"rows{h}{s}"] = rows_attend(
            place, tied(mask, after), frame_reach, q, tiles, sides, sent[f"far{name}"], h, s, C, R * C, (rows, cols)
        )

    send("near0", own[0], "col", col_pairs)
    send("other0", own[0], "col", col_others)
    send("next_own0", own[0], "row", row_others)
    send("pair_own0", own[0], "row", row_pairs)
    send("q0", picked[0], "col", inward)
    send("far00", sent["near0"][:1], "col", col_others, "next_own0")
    send("far01", sent["near0"][1:], "col", col_others, "other0", "next_own0")
    sent["sides0"] = jnp.stack([sent["near0"], sent["other0"]])
    send("next_sides0", sent["sides0"], "row", row_others)
    send("pair_sides0", sent["sides0"], "row", row_pairs, "pair_own0", "far01")
    edge("00", 0, 0)
    send("rest00", sent["part00"], "col", outward)
    send("near1", own[1], "col", col_pairs, "rest00")
    send("other1", own[1], "col", col_others, "far00")
    edge("01", 0, 1)
    send("rest01", sent["part01"], "col", outward)
    rows_of("00", 0, 0)
    rows_of("01", 0, 1)
    sent["merged0"] = merge(tied(place, []), sent["rows00"], sent["rest00"], 0, cols)
    send("theirs0", sent["merged0"], "pair", pair_swap)
    sent["merged1"] = merge(tied(place, []), sent["rows01"], sent["rest01"], 1, cols)
    send("theirs1", sent["merged1"], "pair", pair_swap, "rest00")
    send("next_own1", own[1], "row", row_others)
    send("pair_own1", own[1], "row", row_pairs)
    send("q1", picked[1], "col", inward, "rest01")
    sent["product0"] = product(tied(sent["theirs0"], []), out_weight, 0)
    send("back0", sent["product0"], "pair", pair_swap)
    sent["product1"] = product(tied(sent["theirs1"], []), out_weight, 1)
    send("back1", sent["product1"], "pair", pair_swap)
    send("far10", sent["near1"][:1], "col", col_others, "far01")
    send("far11", sent["near1"][1:], "col", col_others, "other1")
    sent["sides1"] = jnp.stack([sent["near1"], sent["other1"]])
    send("next_sides1", sent["sides1"], "row", row_others)
    send("pair_sides1", sent["sides1"], "row", row_pairs)
    edge("10", 1, 0)
    send("rest10", sent["part10"], "col", outward)
    edge("11", 1, 1)
    send("rest11", sent["part11"], "col", outward)
    rows_of("10", 1, 0)
    rows_of("11", 1, 1)
    output = project(tied(place, []), sent["rows10"], sent["rest10"], out_weight, sent["back0"], None, 0, cols)
    output = project(place, sent["rows11"], sent["rest11"], out_weight, sent["back1"], output, 1, cols)
    return output.reshape(S, F, R, C, model)


def solution(mesh):
    return jax.shard_map(
        per_device,
        mesh=mesh,
        in_specs=(
            P("pair", None, "row", "col", None),
            P("pair", None, "row", "col", None),
            P("pair", None, "row", "col", None),
            P("pair", "row", "col", None),
            P(),
            P(None, "pair", None),
        ),
        out_specs=P("pair", None, "row", "col", None),
        check_vma=False,
    )
```

```python
import functools
import math

import jax
import jax.numpy as jnp
from jax import lax
from jax.experimental import pallas as pl
from jax.experimental.pallas import tpu as pltpu
from jax.sharding import PartitionSpec as P

NEG = -1e30
VMEM_LIMIT = 24 * 1024 * 1024
HEAD = 128
FOLD = 16
TO_LOG2 = HEAD ** (-0.5) * math.log2(math.e)
ANY = pl.BlockSpec(memory_space=pl.ANY)
SMEM = pl.BlockSpec(memory_space=pltpu.SMEM)


def dot_nn(a, b):
    return lax.dot_general(a, b, (((1,), (0,)), ((), ())), preferred_element_type=jnp.float32)


def group_gap(tokens, group):
    q = lax.broadcasted_iota(jnp.int32, (tokens, tokens), 0)
    k = lax.broadcasted_iota(jnp.int32, (tokens, tokens), 1)
    return jnp.abs(q // group - k // group)


def softmax_sums(scores, values):
    tops = [jnp.max(functools.reduce(jnp.maximum, tiles), axis=1, keepdims=True) for tiles in scores]
    weights = [
        [jnp.exp2((s - top) * TO_LOG2) for s in tiles] for tiles, top in zip(scores, tops)
    ]
    sums = [jnp.sum(functools.reduce(jnp.add, w), axis=1, keepdims=True) for w in weights]
    totals = [
        dot_nn(
            jnp.concatenate([x.astype(jnp.bfloat16) for x in w], axis=1),
            jnp.concatenate(tiles, axis=0),
        )
        for w, tiles in zip(weights, values)
    ]
    return [top * TO_LOG2 for top in tops], totals, sums


def place_pieces(stats, values, first):
    lane = lax.broadcasted_iota(jnp.int32, stats.shape, 1)
    for n, value in enumerate(values):
        at = 3 * (first + n)
        high = value.astype(jnp.bfloat16).astype(jnp.float32)
        mid = (value - high).astype(jnp.bfloat16).astype(jnp.float32)
        stats = jnp.where(lane == at, high, stats)
        stats = jnp.where(lane == at + 1, mid, stats)
        stats = jnp.where(lane == at + 2, value - high - mid, stats)
    return stats


def spread_pieces(stats, first, heads):
    lane = lax.broadcasted_iota(jnp.int32, (HEAD, heads * HEAD), 0)
    at = 3 * (first + lax.broadcasted_iota(jnp.int32, (HEAD, heads * HEAD), 1) // HEAD)
    pick_head = jnp.where((lane >= at) & (lane < at + 3), 1.0, 0.0).astype(jnp.bfloat16)
    return dot_nn(stats, pick_head)


def fold_stats(stats, width):
    groups = [stats[start:start + FOLD] for start in range(0, stats.shape[0], FOLD)]
    rest = width // HEAD - len(groups)
    return jnp.concatenate(groups + [jnp.zeros_like(groups[0])] * rest, axis=1)


def unfold_stats(folded, tokens):
    return jnp.concatenate(
        [folded[:, n * HEAD:(n + 1) * HEAD] for n in range(tokens // FOLD)], axis=0
    )


def edge_kernel(place, q_ref, near_ref, far_ref, *refs, heads, cols_tile, cols):
    tokens = q_ref.shape[0]
    out_ref = refs[-1]
    first = 0
    if len(refs) > 1:
        next_ref, next_q_ref = refs[:2]
        first = 2 * tokens
        out_ref[:tokens] = next_ref[0]
        out_ref[tokens:first] = next_ref[1]
    inner = (place[2] > 0) & (place[2] < cols - 1)

    @pl.when(jnp.logical_not(inner))
    def _():
        if first:
            out_ref[first:first + tokens] = next_q_ref[...]
        else:
            out_ref[:tokens] = jnp.zeros((tokens, out_ref.shape[1]), out_ref.dtype)
        out_ref[first + tokens:] = jnp.zeros((FOLD, out_ref.shape[1]), out_ref.dtype)

    @pl.when(inner)
    def _():
        bias = jnp.where(group_gap(tokens, cols_tile) == 0, 0.0, NEG)
        cuts = [slice(n * HEAD, (n + 1) * HEAD) for n in range(heads)]
        tiles = (near_ref, far_ref)
        scores = [[dot_nn(q_ref[:, c], t[0, :, c]) + bias for t in tiles] for c in cuts]
        values = [[t[1, :, c] for t in tiles] for c in cuts]
        tops, totals, weights = softmax_sums(scores, values)
        lse = [top + jnp.log2(w) for top, w in zip(tops, weights)]
        stats = place_pieces(jnp.zeros((tokens, HEAD), jnp.float32), lse, 0)
        out_ref[first:first + tokens] = jnp.concatenate(
            [(t / w).astype(jnp.bfloat16) for t, w in zip(totals, weights)], axis=1
        )
        out_ref[first + tokens:] = fold_stats(stats.astype(jnp.bfloat16), out_ref.shape[1])


def fill_bias(bias_ref, frame_tokens, cols_tile):
    tokens = bias_ref.shape[1]
    frames = tokens // frame_tokens
    gap = group_gap(tokens, frame_tokens)
    for reach in range(frames):
        bias_ref[reach] = jnp.where(gap <= reach, 0.0, NEG)
    bias_ref[frames] = jnp.full((tokens, tokens), NEG, jnp.float32)
    bias_ref[frames + 1] = jnp.where(group_gap(tokens, cols_tile) == 0, 0.0, NEG)


def rows_kernel(place, mask, reach, q_ref, *refs, heads, half, grid, cols_tile, frame_tokens):
    tiles = refs[:10]
    window_ref, row_ref, sums_ref, bias_ref = refs[10:]
    tokens = q_ref.shape[0]
    none = bias_ref.shape[0] - 2
    step = pl.program_id(0)

    @pl.when(step == 0)
    def _():
        fill_bias(bias_ref, frame_tokens, cols_tile)
        sums_ref[...] = jnp.zeros_like(sums_ref)

    rows, cols = grid
    row, col = place[1], place[2]
    row_sign, col_sign = 1 - 2 * (row % 2), 1 - 2 * (col % 2)
    row_steps, col_steps = (row_sign, 0, -row_sign), (0, col_sign, -col_sign)
    listed = []
    for a in row_steps:
        for b in col_steps:
            inside = (row + a >= 0) & (row + a < rows) & (col + b >= 0) & (col + b < cols)
            listed.append(inside & ((mask[3 * (a + 1) + b + 1] > 0) | ((a == 0) & (b == 0))))
    inner = (col > 0) & (col < cols - 1)
    first_head = side(half, place) * heads * pl.num_programs(0)
    cuts = [slice(n * HEAD, (n + 1) * HEAD) for n in range(heads)]
    raw = []
    for c in cuts:
        scores = dot_nn(q_ref[:, c], jnp.concatenate([t[0, :, c] for t in tiles], axis=1))
        raw.append([scores[:, t * tokens:(t + 1) * tokens] for t in range(10)])
    values = [[t[1, :, c] for t in tiles] for c in cuts]
    window, row_scores = [], []
    row_bias = bias_ref[none + 1]
    outer_bias = bias_ref[jnp.where(inner, none + 1, none)]
    for n in range(heads):
        limit = reach[first_head + step * heads + n]
        window.append(
            [raw[n][t] + bias_ref[jnp.where(listed[t], limit, none)] for t in range(9)]
        )
        row_scores.append(
            [raw[n][3] + row_bias, raw[n][4] + row_bias, raw[n][5] + outer_bias, raw[n][9] + outer_bias]
        )
    _, totals, weights = softmax_sums(window, [v[:9] for v in values])
    window_ref[...] = jnp.concatenate([t / w for t, w in zip(totals, weights)], axis=1)
    tops, totals, weights = softmax_sums(row_scores, [v[3:6] + v[9:] for v in values])
    row_ref[...] = jnp.concatenate([t / w for t, w in zip(totals, weights)], axis=1)
    lse = [top + jnp.log2(w) for top, w in zip(tops, weights)]
    sums = place_pieces(sums_ref[...].astype(jnp.float32), lse, step * heads)
    sums_ref[...] = sums.astype(jnp.bfloat16)


def merged(place, window, row, sums, rest, stats, cols, first, heads):
    inner = (place[2] > 0) & (place[2] < cols - 1)
    near = spread_pieces(sums, first, heads)
    far = jnp.where(inner, NEG, spread_pieces(stats, first, heads))
    share = 1.0 / (1.0 + jnp.exp2(near - far))
    axial = row + (rest.astype(jnp.float32) - row) * share
    return (window + axial).astype(jnp.bfloat16)


def merge_kernel(place, window_ref, row_ref, sums_ref, rest_ref, stats_ref, out_ref, *, cols):
    out_ref[...] = merged(
        place, window_ref[...], row_ref[...], sums_ref[...], rest_ref[...],
        unfold_stats(stats_ref[...], rest_ref.shape[0]), cols, 0, out_ref.shape[1] // HEAD,
    )


def add_product(total_ref, rows, weight_ref, lanes=512):
    for start in range(0, total_ref.shape[1], lanes):
        cut = slice(start, start + lanes)
        total_ref[:, cut] += dot_nn(rows, weight_ref[:, cut])


def project_kernel(place, window_ref, row_ref, sums_ref, rest_ref, stats_ref, weight_ref, other_ref, *refs, cols):
    out_ref, total_ref = refs[-2:]

    @pl.when(pl.program_id(0) == 0)
    def _():
        total_ref[...] = other_ref[...].astype(jnp.float32)

    heads = window_ref.shape[1] // HEAD
    rows = merged(
        place, window_ref[...], row_ref[...], sums_ref[...], rest_ref[...],
        unfold_stats(stats_ref[...], rest_ref.shape[0]), cols, pl.program_id(0) * heads, heads,
    )
    add_product(total_ref, rows, weight_ref)

    @pl.when(pl.program_id(0) == pl.num_programs(0) - 1)
    def _():
        out_ref[...] = total_ref[...].astype(jnp.bfloat16)


def product_kernel(rows_ref, weight_ref, out_ref, total_ref):
    @pl.when(pl.program_id(0) == 0)
    def _():
        total_ref[...] = jnp.zeros_like(total_ref)

    add_product(total_ref, rows_ref[...], weight_ref)

    @pl.when(pl.program_id(0) == pl.num_programs(0) - 1)
    def _():
        out_ref[...] = total_ref[...].astype(jnp.bfloat16)


def hbm(*values):
    return [pltpu.with_memory_space_constraint(v, pltpu.HBM) for v in values]


def params():
    return pltpu.CompilerParams(vmem_limit_bytes=VMEM_LIMIT)


def side(half, place):
    return half + (1 - 2 * half) * (1 - place[0])


def pack(place, keys, values, half, earlier=None):
    S, tokens, width = keys.shape
    width //= 2
    spec = pl.BlockSpec((None, tokens, width), lambda h, s, p: (s, 0, side(half, p)))
    block = (None, None, 2, tokens, width)
    given = [] if earlier is None else [earlier]

    def turn(k_ref, v_ref, out_ref):
        for start in range(0, width, HEAD):
            cut = slice(start, start + HEAD)
            out_ref[0, :, cut] = k_ref[:, cut].T
        out_ref[1] = v_ref[...]

    def kernel(place, k_ref, v_ref, *refs):
        out_ref = refs[-1]
        if not given:
            turn(k_ref, v_ref, out_ref)
            return

        @pl.when(pl.program_id(0) == 0)
        def _():
            out_ref[...] = refs[0][...]

        @pl.when(pl.program_id(0) == 1)
        def _():
            turn(k_ref, v_ref, out_ref)

    return pl.pallas_call(
        kernel,
        out_shape=jax.ShapeDtypeStruct((1 + len(given), S, 2, tokens, width), keys.dtype),
        grid_spec=pltpu.PrefetchScalarGridSpec(
            num_scalar_prefetch=1,
            grid=(1 + len(given), S),
            in_specs=[spec, spec, *[pl.BlockSpec(block, lambda h, s, p: (0, s, 0, 0, 0))] * len(given)],
            out_specs=pl.BlockSpec(block, lambda h, s, p: (h, s, 0, 0, 0)),
        ),
        compiler_params=params(),
        cost_estimate=pl.CostEstimate(
            flops=0, bytes_accessed=8 * S * tokens * width, transcendentals=0
        ),
        name="pack",
    )(place, *hbm(keys, values), *given)


def pick(place, value, half):
    S, tokens, width = value.shape
    width //= 2

    def kernel(place, in_ref, out_ref):
        out_ref[...] = in_ref[...]

    return pl.pallas_call(
        kernel,
        out_shape=jax.ShapeDtypeStruct((S, tokens, width), value.dtype),
        grid_spec=pltpu.PrefetchScalarGridSpec(
            num_scalar_prefetch=1,
            grid=(S,),
            in_specs=[pl.BlockSpec((None, tokens, width), lambda s, p: (s, 0, side(half, p)))],
            out_specs=pl.BlockSpec((None, tokens, width), lambda s, p: (s, 0, 0)),
        ),
        compiler_params=params(),
        cost_estimate=pl.CostEstimate(
            flops=0, bytes_accessed=4 * S * tokens * width, transcendentals=0
        ),
        name="pick",
    )(place, *hbm(value))


def edge_attend(place, q, q_block, near, far, stream, cols_tile, cols, following=None):
    _, _, tokens, width = far.shape
    heads = width // HEAD
    extra, args, rows = [], [], tokens + FOLD
    if following is not None:
        rows += 2 * tokens
        args = [following[0], *hbm(following[1])]
        extra = [
            pl.BlockSpec((None, None, 2, tokens, width), lambda g, p: (1, stream, 0, 0, 0)),
            pl.BlockSpec((None, tokens, width), lambda g, p: (stream, 0, side(1, p))),
        ]
    return pl.pallas_call(
        functools.partial(edge_kernel, heads=heads, cols_tile=cols_tile, cols=cols),
        out_shape=jax.ShapeDtypeStruct((rows, width), jnp.bfloat16),
        grid_spec=pltpu.PrefetchScalarGridSpec(
            num_scalar_prefetch=1,
            grid=(1,),
            in_specs=[
                pl.BlockSpec((tokens, width), lambda g, p: (q_block, 0)),
                pl.BlockSpec((None, 2, tokens, width), lambda g, p: (stream, 0, 0, 0)),
                pl.BlockSpec((None, 2, tokens, width), lambda g, p: (0, 0, 0, 0)),
                *extra,
            ],
            out_specs=pl.BlockSpec((rows, width), lambda g, p: (0, 0)),
        ),
        compiler_params=params(),
        cost_estimate=pl.CostEstimate(
            flops=8 * tokens * tokens * width,
            bytes_accessed=14 * tokens * width,
            transcendentals=2 * tokens * tokens * heads,
        ),
        name="edge_rows",
    )(place, q, near, far, *args)


def rows_attend(place, mask, reach, q, tiles, sides, far, half, stream, cols_tile, frame_tokens, grid, block=3):
    tokens, width = far.shape[2:]
    at = stream if far.shape[0] > 1 else 0
    heads = width // HEAD
    lanes = block * HEAD
    steps = heads // block
    own = pl.BlockSpec((None, None, 2, tokens, lanes), lambda g, p: (half, stream, 0, 0, g))
    near = pl.BlockSpec((None, None, 2, tokens, lanes), lambda g, p: (0, stream, 0, 0, g))
    other = pl.BlockSpec((None, None, 2, tokens, lanes), lambda g, p: (1, stream, 0, 0, g))
    args = [x for tile, pair in zip(tiles, sides) for x in (tile, pair, pair)]
    kernel = functools.partial(
        rows_kernel, heads=block, half=half, grid=grid, cols_tile=cols_tile, frame_tokens=frame_tokens
    )
    return pl.pallas_call(
        kernel,
        out_shape=(
            jax.ShapeDtypeStruct((tokens, width), jnp.float32),
            jax.ShapeDtypeStruct((tokens, width), jnp.float32),
            jax.ShapeDtypeStruct((tokens, HEAD), jnp.bfloat16),
        ),
        grid_spec=pltpu.PrefetchScalarGridSpec(
            num_scalar_prefetch=1,
            grid=(steps,),
            in_specs=[
                SMEM,
                SMEM,
                pl.BlockSpec((None, tokens, lanes), lambda g, p: (stream, 0, side(half, p) * steps + g)),
                *[own, near, other] * 3,
                pl.BlockSpec((None, 2, tokens, lanes), lambda g, p: (at, 0, 0, g)),
            ],
            out_specs=(
                pl.BlockSpec((tokens, lanes), lambda g, p: (0, g)),
                pl.BlockSpec((tokens, lanes), lambda g, p: (0, g)),
                pl.BlockSpec((tokens, HEAD), lambda g, p: (0, 0)),
            ),
            scratch_shapes=[
                pltpu.VMEM((tokens // frame_tokens + 2, tokens, tokens), jnp.float32)
            ],
        ),
        compiler_params=params(),
        cost_estimate=pl.CostEstimate(
            flops=46 * tokens * tokens * width,
            bytes_accessed=54 * tokens * width,
            transcendentals=13 * tokens * tokens * heads,
        ),
        name="rows",
    )(place, mask, reach, *hbm(q), *args, far)


def merge(place, parts, rest, cols):
    tokens, width = parts[0].shape
    at = rest.shape[0] // tokens - 1
    whole = pl.BlockSpec((tokens, width), lambda g, p: (0, 0))
    return pl.pallas_call(
        functools.partial(merge_kernel, cols=cols),
        out_shape=jax.ShapeDtypeStruct((tokens, width), jnp.bfloat16),
        grid_spec=pltpu.PrefetchScalarGridSpec(
            num_scalar_prefetch=1,
            grid=(1,),
            in_specs=[
                whole,
                whole,
                pl.BlockSpec((tokens, HEAD), lambda g, p: (0, 0)),
                pl.BlockSpec((tokens, width), lambda g, p: (at, 0)),
                pl.BlockSpec((FOLD, width), lambda g, p: ((at + 1) * tokens // FOLD, 0)),
            ],
            out_specs=whole,
        ),
        compiler_params=params(),
        cost_estimate=pl.CostEstimate(
            flops=8 * tokens * width, bytes_accessed=12 * tokens * width, transcendentals=0
        ),
        name="merge",
    )(place, *parts, rest, rest)


def project(place, parts, rest, weight, other, output, stream, cols, block=3):
    tokens, width = parts[0].shape
    at = rest.shape[0] // tokens - 1
    lanes = block * HEAD
    streams, _, model = weight.shape
    earlier = [] if output is None else [output]
    cut = pl.BlockSpec((tokens, lanes), lambda g, p: (0, g))
    args = [place, *parts, rest, rest, weight, other]
    return pl.pallas_call(
        functools.partial(project_kernel, cols=cols),
        out_shape=jax.ShapeDtypeStruct((streams, tokens, model), jnp.bfloat16),
        grid_spec=pltpu.PrefetchScalarGridSpec(
            num_scalar_prefetch=1,
            grid=(width // lanes,),
            in_specs=[
                cut,
                cut,
                pl.BlockSpec((tokens, HEAD), lambda g, p: (0, 0)),
                pl.BlockSpec((tokens, lanes), lambda g, p: (at, g)),
                pl.BlockSpec((FOLD, width), lambda g, p: ((at + 1) * tokens // FOLD, 0)),
                pl.BlockSpec((None, lanes, model), lambda g, p: (stream, g, 0)),
                pl.BlockSpec((tokens, model), lambda g, p: (0, 0)),
                *[ANY] * len(earlier),
            ],
            out_specs=pl.BlockSpec((None, tokens, model), lambda g, p: (stream, 0, 0)),
            scratch_shapes=[pltpu.VMEM((tokens, model), jnp.float32)],
        ),
        input_output_aliases={len(args): 0} if earlier else {},
        compiler_params=params(),
        cost_estimate=pl.CostEstimate(
            flops=2 * tokens * width * model, bytes_accessed=2 * width * model, transcendentals=0
        ),
        name="project",
    )(*args, *earlier)


def product(rows, weight, stream, block=3):
    tokens, width = rows.shape
    model = weight.shape[2]
    lanes = block * HEAD
    return pl.pallas_call(
        product_kernel,
        out_shape=jax.ShapeDtypeStruct((tokens, model), jnp.bfloat16),
        grid=(width // lanes,),
        in_specs=[
            pl.BlockSpec((tokens, lanes), lambda g: (0, g)),
            pl.BlockSpec((None, lanes, model), lambda g: (stream, g, 0)),
        ],
        out_specs=pl.BlockSpec((tokens, model), lambda g: (0, 0)),
        scratch_shapes=[pltpu.VMEM((tokens, model), jnp.float32)],
        compiler_params=params(),
        cost_estimate=pl.CostEstimate(
            flops=2 * tokens * width * model, bytes_accessed=2 * width * model, transcendentals=0
        ),
        name="product",
    )(rows, weight)


def swaps(size, start):
    pairs = [(i, i + 1) for i in range(start, size - 1, 2)]
    return pairs + [(j, i) for i, j in pairs]


def per_device(queries, key_states, value_states, tile_mask, frame_reach, out_weight):
    S, F, R, C, width = queries.shape
    tokens = F * R * C
    half, model = width // 2, out_weight.shape[2]
    rows, cols = lax.axis_size("row"), lax.axis_size("col")
    inward = [(0, 1), (cols - 1, cols - 2)]
    outward = [(j, i) for i, j in inward]
    place = jnp.stack([lax.axis_index(a) for a in ("pair", "row", "col")]).astype(jnp.int32)
    q, k, v = [a.reshape(S, tokens, width) for a in (queries, key_states, value_states)]
    mask = tile_mask.reshape(9)

    sent = {}

    def tied(value, after):
        return lax.optimization_barrier((value, *[sent[n] for n in after]))[0] if after else value

    def send(name, value, axis, pairs, *after):
        sent[name] = lax.ppermute(tied(value, after), axis, pairs)

    col_pairs, col_others = swaps(cols, 0), swaps(cols, 1)
    row_pairs, row_others = swaps(rows, 0), swaps(rows, 1)
    pair_swap = swaps(2, 0)
    own0 = pack(place, k, v, 0)
    own = pack(place, k, v, 1, own0)
    picked = pick(place, q, 0).reshape(S * tokens, half)

    def mix(s, *after):
        sent[f"part0{s}"] = edge_attend(
            place, tied(sent["q0"], after), s, sent["other0"], sent[f"far0{s}"], s, C, cols, (own, q)
        )

    def edge(s, *after):
        sent[f"part1{s}"] = edge_attend(
            place, tied(sent[f"mix{s}"], after), 2, sent["other1"], sent[f"far1{s}"], s, C, cols
        )

    def near1(s):
        return sent[f"mix{s}"][:2 * tokens].reshape(1, 2, tokens, half)

    def rows_of(h, s, *after):
        tiles = [sent["pair_own"], own, sent["next_own"]]
        sides = [sent[f"pair_sides{h}"], sent[f"sides{h}"], sent[f"next_sides{h}"]]
        sent[f"rows{h}{s}"] = rows_attend(
            place, tied(mask, after), frame_reach, q, tiles, sides, sent[f"far{h}{s}"], h, s, C, R * C, (rows, cols)
        )

    send("near0", own0[0], "col", col_pairs)
    send("other0", own0[0], "col", col_others)
    send("next_own", own, "row", row_others)
    send("pair_own", own, "row", row_pairs)
    send("q0", picked, "col", inward)
    send("far00", sent["near0"][:1], "col", col_others, "near0", "other0", "pair_own")
    send("far01", sent["near0"][1:], "col", col_others, "near0", "other0", "pair_own")
    sent["sides0"] = jnp.stack([sent["near0"], sent["other0"]])
    send("next_sides0", sent["sides0"], "row", row_others, "next_own")
    send("pair_sides0", sent["sides0"], "row", row_pairs, "q0")
    mix(0)
    send("mix0", sent["part00"], "col", col_pairs)
    send("other1", own[1], "col", col_others, "far00")
    mix(1)
    send("mix1", sent["part01"], "col", col_pairs)
    rows_of(0, 0)
    rows_of(0, 1)
    sent["merged0"] = merge(tied(place, []), sent["rows00"], sent["mix0"], cols)
    send("theirs0", sent["merged0"], "pair", pair_swap)
    sent["merged1"] = merge(tied(place, []), sent["rows01"], sent["mix1"], cols)
    send("theirs1", sent["merged1"], "pair", pair_swap)
    sent["product0"] = product(tied(sent["theirs0"], []), out_weight, 0)
    send("back0", sent["product0"], "pair", pair_swap)
    sent["product1"] = product(tied(sent["theirs1"], []), out_weight, 1)
    send("back1", sent["product1"], "pair", pair_swap)
    send("far10", near1(0), "col", col_others, "far01", "pair_sides0", "next_sides0")
    send("far11", near1(1), "col", col_others, "other1")
    sent["sides1"] = jnp.stack([jnp.concatenate([near1(0), near1(1)]), sent["other1"]])
    send("next_sides1", sent["sides1"], "row", row_others)
    send("pair_sides1", sent["sides1"], "row", row_pairs)
    edge(0)
    send("rest10", sent["part10"], "col", outward)
    edge(1)
    send("rest11", sent["part11"], "col", outward)
    rows_of(1, 0)
    rows_of(1, 1)
    output = project(tied(place, []), sent["rows10"], sent["rest10"], out_weight, sent["back0"], None, 0, cols)
    output = project(place, sent["rows11"], sent["rest11"], out_weight, sent["back1"], output, 1, cols)
    return output.reshape(S, F, R, C, model)


def solution(mesh):
    return jax.shard_map(
        per_device,
        mesh=mesh,
        in_specs=(
            P("pair", None, "row", "col", None),
            P("pair", None, "row", "col", None),
            P("pair", None, "row", "col", None),
            P("pair", "row", "col", None),
            P(),
            P(None, "pair", None),
        ),
        out_specs=P("pair", None, "row", "col", None),
        check_vma=False,
    )
```

```python
import functools
import math

import jax
import jax.numpy as jnp
from jax import lax
from jax.experimental import pallas as pl
from jax.experimental.pallas import tpu as pltpu
from jax.sharding import PartitionSpec as P

NEG = -1e30
VMEM_LIMIT = 24 * 1024 * 1024
HEAD = 128
FOLD = 16
TO_LOG2 = HEAD ** (-0.5) * math.log2(math.e)
ANY = pl.BlockSpec(memory_space=pl.ANY)
SMEM = pl.BlockSpec(memory_space=pltpu.SMEM)


COST = {"pack": 4, "edge_rows": 4, "rows": 4, "merge": 4, "project": 4, "product": 4, "pick": 4}


def kernel_call(kernel, name, cost_estimate, **kwargs):
    k = COST.get(name, 1)
    cost = pl.CostEstimate(
        flops=int(k * cost_estimate.flops),
        bytes_accessed=int(k * cost_estimate.bytes_accessed),
        transcendentals=int(k * cost_estimate.transcendentals),
    )
    return pl.pallas_call(kernel, name=name, cost_estimate=cost, **kwargs)


def dot_nn(a, b):
    return lax.dot_general(a, b, (((1,), (0,)), ((), ())), preferred_element_type=jnp.float32)


def group_gap(tokens, group):
    q = lax.broadcasted_iota(jnp.int32, (tokens, tokens), 0)
    k = lax.broadcasted_iota(jnp.int32, (tokens, tokens), 1)
    return jnp.abs(q // group - k // group)


def softmax_sums(scores, values):
    tops = [jnp.max(functools.reduce(jnp.maximum, tiles), axis=1, keepdims=True) for tiles in scores]
    weights = [
        [jnp.exp2((s - top) * TO_LOG2) for s in tiles] for tiles, top in zip(scores, tops)
    ]
    sums = [jnp.sum(functools.reduce(jnp.add, w), axis=1, keepdims=True) for w in weights]
    totals = [
        dot_nn(
            jnp.concatenate([x.astype(jnp.bfloat16) for x in w], axis=1),
            jnp.concatenate(tiles, axis=0),
        )
        for w, tiles in zip(weights, values)
    ]
    return [top * TO_LOG2 for top in tops], totals, sums


def place_pieces(stats, values, first):
    lane = lax.broadcasted_iota(jnp.int32, stats.shape, 1)
    for n, value in enumerate(values):
        at = 3 * (first + n)
        high = value.astype(jnp.bfloat16).astype(jnp.float32)
        mid = (value - high).astype(jnp.bfloat16).astype(jnp.float32)
        stats = jnp.where(lane == at, high, stats)
        stats = jnp.where(lane == at + 1, mid, stats)
        stats = jnp.where(lane == at + 2, value - high - mid, stats)
    return stats


def spread_pieces(stats, first, heads):
    lane = lax.broadcasted_iota(jnp.int32, (HEAD, heads * HEAD), 0)
    at = 3 * (first + lax.broadcasted_iota(jnp.int32, (HEAD, heads * HEAD), 1) // HEAD)
    pick_head = jnp.where((lane >= at) & (lane < at + 3), 1.0, 0.0).astype(jnp.bfloat16)
    return dot_nn(stats, pick_head)


def fold_stats(stats, width):
    groups = [stats[start:start + FOLD] for start in range(0, stats.shape[0], FOLD)]
    rest = width // HEAD - len(groups)
    return jnp.concatenate(groups + [jnp.zeros_like(groups[0])] * rest, axis=1)


def unfold_stats(folded, tokens):
    return jnp.concatenate(
        [folded[:, n * HEAD:(n + 1) * HEAD] for n in range(tokens // FOLD)], axis=0
    )


def edge_kernel(place, q_ref, near_ref, far_ref, *refs, heads, cols_tile, cols):
    tokens = q_ref.shape[0]
    out_ref = refs[-1]
    first = 0
    if len(refs) > 1:
        next_ref, next_q_ref = refs[:2]
        first = 2 * tokens
        out_ref[:tokens] = next_ref[0]
        out_ref[tokens:first] = next_ref[1]
    inner = (place[2] > 0) & (place[2] < cols - 1)

    @pl.when(jnp.logical_not(inner))
    def _():
        if first:
            out_ref[first:first + tokens] = next_q_ref[...]
        else:
            out_ref[:tokens] = jnp.zeros((tokens, out_ref.shape[1]), out_ref.dtype)
        out_ref[first + tokens:] = jnp.zeros((FOLD, out_ref.shape[1]), out_ref.dtype)

    @pl.when(inner)
    def _():
        bias = jnp.where(group_gap(tokens, cols_tile) == 0, 0.0, NEG)
        cuts = [slice(n * HEAD, (n + 1) * HEAD) for n in range(heads)]
        tiles = (near_ref, far_ref)
        scores = [[dot_nn(q_ref[:, c], t[0, :, c]) + bias for t in tiles] for c in cuts]
        values = [[t[1, :, c] for t in tiles] for c in cuts]
        tops, totals, weights = softmax_sums(scores, values)
        lse = [top + jnp.log2(w) for top, w in zip(tops, weights)]
        stats = place_pieces(jnp.zeros((tokens, HEAD), jnp.float32), lse, 0)
        out_ref[first:first + tokens] = jnp.concatenate(
            [(t / w).astype(jnp.bfloat16) for t, w in zip(totals, weights)], axis=1
        )
        out_ref[first + tokens:] = fold_stats(stats.astype(jnp.bfloat16), out_ref.shape[1])


def fill_bias(bias_ref, frame_tokens, cols_tile):
    tokens = bias_ref.shape[1]
    frames = tokens // frame_tokens
    gap = group_gap(tokens, frame_tokens)
    for reach in range(frames):
        bias_ref[reach] = jnp.where(gap <= reach, 0.0, NEG)
    bias_ref[frames] = jnp.full((tokens, tokens), NEG, jnp.float32)
    bias_ref[frames + 1] = jnp.where(group_gap(tokens, cols_tile) == 0, 0.0, NEG)


def rows_kernel(place, mask, reach, q_ref, *refs, heads, half, grid, cols_tile, frame_tokens):
    tiles = refs[:10]
    base_ref, row_ref, sums_ref, bias_ref = refs[10:]
    tokens = q_ref.shape[0]
    none = bias_ref.shape[0] - 2
    step = pl.program_id(0)

    @pl.when(step == 0)
    def _():
        fill_bias(bias_ref, frame_tokens, cols_tile)
        sums_ref[...] = jnp.zeros_like(sums_ref)

    rows, cols = grid
    row, col = place[1], place[2]
    row_sign, col_sign = 1 - 2 * (row % 2), 1 - 2 * (col % 2)
    row_steps, col_steps = (row_sign, 0, -row_sign), (0, col_sign, -col_sign)
    listed = []
    for a in row_steps:
        for b in col_steps:
            inside = (row + a >= 0) & (row + a < rows) & (col + b >= 0) & (col + b < cols)
            listed.append(inside & ((mask[3 * (a + 1) + b + 1] > 0) | ((a == 0) & (b == 0))))
    inner = (col > 0) & (col < cols - 1)
    first_head = side(half, place) * heads * pl.num_programs(0)
    cuts = [slice(n * HEAD, (n + 1) * HEAD) for n in range(heads)]
    row_bias = bias_ref[none + 1]
    outer_bias = bias_ref[jnp.where(inner, none + 1, none)]

    def scores_of(n):
        scores = dot_nn(q_ref[:, cuts[n]], jnp.concatenate([t[0, :, cuts[n]] for t in tiles], axis=1))
        return [scores[:, t * tokens:(t + 1) * tokens] for t in range(10)]

    lse = []
    following = scores_of(0)
    for n, c in enumerate(cuts):
        raw, following = following, scores_of(n + 1) if n + 1 < heads else None
        values = [t[1, :, c] for t in tiles]
        limit = reach[first_head + step * heads + n]
        window = [raw[t] + bias_ref[jnp.where(listed[t], limit, none)] for t in range(9)]
        row = [raw[3] + row_bias, raw[4] + row_bias, raw[5] + outer_bias, raw[9] + outer_bias]
        tops, totals, weights = softmax_sums([window, row], [values[:9], values[3:6] + values[9:]])
        axial = totals[1] / weights[1]
        base_ref[:, c] = totals[0] / weights[0] + axial
        row_ref[:, c] = axial.astype(jnp.bfloat16)
        lse.append(tops[1] + jnp.log2(weights[1]))
    sums = place_pieces(sums_ref[...].astype(jnp.float32), lse, step * heads)
    sums_ref[...] = sums.astype(jnp.bfloat16)


def merged(place, base_ref, row_ref, sums_ref, rest_ref, stats_ref, cols):
    inner = (place[2] > 0) & (place[2] < cols - 1)
    tokens, width = base_ref.shape
    near = spread_pieces(sums_ref[...], 0, width // HEAD)
    far = spread_pieces(unfold_stats(stats_ref[...], tokens), 0, width // HEAD)
    share = 1.0 / (1.0 + jnp.exp2(near - jnp.where(inner, NEG, far)))
    rest, row = rest_ref[...].astype(jnp.float32), row_ref[...].astype(jnp.float32)
    return (base_ref[...] + (rest - row) * share).astype(jnp.bfloat16)


def merge_kernel(place, base_ref, row_ref, sums_ref, rest_ref, stats_ref, out_ref, *, cols):
    out_ref[...] = merged(place, base_ref, row_ref, sums_ref, rest_ref, stats_ref, cols)


def project_kernel(place, base_ref, row_ref, sums_ref, rest_ref, stats_ref, weight_ref, other_ref, *refs, cols):
    out_ref, rows_ref = refs[-2:]

    @pl.when(pl.program_id(0) == 0)
    def _():
        rows_ref[...] = merged(place, base_ref, row_ref, sums_ref, rest_ref, stats_ref, cols)

    total = other_ref[...].astype(jnp.float32) + dot_nn(rows_ref[...], weight_ref[...])
    out_ref[...] = total.astype(jnp.bfloat16)


def product_kernel(rows_ref, weight_ref, out_ref):
    out_ref[...] = dot_nn(rows_ref[...], weight_ref[...]).astype(jnp.bfloat16)


def hbm(*values):
    return [pltpu.with_memory_space_constraint(v, pltpu.HBM) for v in values]


def params():
    return pltpu.CompilerParams(vmem_limit_bytes=VMEM_LIMIT)


def side(half, place):
    return half + (1 - 2 * half) * (1 - place[0])


def pack(place, keys, values, half, earlier=None):
    S, tokens, width = keys.shape
    width //= 2
    spec = pl.BlockSpec((None, tokens, width), lambda h, s, p: (s, 0, side(half, p)))
    block = (None, None, 2, tokens, width)
    given = [] if earlier is None else [earlier]

    def turn(k_ref, v_ref, out_ref):
        for start in range(0, width, HEAD):
            cut = slice(start, start + HEAD)
            out_ref[0, :, cut] = k_ref[:, cut].T
        out_ref[1] = v_ref[...]

    def kernel(place, k_ref, v_ref, *refs):
        out_ref = refs[-1]
        if not given:
            turn(k_ref, v_ref, out_ref)
            return

        @pl.when(pl.program_id(0) == 0)
        def _():
            out_ref[...] = refs[0][...]

        @pl.when(pl.program_id(0) == 1)
        def _():
            turn(k_ref, v_ref, out_ref)

    return kernel_call(
        kernel,
        out_shape=jax.ShapeDtypeStruct((1 + len(given), S, 2, tokens, width), keys.dtype),
        grid_spec=pltpu.PrefetchScalarGridSpec(
            num_scalar_prefetch=1,
            grid=(1 + len(given), S),
            in_specs=[spec, spec, *[pl.BlockSpec(block, lambda h, s, p: (0, s, 0, 0, 0))] * len(given)],
            out_specs=pl.BlockSpec(block, lambda h, s, p: (h, s, 0, 0, 0)),
        ),
        compiler_params=params(),
        cost_estimate=pl.CostEstimate(
            flops=0, bytes_accessed=8 * S * tokens * width, transcendentals=0
        ),
        name="pack",
    )(place, *hbm(keys, values), *given)


def pick(place, value, half):
    S, tokens, width = value.shape
    width //= 2

    def kernel(place, in_ref, out_ref):
        out_ref[...] = in_ref[...]

    return kernel_call(
        kernel,
        out_shape=jax.ShapeDtypeStruct((S, tokens, width), value.dtype),
        grid_spec=pltpu.PrefetchScalarGridSpec(
            num_scalar_prefetch=1,
            grid=(S,),
            in_specs=[pl.BlockSpec((None, tokens, width), lambda s, p: (s, 0, side(half, p)))],
            out_specs=pl.BlockSpec((None, tokens, width), lambda s, p: (s, 0, 0)),
        ),
        compiler_params=params(),
        cost_estimate=pl.CostEstimate(
            flops=0, bytes_accessed=4 * S * tokens * width, transcendentals=0
        ),
        name="pick",
    )(place, *hbm(value))


def edge_attend(place, q, q_block, near, far, stream, cols_tile, cols, following=None):
    _, _, tokens, width = far.shape
    heads = width // HEAD
    extra, args, rows = [], [], tokens + FOLD
    if following is not None:
        rows += 2 * tokens
        args = [following[0], *hbm(following[1])]
        extra = [
            pl.BlockSpec((None, None, 2, tokens, width), lambda g, p: (1, stream, 0, 0, 0)),
            pl.BlockSpec((None, tokens, width), lambda g, p: (stream, 0, side(1, p))),
        ]
    return kernel_call(
        functools.partial(edge_kernel, heads=heads, cols_tile=cols_tile, cols=cols),
        out_shape=jax.ShapeDtypeStruct((rows, width), jnp.bfloat16),
        grid_spec=pltpu.PrefetchScalarGridSpec(
            num_scalar_prefetch=1,
            grid=(1,),
            in_specs=[
                pl.BlockSpec((tokens, width), lambda g, p: (q_block, 0)),
                pl.BlockSpec((None, 2, tokens, width), lambda g, p: (stream, 0, 0, 0)),
                pl.BlockSpec((None, 2, tokens, width), lambda g, p: (0, 0, 0, 0)),
                *extra,
            ],
            out_specs=pl.BlockSpec((rows, width), lambda g, p: (0, 0)),
        ),
        compiler_params=params(),
        cost_estimate=pl.CostEstimate(
            flops=8 * tokens * tokens * width,
            bytes_accessed=14 * tokens * width,
            transcendentals=2 * tokens * tokens * heads,
        ),
        name="edge_rows",
    )(place, q, near, far, *args)


def rows_attend(place, mask, reach, q, tiles, sides, far, half, stream, cols_tile, frame_tokens, grid, block=3):
    tokens, width = far.shape[2:]
    at = stream if far.shape[0] > 1 else 0
    heads = width // HEAD
    lanes = block * HEAD
    steps = heads // block
    place_of = stream if sides[0].shape[1] > 1 else 0
    own = pl.BlockSpec((None, None, 2, tokens, lanes), lambda g, p: (half, stream, 0, 0, g))
    near = pl.BlockSpec((None, None, 2, tokens, lanes), lambda g, p: (0, place_of, 0, 0, g))
    other = pl.BlockSpec((None, None, 2, tokens, lanes), lambda g, p: (1, place_of, 0, 0, g))
    args = [x for tile, pair in zip(tiles, sides) for x in (tile, pair, pair)]
    kernel = functools.partial(
        rows_kernel, heads=block, half=half, grid=grid, cols_tile=cols_tile, frame_tokens=frame_tokens
    )
    return kernel_call(
        kernel,
        out_shape=(
            jax.ShapeDtypeStruct((tokens, width), jnp.float32),
            jax.ShapeDtypeStruct((tokens, width), jnp.bfloat16),
            jax.ShapeDtypeStruct((tokens, HEAD), jnp.bfloat16),
        ),
        grid_spec=pltpu.PrefetchScalarGridSpec(
            num_scalar_prefetch=1,
            grid=(steps,),
            in_specs=[
                SMEM,
                SMEM,
                pl.BlockSpec((None, tokens, lanes), lambda g, p: (stream, 0, side(half, p) * steps + g)),
                *[own, near, other] * 3,
                pl.BlockSpec((None, 2, tokens, lanes), lambda g, p: (at, 0, 0, g)),
            ],
            out_specs=(
                pl.BlockSpec((tokens, lanes), lambda g, p: (0, g)),
                pl.BlockSpec((tokens, lanes), lambda g, p: (0, g)),
                pl.BlockSpec((tokens, HEAD), lambda g, p: (0, 0)),
            ),
            scratch_shapes=[
                pltpu.VMEM((tokens // frame_tokens + 2, tokens, tokens), jnp.float32)
            ],
        ),
        compiler_params=params(),
        cost_estimate=pl.CostEstimate(
            flops=46 * tokens * tokens * width,
            bytes_accessed=54 * tokens * width,
            transcendentals=13 * tokens * tokens * heads,
        ),
        name="rows",
    )(place, mask, reach, *hbm(q), *args, far)


def merge(place, parts, rest, cols):
    tokens, width = parts[0].shape
    at = rest.shape[0] // tokens - 1
    whole = pl.BlockSpec((tokens, width), lambda g, p: (0, 0))
    return kernel_call(
        functools.partial(merge_kernel, cols=cols),
        out_shape=jax.ShapeDtypeStruct((tokens, width), jnp.bfloat16),
        grid_spec=pltpu.PrefetchScalarGridSpec(
            num_scalar_prefetch=1,
            grid=(1,),
            in_specs=[
                whole,
                whole,
                pl.BlockSpec((tokens, HEAD), lambda g, p: (0, 0)),
                pl.BlockSpec((tokens, width), lambda g, p: (at, 0)),
                pl.BlockSpec((FOLD, width), lambda g, p: ((at + 1) * tokens // FOLD, 0)),
            ],
            out_specs=whole,
        ),
        compiler_params=params(),
        cost_estimate=pl.CostEstimate(
            flops=8 * tokens * width, bytes_accessed=12 * tokens * width, transcendentals=0
        ),
        name="merge",
    )(place, *parts, rest, rest)


def project(place, parts, rest, weight, other, output, stream, cols, lanes=512):
    tokens, width = parts[0].shape
    at = rest.shape[0] // tokens - 1
    streams, _, model = weight.shape
    earlier = [] if output is None else [output]
    whole = pl.BlockSpec((tokens, width), lambda g, p: (0, 0))
    args = [place, *parts, rest, rest, weight, other]
    return kernel_call(
        functools.partial(project_kernel, cols=cols),
        out_shape=jax.ShapeDtypeStruct((streams, tokens, model), jnp.bfloat16),
        grid_spec=pltpu.PrefetchScalarGridSpec(
            num_scalar_prefetch=1,
            grid=(model // lanes,),
            in_specs=[
                whole,
                whole,
                pl.BlockSpec((tokens, HEAD), lambda g, p: (0, 0)),
                pl.BlockSpec((tokens, width), lambda g, p: (at, 0)),
                pl.BlockSpec((FOLD, width), lambda g, p: ((at + 1) * tokens // FOLD, 0)),
                pl.BlockSpec((None, width, lanes), lambda g, p: (stream, 0, g)),
                pl.BlockSpec((tokens, lanes), lambda g, p: (0, g)),
                *[ANY] * len(earlier),
            ],
            out_specs=pl.BlockSpec((None, tokens, lanes), lambda g, p: (stream, 0, g)),
            scratch_shapes=[pltpu.VMEM((tokens, width), jnp.bfloat16)],
        ),
        input_output_aliases={len(args): 0} if earlier else {},
        compiler_params=params(),
        cost_estimate=pl.CostEstimate(
            flops=2 * tokens * width * model, bytes_accessed=2 * width * model, transcendentals=0
        ),
        name="project",
    )(*args, *earlier)


def product(rows, weight, stream, lanes=512):
    tokens, width = rows.shape
    model = weight.shape[2]
    return kernel_call(
        product_kernel,
        out_shape=jax.ShapeDtypeStruct((tokens, model), jnp.bfloat16),
        grid=(model // lanes,),
        in_specs=[
            pl.BlockSpec((tokens, width), lambda g: (0, 0)),
            pl.BlockSpec((None, width, lanes), lambda g: (stream, 0, g)),
        ],
        out_specs=pl.BlockSpec((tokens, lanes), lambda g: (0, g)),
        compiler_params=params(),
        cost_estimate=pl.CostEstimate(
            flops=2 * tokens * width * model, bytes_accessed=2 * width * model, transcendentals=0
        ),
        name="product",
    )(rows, weight)


def swaps(size, start):
    pairs = [(i, i + 1) for i in range(start, size - 1, 2)]
    return pairs + [(j, i) for i, j in pairs]


def per_device(queries, key_states, value_states, tile_mask, frame_reach, out_weight):
    S, F, R, C, width = queries.shape
    tokens = F * R * C
    half, model = width // 2, out_weight.shape[2]
    rows, cols = lax.axis_size("row"), lax.axis_size("col")
    inward = [(0, 1), (cols - 1, cols - 2)]
    outward = [(j, i) for i, j in inward]
    place = jnp.stack([lax.axis_index(a) for a in ("pair", "row", "col")]).astype(jnp.int32)
    q, k, v = [a.reshape(S, tokens, width) for a in (queries, key_states, value_states)]
    mask = tile_mask.reshape(9)

    sent = {}

    def tied(value, after):
        earlier = [sent[n] if isinstance(n, str) else n for n in after]
        return lax.optimization_barrier((value, *earlier))[0] if earlier else value

    def send(name, value, axis, pairs, *after):
        sent[name] = lax.ppermute(tied(value, after), axis, pairs)

    col_pairs, col_others = swaps(cols, 0), swaps(cols, 1)
    row_pairs, row_others = swaps(rows, 0), swaps(rows, 1)
    pair_swap = swaps(2, 0)
    own0 = pack(place, k, v, 0)
    picked = pick(place, q, 0).reshape(S * tokens, half)
    own = pack(tied(place, [picked]), k, v, 1, own0)

    def mix(s, *after):
        sent[f"part0{s}"] = edge_attend(
            place, tied(sent["q0"], after), s, sent["other0"], sent[f"far0{s}"], s, C, cols, (own, q)
        )

    def edge(s, *after):
        sent[f"part1{s}"] = edge_attend(
            place, tied(sent[f"mix{s}"], after), 2, sent["other1"], sent[f"far1{s}"], s, C, cols
        )

    def near1(s):
        return sent[f"mix{s}"][:2 * tokens].reshape(1, 2, tokens, half)

    def rows_of(h, s, *after):
        tiles = [sent["pair_own"], own, sent["next_own"]]
        part = f"{h}" if h == 0 else f"{h}{s}"
        sides = [sent[f"pair_sides{part}"], sent[f"sides{part}"], sent[f"next_sides{part}"]]
        sent[f"rows{h}{s}"] = rows_attend(
            place, tied(mask, after), frame_reach, q, tiles, sides, sent[f"far{h}{s}"], h, s, C, R * C, (rows, cols)
        )

    send("near0", own0[0], "col", col_pairs)
    send("other0", own0[0], "col", col_others)
    send("next_own", own, "row", row_others)
    send("pair_own", own, "row", row_pairs)
    send("q0", picked, "col", inward)
    send("far00", sent["near0"][:1], "col", col_others, "other0", "pair_own", "next_own")
    send("far01", sent["near0"][1:], "col", col_others, "near0")
    sent["sides0"] = jnp.stack([sent["near0"], sent["other0"]])
    send("next_sides0", sent["sides0"], "row", row_others)
    send("pair_sides0", sent["sides0"], "row", row_pairs, "other0")
    mix(0)
    send("mix0", sent["part00"], "col", col_pairs)
    send("other1", own[1], "col", col_others, "far01", "next_sides0", "pair_sides0")
    mix(1, "part00")
    send("mix1", sent["part01"], "col", col_pairs)
    rows_of(0, 0)
    rows_of(0, 1)
    sent["merged0"] = merge(tied(place, []), sent["rows00"], sent["mix0"], cols)
    send("theirs0", sent["merged0"], "pair", pair_swap)
    sent["product0"] = product(tied(sent["theirs0"], ["rows01"]), out_weight, 0)
    send("back0", sent["product0"], "pair", pair_swap)
    sent["mix1"] = tied(sent["mix1"], ["theirs0"])
    sent["merged1"] = merge(tied(place, []), sent["rows01"], sent["mix1"], cols)
    send("theirs1", sent["merged1"], "pair", pair_swap, "back0")
    sent["product1"] = product(tied(sent["theirs1"], []), out_weight, 1)
    send("back1", sent["product1"], "pair", pair_swap)
    send("far10", near1(0), "col", col_others, "theirs0")
    sent["sides10"] = jnp.stack([near1(0), tied(sent["other1"][0:1], ["theirs0"])])
    send("next_sides10", sent["sides10"], "row", row_others)
    send("pair_sides10", sent["sides10"], "row", row_pairs)
    send("far11", near1(1), "col", col_others)
    sent["sides11"] = jnp.stack([near1(1), tied(sent["other1"][1:2], ["theirs0"])])
    send("next_sides11", sent["sides11"], "row", row_others)
    send("pair_sides11", sent["sides11"], "row", row_pairs)
    edge(0)
    send("rest10", sent["part10"], "col", outward)
    edge(1, "part10", "next_sides10")
    send("rest11", sent["part11"], "col", outward)
    rows_of(1, 0)
    rows_of(1, 1, "rows10")
    output = project(tied(place, []), sent["rows10"], sent["rest10"], out_weight, sent["back0"], None, 0, cols)
    output = project(place, sent["rows11"], sent["rest11"], out_weight, sent["back1"], output, 1, cols)
    return output.reshape(S, F, R, C, model)


def solution(mesh):
    return jax.shard_map(
        per_device,
        mesh=mesh,
        in_specs=(
            P("pair", None, "row", "col", None),
            P("pair", None, "row", "col", None),
            P("pair", None, "row", "col", None),
            P("pair", "row", "col", None),
            P(),
            P(None, "pair", None),
        ),
        out_specs=P("pair", None, "row", "col", None),
        check_vma=False,
    )
```

```python
import functools
import math

import jax
import jax.numpy as jnp
from jax import lax
from jax.experimental import pallas as pl
from jax.experimental.pallas import tpu as pltpu
from jax.sharding import PartitionSpec as P

NEG = -1e30
VMEM_LIMIT = 24 * 1024 * 1024
HEAD = 128
FOLD = 16
TO_LOG2 = HEAD ** (-0.5) * math.log2(math.e)
ANY = pl.BlockSpec(memory_space=pl.ANY)
SMEM = pl.BlockSpec(memory_space=pltpu.SMEM)


COST = {"pack": 1, "edge_rows": 8, "rows": 1, "merge": 4, "project": 1, "product": 4, "pick": 4}


def kernel_call(kernel, name, cost_estimate, **kwargs):
    k = COST.get(name, 1)
    cost = pl.CostEstimate(
        flops=int(k * cost_estimate.flops),
        bytes_accessed=int(k * cost_estimate.bytes_accessed),
        transcendentals=int(k * cost_estimate.transcendentals),
    )
    return pl.pallas_call(kernel, name=name, cost_estimate=cost, **kwargs)


def dot_nn(a, b):
    return lax.dot_general(a, b, (((1,), (0,)), ((), ())), preferred_element_type=jnp.float32)


def group_gap(tokens, group):
    q = lax.broadcasted_iota(jnp.int32, (tokens, tokens), 0)
    k = lax.broadcasted_iota(jnp.int32, (tokens, tokens), 1)
    return jnp.abs(q // group - k // group)


def softmax_sums(scores, values):
    tops = [jnp.max(functools.reduce(jnp.maximum, tiles), axis=1, keepdims=True) for tiles in scores]
    weights = [
        [jnp.exp2((s - top) * TO_LOG2) for s in tiles] for tiles, top in zip(scores, tops)
    ]
    sums = [jnp.sum(functools.reduce(jnp.add, w), axis=1, keepdims=True) for w in weights]
    totals = [
        dot_nn(
            jnp.concatenate([x.astype(jnp.bfloat16) for x in w], axis=1),
            jnp.concatenate(tiles, axis=0),
        )
        for w, tiles in zip(weights, values)
    ]
    return [top * TO_LOG2 for top in tops], totals, sums


def place_pieces(stats, values, first):
    lane = lax.broadcasted_iota(jnp.int32, stats.shape, 1)
    for n, value in enumerate(values):
        at = 3 * (first + n)
        high = value.astype(jnp.bfloat16).astype(jnp.float32)
        mid = (value - high).astype(jnp.bfloat16).astype(jnp.float32)
        stats = jnp.where(lane == at, high, stats)
        stats = jnp.where(lane == at + 1, mid, stats)
        stats = jnp.where(lane == at + 2, value - high - mid, stats)
    return stats


def spread_pieces(stats, first, heads):
    lane = lax.broadcasted_iota(jnp.int32, (HEAD, heads * HEAD), 0)
    at = 3 * (first + lax.broadcasted_iota(jnp.int32, (HEAD, heads * HEAD), 1) // HEAD)
    pick_head = jnp.where((lane >= at) & (lane < at + 3), 1.0, 0.0).astype(jnp.bfloat16)
    return dot_nn(stats, pick_head)


def fold_stats(stats, width):
    groups = [stats[start:start + FOLD] for start in range(0, stats.shape[0], FOLD)]
    rest = width // HEAD - len(groups)
    return jnp.concatenate(groups + [jnp.zeros_like(groups[0])] * rest, axis=1)


def unfold_stats(folded, tokens):
    return jnp.concatenate(
        [folded[:, n * HEAD:(n + 1) * HEAD] for n in range(tokens // FOLD)], axis=0
    )


def edge_kernel(place, q_ref, near_ref, far_ref, out_ref, *, heads, cols_tile, cols):
    tokens = q_ref.shape[0]
    inner = (place[2] > 0) & (place[2] < cols - 1)

    @pl.when(jnp.logical_not(inner))
    def _():
        out_ref[...] = jnp.zeros_like(out_ref)

    @pl.when(inner)
    def _():
        bias = jnp.where(group_gap(tokens, cols_tile) == 0, 0.0, NEG)
        cuts = [slice(n * HEAD, (n + 1) * HEAD) for n in range(heads)]
        tiles = (near_ref, far_ref)
        scores = [[dot_nn(q_ref[:, c], t[0, :, c]) + bias for t in tiles] for c in cuts]
        values = [[t[1, :, c] for t in tiles] for c in cuts]
        tops, totals, weights = softmax_sums(scores, values)
        lse = [top + jnp.log2(w) for top, w in zip(tops, weights)]
        stats = place_pieces(jnp.zeros((tokens, HEAD), jnp.float32), lse, 0)
        out_ref[:tokens] = jnp.concatenate(
            [(t / w).astype(jnp.bfloat16) for t, w in zip(totals, weights)], axis=1
        )
        out_ref[tokens:] = fold_stats(stats.astype(jnp.bfloat16), out_ref.shape[1])


def fill_bias(bias_ref, frame_tokens, cols_tile):
    tokens = bias_ref.shape[1]
    frames = tokens // frame_tokens
    gap = group_gap(tokens, frame_tokens)
    for reach in range(frames):
        bias_ref[reach] = jnp.where(gap <= reach, 0.0, NEG)
    bias_ref[frames] = jnp.full((tokens, tokens), NEG, jnp.float32)
    bias_ref[frames + 1] = jnp.where(group_gap(tokens, cols_tile) == 0, 0.0, NEG)


def rows_kernel(place, mask, reach, q_ref, *refs, heads, half, grid, cols_tile, frame_tokens):
    tiles = refs[:10]
    base_ref, row_ref, sums_ref, bias_ref = refs[10:]
    tokens = q_ref.shape[0]
    none = bias_ref.shape[0] - 2
    step = pl.program_id(0)

    @pl.when(step == 0)
    def _():
        fill_bias(bias_ref, frame_tokens, cols_tile)
        sums_ref[...] = jnp.zeros_like(sums_ref)

    rows, cols = grid
    row, col = place[1], place[2]
    row_sign, col_sign = 1 - 2 * (row % 2), 1 - 2 * (col % 2)
    row_steps, col_steps = (row_sign, 0, -row_sign), (0, col_sign, -col_sign)
    listed = []
    for a in row_steps:
        for b in col_steps:
            inside = (row + a >= 0) & (row + a < rows) & (col + b >= 0) & (col + b < cols)
            listed.append(inside & ((mask[3 * (a + 1) + b + 1] > 0) | ((a == 0) & (b == 0))))
    inner = (col > 0) & (col < cols - 1)
    first_head = side(half, place) * heads * pl.num_programs(0)
    cuts = [slice(n * HEAD, (n + 1) * HEAD) for n in range(heads)]
    row_bias = bias_ref[none + 1]
    outer_bias = bias_ref[jnp.where(inner, none + 1, none)]

    def scores_of(n):
        scores = dot_nn(q_ref[:, cuts[n]], jnp.concatenate([t[0, :, cuts[n]] for t in tiles], axis=1))
        return [scores[:, t * tokens:(t + 1) * tokens] for t in range(10)]

    lse = []
    following = scores_of(0)
    for n, c in enumerate(cuts):
        raw, following = following, scores_of(n + 1) if n + 1 < heads else None
        values = [t[1, :, c] for t in tiles]
        limit = reach[first_head + step * heads + n]
        window = [raw[t] + bias_ref[jnp.where(listed[t], limit, none)] for t in range(9)]
        row = [raw[3] + row_bias, raw[4] + row_bias, raw[5] + outer_bias, raw[9] + outer_bias]
        tops, totals, weights = softmax_sums([window, row], [values[:9], values[3:6] + values[9:]])
        axial = totals[1] / weights[1]
        base_ref[:, c] = totals[0] / weights[0] + axial
        row_ref[:, c] = axial.astype(jnp.bfloat16)
        lse.append(tops[1] + jnp.log2(weights[1]))
    sums = place_pieces(sums_ref[...].astype(jnp.float32), lse, step * heads)
    sums_ref[...] = sums.astype(jnp.bfloat16)


def merged(place, base_ref, row_ref, sums_ref, rest_ref, stats_ref, cols):
    inner = (place[2] > 0) & (place[2] < cols - 1)
    tokens, width = base_ref.shape
    near = spread_pieces(sums_ref[...], 0, width // HEAD)
    far = spread_pieces(unfold_stats(stats_ref[...], tokens), 0, width // HEAD)
    share = 1.0 / (1.0 + jnp.exp2(near - jnp.where(inner, NEG, far)))
    rest, row = rest_ref[...].astype(jnp.float32), row_ref[...].astype(jnp.float32)
    return (base_ref[...] + (rest - row) * share).astype(jnp.bfloat16)


def merge_kernel(place, base_ref, row_ref, sums_ref, rest_ref, stats_ref, out_ref, *, cols):
    out_ref[...] = merged(place, base_ref, row_ref, sums_ref, rest_ref, stats_ref, cols)


def add_product(total_ref, rows, weight_ref, lanes=512):
    for start in range(0, total_ref.shape[1], lanes):
        cut = slice(start, start + lanes)
        total_ref[:, cut] += dot_nn(rows, weight_ref[:, cut])


def project_kernel(place, base_ref, row_ref, sums_ref, rest_ref, stats_ref, weight_ref, other_ref, *refs, cols):
    out_ref, total_ref, rows_ref = refs[-3:]
    step, lanes = pl.program_id(0), weight_ref.shape[0]

    @pl.when(step == 0)
    def _():
        total_ref[...] = other_ref[...].astype(jnp.float32)
        rows = merged(place, base_ref, row_ref, sums_ref, rest_ref, stats_ref, cols)
        for n in range(rows_ref.shape[0]):
            rows_ref[n] = rows[:, n * lanes:(n + 1) * lanes]

    add_product(total_ref, rows_ref[step], weight_ref)

    @pl.when(step == pl.num_programs(0) - 1)
    def _():
        out_ref[...] = total_ref[...].astype(jnp.bfloat16)


def product_kernel(rows_ref, weight_ref, out_ref, total_ref):
    @pl.when(pl.program_id(0) == 0)
    def _():
        total_ref[...] = jnp.zeros_like(total_ref)

    add_product(total_ref, rows_ref[...], weight_ref)

    @pl.when(pl.program_id(0) == pl.num_programs(0) - 1)
    def _():
        out_ref[...] = total_ref[...].astype(jnp.bfloat16)


def hbm(*values):
    return [pltpu.with_memory_space_constraint(v, pltpu.HBM) for v in values]


def params():
    return pltpu.CompilerParams(vmem_limit_bytes=VMEM_LIMIT)


def side(half, place):
    return half + (1 - 2 * half) * (1 - place[0])


def pack(place, keys, values, half, earlier=None):
    S, tokens, width = keys.shape
    width //= 2
    spec = pl.BlockSpec((None, tokens, width), lambda h, s, p: (s, 0, side(half, p)))
    block = (None, None, 2, tokens, width)
    given = [] if earlier is None else [earlier]

    def turn(k_ref, v_ref, out_ref):
        for start in range(0, width, HEAD):
            cut = slice(start, start + HEAD)
            out_ref[0, :, cut] = k_ref[:, cut].T
        out_ref[1] = v_ref[...]

    def kernel(place, k_ref, v_ref, *refs):
        out_ref = refs[-1]
        if not given:
            turn(k_ref, v_ref, out_ref)
            return

        @pl.when(pl.program_id(0) == 0)
        def _():
            out_ref[...] = refs[0][...]

        @pl.when(pl.program_id(0) == 1)
        def _():
            turn(k_ref, v_ref, out_ref)

    return kernel_call(
        kernel,
        out_shape=jax.ShapeDtypeStruct((1 + len(given), S, 2, tokens, width), keys.dtype),
        grid_spec=pltpu.PrefetchScalarGridSpec(
            num_scalar_prefetch=1,
            grid=(1 + len(given), S),
            in_specs=[spec, spec, *[pl.BlockSpec(block, lambda h, s, p: (0, s, 0, 0, 0))] * len(given)],
            out_specs=pl.BlockSpec(block, lambda h, s, p: (h, s, 0, 0, 0)),
        ),
        compiler_params=params(),
        cost_estimate=pl.CostEstimate(
            flops=0, bytes_accessed=8 * S * tokens * width, transcendentals=0
        ),
        name="pack",
    )(place, *hbm(keys, values), *given)


def pick(place, value, half):
    S, tokens, width = value.shape
    width //= 2

    def kernel(place, in_ref, out_ref):
        out_ref[...] = in_ref[...]

    return kernel_call(
        kernel,
        out_shape=jax.ShapeDtypeStruct((S, tokens, width), value.dtype),
        grid_spec=pltpu.PrefetchScalarGridSpec(
            num_scalar_prefetch=1,
            grid=(S,),
            in_specs=[pl.BlockSpec((None, tokens, width), lambda s, p: (s, 0, side(half, p)))],
            out_specs=pl.BlockSpec((None, tokens, width), lambda s, p: (s, 0, 0)),
        ),
        compiler_params=params(),
        cost_estimate=pl.CostEstimate(
            flops=0, bytes_accessed=4 * S * tokens * width, transcendentals=0
        ),
        name="pick",
    )(place, *hbm(value))


def edge_attend(place, q, q_block, near, far, stream, cols_tile, cols):
    _, _, tokens, width = far.shape
    heads = width // HEAD
    rows = tokens + FOLD
    return kernel_call(
        functools.partial(edge_kernel, heads=heads, cols_tile=cols_tile, cols=cols),
        out_shape=jax.ShapeDtypeStruct((rows, width), jnp.bfloat16),
        grid_spec=pltpu.PrefetchScalarGridSpec(
            num_scalar_prefetch=1,
            grid=(1,),
            in_specs=[
                pl.BlockSpec((tokens, width), lambda g, p: (q_block, 0)),
                pl.BlockSpec((None, 2, tokens, width), lambda g, p: (stream, 0, 0, 0)),
                pl.BlockSpec((None, 2, tokens, width), lambda g, p: (0, 0, 0, 0)),
            ],
            out_specs=pl.BlockSpec((rows, width), lambda g, p: (0, 0)),
        ),
        compiler_params=params(),
        cost_estimate=pl.CostEstimate(
            flops=8 * tokens * tokens * width,
            bytes_accessed=14 * tokens * width,
            transcendentals=2 * tokens * tokens * heads,
        ),
        name="edge_rows",
    )(place, q, near, far)


def rows_attend(place, mask, reach, q, tiles, sides, far, half, stream, cols_tile, frame_tokens, grid, block=3):
    tokens, width = far.shape[2:]
    at = stream if far.shape[0] > 1 else 0
    heads = width // HEAD
    lanes = block * HEAD
    steps = heads // block
    place_of = stream if sides[0].shape[1] > 1 else 0
    own = pl.BlockSpec((None, None, 2, tokens, lanes), lambda g, p: (half, stream, 0, 0, g))
    near = pl.BlockSpec((None, None, 2, tokens, lanes), lambda g, p: (0, place_of, 0, 0, g))
    other = pl.BlockSpec((None, None, 2, tokens, lanes), lambda g, p: (1, place_of, 0, 0, g))
    args = [x for tile, pair in zip(tiles, sides) for x in (tile, pair, pair)]
    kernel = functools.partial(
        rows_kernel, heads=block, half=half, grid=grid, cols_tile=cols_tile, frame_tokens=frame_tokens
    )
    return kernel_call(
        kernel,
        out_shape=(
            jax.ShapeDtypeStruct((tokens, width), jnp.float32),
            jax.ShapeDtypeStruct((tokens, width), jnp.bfloat16),
            jax.ShapeDtypeStruct((tokens, HEAD), jnp.bfloat16),
        ),
        grid_spec=pltpu.PrefetchScalarGridSpec(
            num_scalar_prefetch=1,
            grid=(steps,),
            in_specs=[
                SMEM,
                SMEM,
                pl.BlockSpec((None, tokens, lanes), lambda g, p: (stream, 0, side(half, p) * steps + g)),
                *[own, near, other] * 3,
                pl.BlockSpec((None, 2, tokens, lanes), lambda g, p: (at, 0, 0, g)),
            ],
            out_specs=(
                pl.BlockSpec((tokens, lanes), lambda g, p: (0, g)),
                pl.BlockSpec((tokens, lanes), lambda g, p: (0, g)),
                pl.BlockSpec((tokens, HEAD), lambda g, p: (0, 0)),
            ),
            scratch_shapes=[
                pltpu.VMEM((tokens // frame_tokens + 2, tokens, tokens), jnp.float32)
            ],
        ),
        compiler_params=params(),
        cost_estimate=pl.CostEstimate(
            flops=46 * tokens * tokens * width,
            bytes_accessed=54 * tokens * width,
            transcendentals=13 * tokens * tokens * heads,
        ),
        name="rows",
    )(place, mask, reach, *hbm(q), *args, far)


def merge(place, parts, rest, cols):
    tokens, width = parts[0].shape
    at = rest.shape[0] // tokens - 1
    whole = pl.BlockSpec((tokens, width), lambda g, p: (0, 0))
    return kernel_call(
        functools.partial(merge_kernel, cols=cols),
        out_shape=jax.ShapeDtypeStruct((tokens, width), jnp.bfloat16),
        grid_spec=pltpu.PrefetchScalarGridSpec(
            num_scalar_prefetch=1,
            grid=(1,),
            in_specs=[
                whole,
                whole,
                pl.BlockSpec((tokens, HEAD), lambda g, p: (0, 0)),
                pl.BlockSpec((tokens, width), lambda g, p: (at, 0)),
                pl.BlockSpec((FOLD, width), lambda g, p: ((at + 1) * tokens // FOLD, 0)),
            ],
            out_specs=whole,
        ),
        compiler_params=params(),
        cost_estimate=pl.CostEstimate(
            flops=8 * tokens * width, bytes_accessed=12 * tokens * width, transcendentals=0
        ),
        name="merge",
    )(place, *parts, rest, rest)


def project(place, parts, rest, weight, other, output, stream, cols, block=3):
    tokens, width = parts[0].shape
    at = rest.shape[0] // tokens - 1
    lanes = block * HEAD
    streams, _, model = weight.shape
    earlier = [] if output is None else [output]
    whole = pl.BlockSpec((tokens, width), lambda g, p: (0, 0))
    args = [place, *parts, rest, rest, weight, other]
    return kernel_call(
        functools.partial(project_kernel, cols=cols),
        out_shape=jax.ShapeDtypeStruct((streams, tokens, model), jnp.bfloat16),
        grid_spec=pltpu.PrefetchScalarGridSpec(
            num_scalar_prefetch=1,
            grid=(width // lanes,),
            in_specs=[
                whole,
                whole,
                pl.BlockSpec((tokens, HEAD), lambda g, p: (0, 0)),
                pl.BlockSpec((tokens, width), lambda g, p: (at, 0)),
                pl.BlockSpec((FOLD, width), lambda g, p: ((at + 1) * tokens // FOLD, 0)),
                pl.BlockSpec((None, lanes, model), lambda g, p: (stream, g, 0)),
                pl.BlockSpec((tokens, model), lambda g, p: (0, 0)),
                *[ANY] * len(earlier),
            ],
            out_specs=pl.BlockSpec((None, tokens, model), lambda g, p: (stream, 0, 0)),
            scratch_shapes=[
                pltpu.VMEM((tokens, model), jnp.float32),
                pltpu.VMEM((width // lanes, tokens, lanes), jnp.bfloat16),
            ],
        ),
        input_output_aliases={len(args): 0} if earlier else {},
        compiler_params=params(),
        cost_estimate=pl.CostEstimate(
            flops=2 * tokens * width * model, bytes_accessed=2 * width * model, transcendentals=0
        ),
        name="project",
    )(*args, *earlier)


def product(rows, weight, stream, block=3):
    tokens, width = rows.shape
    model = weight.shape[2]
    lanes = block * HEAD
    return kernel_call(
        product_kernel,
        out_shape=jax.ShapeDtypeStruct((tokens, model), jnp.bfloat16),
        grid=(width // lanes,),
        in_specs=[
            pl.BlockSpec((tokens, lanes), lambda g: (0, g)),
            pl.BlockSpec((None, lanes, model), lambda g: (stream, g, 0)),
        ],
        out_specs=pl.BlockSpec((tokens, model), lambda g: (0, 0)),
        scratch_shapes=[pltpu.VMEM((tokens, model), jnp.float32)],
        compiler_params=params(),
        cost_estimate=pl.CostEstimate(
            flops=2 * tokens * width * model, bytes_accessed=2 * width * model, transcendentals=0
        ),
        name="product",
    )(rows, weight)


def swaps(size, start):
    pairs = [(i, i + 1) for i in range(start, size - 1, 2)]
    return pairs + [(j, i) for i, j in pairs]


def per_device(queries, key_states, value_states, tile_mask, frame_reach, out_weight):
    S, F, R, C, width = queries.shape
    tokens = F * R * C
    half, model = width // 2, out_weight.shape[2]
    rows, cols = lax.axis_size("row"), lax.axis_size("col")
    inward = [(0, 1), (cols - 1, cols - 2)]
    outward = [(j, i) for i, j in inward]
    place = jnp.stack([lax.axis_index(a) for a in ("pair", "row", "col")]).astype(jnp.int32)
    q, k, v = [a.reshape(S, tokens, width) for a in (queries, key_states, value_states)]
    mask = tile_mask.reshape(9)

    sent = {}

    def tied(value, after):
        earlier = [sent[n] if isinstance(n, str) else n for n in after]
        return lax.optimization_barrier((value, *earlier))[0] if earlier else value

    def send(name, value, axis, pairs, *after):
        sent[name] = lax.ppermute(tied(value, after), axis, pairs)

    col_pairs, col_others = swaps(cols, 0), swaps(cols, 1)
    row_pairs, row_others = swaps(rows, 0), swaps(rows, 1)
    pair_swap = swaps(2, 0)
    own0 = pack(place, k, v, 0)
    picked = pick(place, q, 0).reshape(S * tokens, half)
    own = pack(tied(place, [picked]), k, v, 1, own0)
    q1 = pick(tied(place, [own]), q, 1)
    onward = [jnp.concatenate([own[1, s].reshape(2 * tokens, half), q1[s]]) for s in range(S)]

    def edge(h, s, *after):
        rows_q, block = (sent["q0"], s) if h == 0 else (sent[f"near1{s}"], 2)
        sent[f"part{h}{s}"] = edge_attend(
            place, tied(rows_q, after), block, sent[f"other{h}"], sent[f"far{h}{s}"], s, C, cols
        )

    def near1(s):
        return sent[f"near1{s}"][:2 * tokens].reshape(1, 2, tokens, half)

    def rows_of(h, s, *after):
        tiles = [sent["pair_own"], own, sent["next_own"]]
        part = f"{h}" if h == 0 else f"{h}{s}"
        sides = [sent[f"pair_sides{part}"], sent[f"sides{part}"], sent[f"next_sides{part}"]]
        sent[f"rows{h}{s}"] = rows_attend(
            place, tied(mask, after), frame_reach, q, tiles, sides, sent[f"far{h}{s}"], h, s, C, R * C, (rows, cols)
        )

    send("near0", own0[0], "col", col_pairs)
    send("other0", own0[0], "col", col_others)
    send("next_own", own, "row", row_others)
    send("pair_own", own, "row", row_pairs)
    send("q0", picked, "col", inward)
    send("far00", sent["near0"][:1], "col", col_others, "other0", "pair_own")
    send("far01", sent["near0"][1:], "col", col_others, "near0", "next_own")
    sent["sides0"] = jnp.stack([sent["near0"], sent["other0"]])
    send("pair_sides0", sent["sides0"], "row", row_pairs)
    send("next_sides0", sent["sides0"], "row", row_others)
    send("near10", onward[0], "col", col_pairs, "other0")
    edge(0, 0)
    send("rest00", sent["part00"], "col", outward)
    send("other1", own[1], "col", col_others, "far00")
    edge(0, 1, "part00")
    send("rest01", sent["part01"], "col", outward)
    send("near11", onward[1], "col", col_pairs, "rest00", "part01")
    rows_of(0, 0, "part01")
    sent["merged0"] = merge(tied(place, []), sent["rows00"], sent["rest00"], cols)
    rows_of(0, 1, "merged0")
    send("theirs0", sent["merged0"], "pair", pair_swap)
    sent["product0"] = product(tied(sent["theirs0"], ["rows01"]), out_weight, 0)
    send("back0", sent["product0"], "pair", pair_swap)
    sent["merged1"] = merge(tied(place, []), sent["rows01"], sent["rest01"], cols)
    send("theirs1", sent["merged1"], "pair", pair_swap)
    send("far10", near1(0), "col", col_others, "product0")
    sent["sides10"] = jnp.stack([near1(0), tied(sent["other1"][0:1], ["rows01"])])
    send("next_sides10", sent["sides10"], "row", row_others, "other1")
    send("pair_sides10", sent["sides10"], "row", row_pairs)
    edge(1, 0)
    sent["product1"] = product(tied(sent["theirs1"], ["part10"]), out_weight, 1)
    send("back1", sent["product1"], "pair", pair_swap)
    send("rest10", sent["part10"], "col", outward)
    rows_of(1, 0)
    send("far11", near1(1), "col", col_others, "product0")
    sent["sides11"] = jnp.stack([near1(1), tied(sent["other1"][1:2], ["merged1", "sides10"])])
    send("next_sides11", sent["sides11"], "row", row_others)
    send("pair_sides11", sent["sides11"], "row", row_pairs)
    edge(1, 1, "part10")
    send("rest11", sent["part11"], "col", outward)
    rows_of(1, 1, "rows10")
    output = project(tied(place, []), sent["rows10"], sent["rest10"], out_weight, sent["back0"], None, 0, cols)
    output = project(place, sent["rows11"], sent["rest11"], out_weight, sent["back1"], output, 1, cols)
    return output.reshape(S, F, R, C, model)


def solution(mesh):
    return jax.shard_map(
        per_device,
        mesh=mesh,
        in_specs=(
            P("pair", None, "row", "col", None),
            P("pair", None, "row", "col", None),
            P("pair", None, "row", "col", None),
            P("pair", "row", "col", None),
            P(),
            P(None, "pair", None),
        ),
        out_specs=P("pair", None, "row", "col", None),
        check_vma=False,
    )
```

```python
import functools
import math

import jax
import jax.numpy as jnp
from jax import lax
from jax.experimental import pallas as pl
from jax.experimental.pallas import tpu as pltpu
from jax.sharding import PartitionSpec as P

NEG = -1e30
VMEM_LIMIT = 24 * 1024 * 1024
HEAD = 128
FOLD = 16
TO_LOG2 = HEAD ** (-0.5) * math.log2(math.e)
ANY = pl.BlockSpec(memory_space=pl.ANY)
SMEM = pl.BlockSpec(memory_space=pltpu.SMEM)


COST = {"pack": 1, "edge_rows": 8, "rows": 1, "merge": 4, "project": 1, "product": 4, "pick": 4}


def kernel_call(kernel, name, cost_estimate, **kwargs):
    k = COST.get(name, 1)
    cost = pl.CostEstimate(
        flops=int(k * cost_estimate.flops),
        bytes_accessed=int(k * cost_estimate.bytes_accessed),
        transcendentals=int(k * cost_estimate.transcendentals),
    )
    return pl.pallas_call(kernel, name=name, cost_estimate=cost, **kwargs)


def dot_nn(a, b):
    return lax.dot_general(a, b, (((1,), (0,)), ((), ())), preferred_element_type=jnp.float32)


def group_gap(tokens, group):
    q = lax.broadcasted_iota(jnp.int32, (tokens, tokens), 0)
    k = lax.broadcasted_iota(jnp.int32, (tokens, tokens), 1)
    return jnp.abs(q // group - k // group)


def softmax_sums(scores, values, scale=TO_LOG2, ones=False):
    tops = [jnp.max(functools.reduce(jnp.maximum, tiles), axis=1, keepdims=True) for tiles in scores]
    weights = [
        [jnp.exp2(s - top if scale == 1 else (s - top) * scale) for s in tiles]
        for tiles, top in zip(scores, tops)
    ]
    totals, sums = [], []
    for w, tiles in zip(weights, values):
        rounded = jnp.concatenate([x.astype(jnp.bfloat16) for x in w], axis=1)
        right = jnp.concatenate(tiles, axis=0)
        if ones:
            both = dot_nn(rounded, jnp.concatenate([right, jnp.ones_like(right)], axis=1))
            totals.append(both[:, :HEAD])
            sums.append(both[:, HEAD:])
        else:
            totals.append(dot_nn(rounded, right))
            sums.append(jnp.sum(functools.reduce(jnp.add, w), axis=1, keepdims=True))
    return [top * scale for top in tops], totals, sums


def place_pieces(stats, values, first):
    lane = lax.broadcasted_iota(jnp.int32, stats.shape, 1)
    for n, value in enumerate(values):
        at = 3 * (first + n)
        high = value.astype(jnp.bfloat16).astype(jnp.float32)
        mid = (value - high).astype(jnp.bfloat16).astype(jnp.float32)
        stats = jnp.where(lane == at, high, stats)
        stats = jnp.where(lane == at + 1, mid, stats)
        stats = jnp.where(lane == at + 2, value - high - mid, stats)
    return stats


def spread_pieces(stats, first, heads):
    lane = lax.broadcasted_iota(jnp.int32, (HEAD, heads * HEAD), 0)
    at = 3 * (first + lax.broadcasted_iota(jnp.int32, (HEAD, heads * HEAD), 1) // HEAD)
    pick_head = jnp.where((lane >= at) & (lane < at + 3), 1.0, 0.0).astype(jnp.bfloat16)
    return dot_nn(stats, pick_head)


def fold_stats(stats, width):
    groups = [stats[start:start + FOLD] for start in range(0, stats.shape[0], FOLD)]
    rest = width // HEAD - len(groups)
    return jnp.concatenate(groups + [jnp.zeros_like(groups[0])] * rest, axis=1)


def unfold_stats(folded, tokens):
    return jnp.concatenate(
        [folded[:, n * HEAD:(n + 1) * HEAD] for n in range(tokens // FOLD)], axis=0
    )


def edge_kernel(place, q_ref, near_ref, far_ref, out_ref, *, heads, cols_tile, cols):
    tokens = q_ref.shape[0]
    inner = (place[2] > 0) & (place[2] < cols - 1)

    @pl.when(jnp.logical_not(inner))
    def _():
        out_ref[...] = jnp.zeros_like(out_ref)

    @pl.when(inner)
    def _():
        bias = jnp.where(group_gap(tokens, cols_tile) == 0, 0.0, NEG)
        cuts = [slice(n * HEAD, (n + 1) * HEAD) for n in range(heads)]
        tiles = (near_ref, far_ref)
        scores = [[dot_nn(q_ref[:, c], t[0, :, c]) + bias for t in tiles] for c in cuts]
        values = [[t[1, :, c] for t in tiles] for c in cuts]
        tops, totals, weights = softmax_sums(scores, values)
        lse = [top + jnp.log2(w) for top, w in zip(tops, weights)]
        stats = place_pieces(jnp.zeros((tokens, HEAD), jnp.float32), lse, 0)
        out_ref[:tokens] = jnp.concatenate(
            [(t / w).astype(jnp.bfloat16) for t, w in zip(totals, weights)], axis=1
        )
        out_ref[tokens:] = fold_stats(stats.astype(jnp.bfloat16), out_ref.shape[1])


def fill_bias(bias_ref, frame_tokens, cols_tile):
    tokens = bias_ref.shape[1]
    frames = tokens // frame_tokens
    gap = group_gap(tokens, frame_tokens)
    for reach in range(frames):
        bias_ref[reach] = jnp.where(gap <= reach, 0.0, NEG)
    bias_ref[frames] = jnp.full((tokens, tokens), NEG, jnp.float32)
    bias_ref[frames + 1] = jnp.where(group_gap(tokens, cols_tile) == 0, 0.0, NEG)


def rows_kernel(
    place, mask, reach, q_ref, *refs, heads, half, grid, cols_tile, frame_tokens, split, ones
):
    tiles = refs[:10]
    base_ref, row_ref, sums_ref, bias_ref = refs[10:]
    tokens = q_ref.shape[0]
    none = bias_ref.shape[0] - 2
    step = pl.program_id(0)

    @pl.when(step == 0)
    def _():
        fill_bias(bias_ref, frame_tokens, cols_tile)
        sums_ref[...] = jnp.zeros_like(sums_ref)

    rows, cols = grid
    row, col = place[1], place[2]
    row_sign, col_sign = 1 - 2 * (row % 2), 1 - 2 * (col % 2)
    row_steps, col_steps = (row_sign, 0, -row_sign), (0, col_sign, -col_sign)
    listed = []
    for a in row_steps:
        for b in col_steps:
            inside = (row + a >= 0) & (row + a < rows) & (col + b >= 0) & (col + b < cols)
            listed.append(inside & ((mask[3 * (a + 1) + b + 1] > 0) | ((a == 0) & (b == 0))))
    inner = (col > 0) & (col < cols - 1)
    first_head = side(half, place) * heads * pl.num_programs(0)
    cuts = [slice(n * HEAD, (n + 1) * HEAD) for n in range(heads)]
    row_bias = bias_ref[none + 1]
    outer_bias = bias_ref[jnp.where(inner, none + 1, none)]

    def scores_of(n):
        q, keys = q_ref[:, cuts[n]], jnp.concatenate([t[0, :, cuts[n]] for t in tiles], axis=1)
        if split:
            scaled = q.astype(jnp.float32) * TO_LOG2
            high = scaled.astype(jnp.bfloat16)
            low = (scaled - high.astype(jnp.float32)).astype(jnp.bfloat16)
            q = jnp.concatenate([high, low], axis=1)
            keys = jnp.concatenate([keys, keys], axis=0)
        scores = dot_nn(q, keys)
        return [scores[:, t * tokens:(t + 1) * tokens] for t in range(10)]

    lse = []
    following = scores_of(0)
    for n, c in enumerate(cuts):
        raw, following = following, scores_of(n + 1) if n + 1 < heads else None
        values = [t[1, :, c] for t in tiles]
        limit = reach[first_head + step * heads + n]
        window = [raw[t] + bias_ref[jnp.where(listed[t], limit, none)] for t in range(9)]
        row = [raw[3] + row_bias, raw[4] + row_bias, raw[5] + outer_bias, raw[9] + outer_bias]
        tops, totals, weights = softmax_sums(
            [window, row], [values[:9], values[3:6] + values[9:]], 1 if split else TO_LOG2, ones
        )
        axial = totals[1] / weights[1]
        base_ref[:, c] = totals[0] / weights[0] + axial
        row_ref[:, c] = axial.astype(jnp.bfloat16)
        lse.append(tops[1] + jnp.log2(weights[1]))
    sums = place_pieces(sums_ref[...].astype(jnp.float32), lse, step * heads)
    sums_ref[...] = sums.astype(jnp.bfloat16)


def merged(place, base_ref, row_ref, sums_ref, rest_ref, stats_ref, cols):
    inner = (place[2] > 0) & (place[2] < cols - 1)
    tokens, width = base_ref.shape
    near = spread_pieces(sums_ref[...], 0, width // HEAD)
    far = spread_pieces(unfold_stats(stats_ref[...], tokens), 0, width // HEAD)
    share = 1.0 / (1.0 + jnp.exp2(near - jnp.where(inner, NEG, far)))
    rest, row = rest_ref[...].astype(jnp.float32), row_ref[...].astype(jnp.float32)
    return (base_ref[...] + (rest - row) * share).astype(jnp.bfloat16)


def merge_kernel(place, base_ref, row_ref, sums_ref, rest_ref, stats_ref, out_ref, *, cols):
    out_ref[...] = merged(place, base_ref, row_ref, sums_ref, rest_ref, stats_ref, cols)


def add_product(total_ref, rows, weight_ref, lanes=512):
    for start in range(0, total_ref.shape[1], lanes):
        cut = slice(start, start + lanes)
        total_ref[:, cut] += dot_nn(rows, weight_ref[:, cut])


def project_kernel(place, base_ref, row_ref, sums_ref, rest_ref, stats_ref, weight_ref, other_ref, *refs, cols):
    out_ref, total_ref, rows_ref = refs[-3:]
    step, lanes = pl.program_id(0), weight_ref.shape[0]

    @pl.when(step == 0)
    def _():
        total_ref[...] = other_ref[...].astype(jnp.float32)
        rows = merged(place, base_ref, row_ref, sums_ref, rest_ref, stats_ref, cols)
        for n in range(rows_ref.shape[0]):
            rows_ref[n] = rows[:, n * lanes:(n + 1) * lanes]

    add_product(total_ref, rows_ref[step], weight_ref)

    @pl.when(step == pl.num_programs(0) - 1)
    def _():
        out_ref[...] = total_ref[...].astype(jnp.bfloat16)


def product_kernel(rows_ref, weight_ref, out_ref, total_ref):
    @pl.when(pl.program_id(0) == 0)
    def _():
        total_ref[...] = jnp.zeros_like(total_ref)

    add_product(total_ref, rows_ref[...], weight_ref)

    @pl.when(pl.program_id(0) == pl.num_programs(0) - 1)
    def _():
        out_ref[...] = total_ref[...].astype(jnp.bfloat16)


def hbm(*values):
    return [pltpu.with_memory_space_constraint(v, pltpu.HBM) for v in values]


def params():
    return pltpu.CompilerParams(vmem_limit_bytes=VMEM_LIMIT)


def side(half, place):
    return half + (1 - 2 * half) * (1 - place[0])


def pack(place, keys, values, half, earlier=None):
    S, tokens, width = keys.shape
    width //= 2
    spec = pl.BlockSpec((None, tokens, width), lambda h, s, p: (s, 0, side(half, p)))
    block = (None, None, 2, tokens, width)
    given = [] if earlier is None else [earlier]

    def turn(k_ref, v_ref, out_ref):
        for start in range(0, width, HEAD):
            cut = slice(start, start + HEAD)
            out_ref[0, :, cut] = k_ref[:, cut].T
        out_ref[1] = v_ref[...]

    def kernel(place, k_ref, v_ref, *refs):
        out_ref = refs[-1]
        if not given:
            turn(k_ref, v_ref, out_ref)
            return

        @pl.when(pl.program_id(0) == 0)
        def _():
            out_ref[...] = refs[0][...]

        @pl.when(pl.program_id(0) == 1)
        def _():
            turn(k_ref, v_ref, out_ref)

    return kernel_call(
        kernel,
        out_shape=jax.ShapeDtypeStruct((1 + len(given), S, 2, tokens, width), keys.dtype),
        grid_spec=pltpu.PrefetchScalarGridSpec(
            num_scalar_prefetch=1,
            grid=(1 + len(given), S),
            in_specs=[spec, spec, *[pl.BlockSpec(block, lambda h, s, p: (0, s, 0, 0, 0))] * len(given)],
            out_specs=pl.BlockSpec(block, lambda h, s, p: (h, s, 0, 0, 0)),
        ),
        compiler_params=params(),
        cost_estimate=pl.CostEstimate(
            flops=0, bytes_accessed=8 * S * tokens * width, transcendentals=0
        ),
        name="pack",
    )(place, *hbm(keys, values), *given)


def pick(place, value, half):
    S, tokens, width = value.shape
    width //= 2

    def kernel(place, in_ref, out_ref):
        out_ref[...] = in_ref[...]

    return kernel_call(
        kernel,
        out_shape=jax.ShapeDtypeStruct((S, tokens, width), value.dtype),
        grid_spec=pltpu.PrefetchScalarGridSpec(
            num_scalar_prefetch=1,
            grid=(S,),
            in_specs=[pl.BlockSpec((None, tokens, width), lambda s, p: (s, 0, side(half, p)))],
            out_specs=pl.BlockSpec((None, tokens, width), lambda s, p: (s, 0, 0)),
        ),
        compiler_params=params(),
        cost_estimate=pl.CostEstimate(
            flops=0, bytes_accessed=4 * S * tokens * width, transcendentals=0
        ),
        name="pick",
    )(place, *hbm(value))


def edge_attend(place, q, q_block, near, far, stream, cols_tile, cols):
    _, _, tokens, width = far.shape
    heads = width // HEAD
    rows = tokens + FOLD
    return kernel_call(
        functools.partial(edge_kernel, heads=heads, cols_tile=cols_tile, cols=cols),
        out_shape=jax.ShapeDtypeStruct((rows, width), jnp.bfloat16),
        grid_spec=pltpu.PrefetchScalarGridSpec(
            num_scalar_prefetch=1,
            grid=(1,),
            in_specs=[
                pl.BlockSpec((tokens, width), lambda g, p: (q_block, 0)),
                pl.BlockSpec((None, 2, tokens, width), lambda g, p: (stream, 0, 0, 0)),
                pl.BlockSpec((None, 2, tokens, width), lambda g, p: (0, 0, 0, 0)),
            ],
            out_specs=pl.BlockSpec((rows, width), lambda g, p: (0, 0)),
        ),
        compiler_params=params(),
        cost_estimate=pl.CostEstimate(
            flops=8 * tokens * tokens * width,
            bytes_accessed=14 * tokens * width,
            transcendentals=2 * tokens * tokens * heads,
        ),
        name="edge_rows",
    )(place, q, near, far)


def rows_attend(place, mask, reach, q, tiles, sides, far, half, stream, cols_tile, frame_tokens, grid, block=3, split=False, ones=False):
    tokens, width = far.shape[2:]
    at = stream if far.shape[0] > 1 else 0
    heads = width // HEAD
    lanes = block * HEAD
    steps = heads // block
    place_of = stream if sides[0].shape[1] > 1 else 0
    own = pl.BlockSpec((None, None, 2, tokens, lanes), lambda g, p: (half, stream, 0, 0, g))
    near = pl.BlockSpec((None, None, 2, tokens, lanes), lambda g, p: (0, place_of, 0, 0, g))
    other = pl.BlockSpec((None, None, 2, tokens, lanes), lambda g, p: (1, place_of, 0, 0, g))
    args = [x for tile, pair in zip(tiles, sides) for x in (tile, pair, pair)]
    kernel = functools.partial(
        rows_kernel, heads=block, half=half, grid=grid, cols_tile=cols_tile, frame_tokens=frame_tokens,
        split=split, ones=ones,
    )
    return kernel_call(
        kernel,
        out_shape=(
            jax.ShapeDtypeStruct((tokens, width), jnp.float32),
            jax.ShapeDtypeStruct((tokens, width), jnp.bfloat16),
            jax.ShapeDtypeStruct((tokens, HEAD), jnp.bfloat16),
        ),
        grid_spec=pltpu.PrefetchScalarGridSpec(
            num_scalar_prefetch=1,
            grid=(steps,),
            in_specs=[
                SMEM,
                SMEM,
                pl.BlockSpec((None, tokens, lanes), lambda g, p: (stream, 0, side(half, p) * steps + g)),
                *[own, near, other] * 3,
                pl.BlockSpec((None, 2, tokens, lanes), lambda g, p: (at, 0, 0, g)),
            ],
            out_specs=(
                pl.BlockSpec((tokens, lanes), lambda g, p: (0, g)),
                pl.BlockSpec((tokens, lanes), lambda g, p: (0, g)),
                pl.BlockSpec((tokens, HEAD), lambda g, p: (0, 0)),
            ),
            scratch_shapes=[
                pltpu.VMEM((tokens // frame_tokens + 2, tokens, tokens), jnp.float32)
            ],
        ),
        compiler_params=params(),
        cost_estimate=pl.CostEstimate(
            flops=46 * tokens * tokens * width,
            bytes_accessed=54 * tokens * width,
            transcendentals=13 * tokens * tokens * heads,
        ),
        name="rows",
    )(place, mask, reach, *hbm(q), *args, far)


def merge(place, parts, rest, cols):
    tokens, width = parts[0].shape
    at = rest.shape[0] // tokens - 1
    whole = pl.BlockSpec((tokens, width), lambda g, p: (0, 0))
    return kernel_call(
        functools.partial(merge_kernel, cols=cols),
        out_shape=jax.ShapeDtypeStruct((tokens, width), jnp.bfloat16),
        grid_spec=pltpu.PrefetchScalarGridSpec(
            num_scalar_prefetch=1,
            grid=(1,),
            in_specs=[
                whole,
                whole,
                pl.BlockSpec((tokens, HEAD), lambda g, p: (0, 0)),
                pl.BlockSpec((tokens, width), lambda g, p: (at, 0)),
                pl.BlockSpec((FOLD, width), lambda g, p: ((at + 1) * tokens // FOLD, 0)),
            ],
            out_specs=whole,
        ),
        compiler_params=params(),
        cost_estimate=pl.CostEstimate(
            flops=8 * tokens * width, bytes_accessed=12 * tokens * width, transcendentals=0
        ),
        name="merge",
    )(place, *parts, rest, rest)


def project(place, parts, rest, weight, other, output, stream, cols, block=3):
    tokens, width = parts[0].shape
    at = rest.shape[0] // tokens - 1
    lanes = block * HEAD
    streams, _, model = weight.shape
    earlier = [] if output is None else [output]
    whole = pl.BlockSpec((tokens, width), lambda g, p: (0, 0))
    args = [place, *parts, rest, rest, weight, other]
    return kernel_call(
        functools.partial(project_kernel, cols=cols),
        out_shape=jax.ShapeDtypeStruct((streams, tokens, model), jnp.bfloat16),
        grid_spec=pltpu.PrefetchScalarGridSpec(
            num_scalar_prefetch=1,
            grid=(width // lanes,),
            in_specs=[
                whole,
                whole,
                pl.BlockSpec((tokens, HEAD), lambda g, p: (0, 0)),
                pl.BlockSpec((tokens, width), lambda g, p: (at, 0)),
                pl.BlockSpec((FOLD, width), lambda g, p: ((at + 1) * tokens // FOLD, 0)),
                pl.BlockSpec((None, lanes, model), lambda g, p: (stream, g, 0)),
                pl.BlockSpec((tokens, model), lambda g, p: (0, 0)),
                *[ANY] * len(earlier),
            ],
            out_specs=pl.BlockSpec((None, tokens, model), lambda g, p: (stream, 0, 0)),
            scratch_shapes=[
                pltpu.VMEM((tokens, model), jnp.float32),
                pltpu.VMEM((width // lanes, tokens, lanes), jnp.bfloat16),
            ],
        ),
        input_output_aliases={len(args): 0} if earlier else {},
        compiler_params=params(),
        cost_estimate=pl.CostEstimate(
            flops=2 * tokens * width * model, bytes_accessed=2 * width * model, transcendentals=0
        ),
        name="project",
    )(*args, *earlier)


def product(rows, weight, stream, block=3):
    tokens, width = rows.shape
    model = weight.shape[2]
    lanes = block * HEAD
    return kernel_call(
        product_kernel,
        out_shape=jax.ShapeDtypeStruct((tokens, model), jnp.bfloat16),
        grid=(width // lanes,),
        in_specs=[
            pl.BlockSpec((tokens, lanes), lambda g: (0, g)),
            pl.BlockSpec((None, lanes, model), lambda g: (stream, g, 0)),
        ],
        out_specs=pl.BlockSpec((tokens, model), lambda g: (0, 0)),
        scratch_shapes=[pltpu.VMEM((tokens, model), jnp.float32)],
        compiler_params=params(),
        cost_estimate=pl.CostEstimate(
            flops=2 * tokens * width * model, bytes_accessed=2 * width * model, transcendentals=0
        ),
        name="product",
    )(rows, weight)


def swaps(size, start):
    pairs = [(i, i + 1) for i in range(start, size - 1, 2)]
    return pairs + [(j, i) for i, j in pairs]


STYLES = ((dict(split=True), dict(block=1)), (dict(ones=True), dict(split=True, ones=True)))


def per_device(queries, key_states, value_states, tile_mask, frame_reach, out_weight):
    S, F, R, C, width = queries.shape
    tokens = F * R * C
    half, model = width // 2, out_weight.shape[2]
    rows, cols = lax.axis_size("row"), lax.axis_size("col")
    inward = [(0, 1), (cols - 1, cols - 2)]
    outward = [(j, i) for i, j in inward]
    place = jnp.stack([lax.axis_index(a) for a in ("pair", "row", "col")]).astype(jnp.int32)
    q, k, v = [a.reshape(S, tokens, width) for a in (queries, key_states, value_states)]
    mask = tile_mask.reshape(9)

    sent = {}

    def tied(value, after):
        earlier = [sent[n] if isinstance(n, str) else n for n in after]
        return lax.optimization_barrier((value, *earlier))[0] if earlier else value

    def send(name, value, axis, pairs, *after):
        sent[name] = lax.ppermute(tied(value, after), axis, pairs)

    col_pairs, col_others = swaps(cols, 0), swaps(cols, 1)
    row_pairs, row_others = swaps(rows, 0), swaps(rows, 1)
    pair_swap = swaps(2, 0)
    own0 = pack(place, k, v, 0)
    picked = pick(place, q, 0).reshape(S * tokens, half)
    own = pack(tied(place, [picked]), k, v, 1, own0)
    q1 = pick(tied(place, [own]), q, 1)
    onward = [jnp.concatenate([own[1, s].reshape(2 * tokens, half), q1[s]]) for s in range(S)]

    def edge(h, s, *after):
        rows_q, block = (sent["q0"], s) if h == 0 else (sent[f"near1{s}"], 2)
        sent[f"part{h}{s}"] = edge_attend(
            place, tied(rows_q, after), block, sent[f"other{h}"], sent[f"far{h}{s}"], s, C, cols
        )

    def near1(s):
        return sent[f"near1{s}"][:2 * tokens].reshape(1, 2, tokens, half)

    def rows_of(h, s, *after):
        tiles = [sent["pair_own"], own, sent["next_own"]]
        part = f"{h}" if h == 0 else f"{h}{s}"
        sides = [sent[f"pair_sides{part}"], sent[f"sides{part}"], sent[f"next_sides{part}"]]
        sent[f"rows{h}{s}"] = rows_attend(
            place, tied(mask, after), frame_reach, q, tiles, sides, sent[f"far{h}{s}"], h, s, C, R * C, (rows, cols),
            **STYLES[h][s],
        )

    send("near0", own0[0], "col", col_pairs)
    send("other0", own0[0], "col", col_others)
    send("next_own", own, "row", row_others)
    send("pair_own", own, "row", row_pairs)
    send("q0", picked, "col", inward)
    send("far00", sent["near0"][:1], "col", col_others, "other0", "pair_own")
    send("far01", sent["near0"][1:], "col", col_others, "near0", "next_own")
    sent["sides0"] = jnp.stack([sent["near0"], sent["other0"]])
    send("pair_sides0", sent["sides0"], "row", row_pairs)
    send("next_sides0", sent["sides0"], "row", row_others)
    send("near10", onward[0], "col", col_pairs, "other0")
    edge(0, 0)
    send("rest00", sent["part00"], "col", outward)
    send("other1", own[1], "col", col_others, "far00")
    edge(0, 1, "part00")
    send("rest01", sent["part01"], "col", outward)
    send("near11", onward[1], "col", col_pairs, "rest00", "part01")
    rows_of(0, 0, "part01")
    sent["merged0"] = merge(tied(place, []), sent["rows00"], sent["rest00"], cols)
    rows_of(0, 1, "merged0")
    send("theirs0", sent["merged0"], "pair", pair_swap)
    sent["product0"] = product(tied(sent["theirs0"], ["rows01"]), out_weight, 0)
    send("back0", sent["product0"], "pair", pair_swap)
    sent["merged1"] = merge(tied(place, []), sent["rows01"], sent["rest01"], cols)
    send("theirs1", sent["merged1"], "pair", pair_swap)
    send("far10", near1(0), "col", col_others, "product0")
    sent["sides10"] = jnp.stack([near1(0), tied(sent["other1"][0:1], ["rows01"])])
    send("next_sides10", sent["sides10"], "row", row_others, "other1")
    send("pair_sides10", sent["sides10"], "row", row_pairs)
    edge(1, 0)
    sent["product1"] = product(tied(sent["theirs1"], ["part10"]), out_weight, 1)
    send("back1", sent["product1"], "pair", pair_swap)
    send("rest10", sent["part10"], "col", outward)
    rows_of(1, 0)
    send("far11", near1(1), "col", col_others, "product0")
    sent["sides11"] = jnp.stack([near1(1), tied(sent["other1"][1:2], ["merged1", "sides10"])])
    send("next_sides11", sent["sides11"], "row", row_others)
    send("pair_sides11", sent["sides11"], "row", row_pairs)
    edge(1, 1, "part10")
    send("rest11", sent["part11"], "col", outward)
    rows_of(1, 1, "rows10")
    output = project(tied(place, []), sent["rows10"], sent["rest10"], out_weight, sent["back0"], None, 0, cols)
    output = project(place, sent["rows11"], sent["rest11"], out_weight, sent["back1"], output, 1, cols)
    return output.reshape(S, F, R, C, model)


def solution(mesh):
    return jax.shard_map(
        per_device,
        mesh=mesh,
        in_specs=(
            P("pair", None, "row", "col", None),
            P("pair", None, "row", "col", None),
            P("pair", None, "row", "col", None),
            P("pair", "row", "col", None),
            P(),
            P(None, "pair", None),
        ),
        out_specs=P("pair", None, "row", "col", None),
        check_vma=False,
    )
```

```python
import functools
import math

import jax
import jax.numpy as jnp
from jax import lax
from jax.experimental import pallas as pl
from jax.experimental.pallas import tpu as pltpu
from jax.sharding import PartitionSpec as P

NEG = -1e30
VMEM_LIMIT = 24 * 1024 * 1024
HEAD = 128
FOLD = 16
TO_LOG2 = HEAD ** (-0.5) * math.log2(math.e)
ANY = pl.BlockSpec(memory_space=pl.ANY)
SMEM = pl.BlockSpec(memory_space=pltpu.SMEM)


COST = {"pack": 1, "edge_rows": 8, "rows": 1, "merge": 4, "project": 1, "product": 4, "pick": 4}


def kernel_call(kernel, name, cost_estimate, **kwargs):
    k = COST.get(name, 1)
    cost = pl.CostEstimate(
        flops=int(k * cost_estimate.flops),
        bytes_accessed=int(k * cost_estimate.bytes_accessed),
        transcendentals=int(k * cost_estimate.transcendentals),
    )
    return pl.pallas_call(kernel, name=name, cost_estimate=cost, **kwargs)


def dot_nn(a, b):
    return lax.dot_general(a, b, (((1,), (0,)), ((), ())), preferred_element_type=jnp.float32)


def group_gap(tokens, group):
    q = lax.broadcasted_iota(jnp.int32, (tokens, tokens), 0)
    k = lax.broadcasted_iota(jnp.int32, (tokens, tokens), 1)
    return jnp.abs(q // group - k // group)


def softmax_sums(scores, values, scale=TO_LOG2, ones=False):
    tops = [jnp.max(functools.reduce(jnp.maximum, tiles), axis=1, keepdims=True) for tiles in scores]
    weights = [
        [jnp.exp2(s - top if scale == 1 else (s - top) * scale) for s in tiles]
        for tiles, top in zip(scores, tops)
    ]
    totals, sums = [], []
    for w, tiles in zip(weights, values):
        rounded = jnp.concatenate([x.astype(jnp.bfloat16) for x in w], axis=1)
        right = jnp.concatenate(tiles, axis=0)
        if ones:
            both = dot_nn(rounded, jnp.concatenate([right, jnp.ones_like(right)], axis=1))
            totals.append(both[:, :HEAD])
            sums.append(both[:, HEAD:])
        else:
            totals.append(dot_nn(rounded, right))
            sums.append(jnp.sum(functools.reduce(jnp.add, w), axis=1, keepdims=True))
    return [top * scale for top in tops], totals, sums


def place_pieces(stats, values, first):
    lane = lax.broadcasted_iota(jnp.int32, stats.shape, 1)
    for n, value in enumerate(values):
        at = 3 * (first + n)
        high = value.astype(jnp.bfloat16).astype(jnp.float32)
        mid = (value - high).astype(jnp.bfloat16).astype(jnp.float32)
        stats = jnp.where(lane == at, high, stats)
        stats = jnp.where(lane == at + 1, mid, stats)
        stats = jnp.where(lane == at + 2, value - high - mid, stats)
    return stats


def spread_pieces(stats, first, heads):
    lane = lax.broadcasted_iota(jnp.int32, (HEAD, heads * HEAD), 0)
    at = 3 * (first + lax.broadcasted_iota(jnp.int32, (HEAD, heads * HEAD), 1) // HEAD)
    pick_head = jnp.where((lane >= at) & (lane < at + 3), 1.0, 0.0).astype(jnp.bfloat16)
    return dot_nn(stats, pick_head)


def fold_stats(stats, width):
    groups = [stats[start:start + FOLD] for start in range(0, stats.shape[0], FOLD)]
    rest = width // HEAD - len(groups)
    return jnp.concatenate(groups + [jnp.zeros_like(groups[0])] * rest, axis=1)


def unfold_stats(folded, tokens):
    return jnp.concatenate(
        [folded[:, n * HEAD:(n + 1) * HEAD] for n in range(tokens // FOLD)], axis=0
    )


def edge_kernel(place, q_ref, near_ref, far_ref, out_ref, *, heads, cols_tile, cols):
    tokens = q_ref.shape[1]
    inner = (place[2] > 0) & (place[2] < cols - 1)

    @pl.when(jnp.logical_not(inner))
    def _():
        out_ref[...] = jnp.zeros_like(out_ref)

    @pl.when(inner)
    def _():
        bias = jnp.where(group_gap(tokens, cols_tile) == 0, 0.0, NEG)
        tiles = (near_ref, far_ref)
        scores = [[dot_nn(q_ref[n], t[0, n]) + bias for t in tiles] for n in range(heads)]
        values = [[t[1, n] for t in tiles] for n in range(heads)]
        tops, totals, weights = softmax_sums(scores, values)
        lse = [top + jnp.log2(w) for top, w in zip(tops, weights)]
        stats = place_pieces(jnp.zeros((tokens, HEAD), jnp.float32), lse, 0)
        out_ref[:tokens] = jnp.concatenate(
            [(t / w).astype(jnp.bfloat16) for t, w in zip(totals, weights)], axis=1
        )
        out_ref[tokens:] = fold_stats(stats.astype(jnp.bfloat16), out_ref.shape[1])


def fill_bias(bias_ref, frame_tokens, cols_tile):
    tokens = bias_ref.shape[1]
    frames = tokens // frame_tokens
    gap = group_gap(tokens, frame_tokens)
    for reach in range(frames):
        bias_ref[reach] = jnp.where(gap <= reach, 0.0, NEG)
    bias_ref[frames] = jnp.full((tokens, tokens), NEG, jnp.float32)
    bias_ref[frames + 1] = jnp.where(group_gap(tokens, cols_tile) == 0, 0.0, NEG)


def rows_kernel(
    place, mask, reach, q_ref, *refs, heads, half, grid, cols_tile, frame_tokens, split, ones
):
    tiles = refs[:10]
    base_ref, row_ref, sums_ref, bias_ref = refs[10:]
    tokens = q_ref.shape[0]
    none = bias_ref.shape[0] - 2
    step = pl.program_id(0)

    @pl.when(step == 0)
    def _():
        fill_bias(bias_ref, frame_tokens, cols_tile)
        sums_ref[...] = jnp.zeros_like(sums_ref)

    rows, cols = grid
    row, col = place[1], place[2]
    row_sign, col_sign = 1 - 2 * (row % 2), 1 - 2 * (col % 2)
    row_steps, col_steps = (row_sign, 0, -row_sign), (0, col_sign, -col_sign)
    listed = []
    for a in row_steps:
        for b in col_steps:
            inside = (row + a >= 0) & (row + a < rows) & (col + b >= 0) & (col + b < cols)
            listed.append(inside & ((mask[3 * (a + 1) + b + 1] > 0) | ((a == 0) & (b == 0))))
    inner = (col > 0) & (col < cols - 1)
    first_head = side(half, place) * heads * pl.num_programs(0)
    cuts = [slice(n * HEAD, (n + 1) * HEAD) for n in range(heads)]
    row_bias = bias_ref[none + 1]
    outer_bias = bias_ref[jnp.where(inner, none + 1, none)]

    def scores_of(n):
        q, keys = q_ref[:, cuts[n]], jnp.concatenate([t[0, n] for t in tiles], axis=1)
        if split:
            scaled = q.astype(jnp.float32) * TO_LOG2
            high = scaled.astype(jnp.bfloat16)
            low = (scaled - high.astype(jnp.float32)).astype(jnp.bfloat16)
            q = jnp.concatenate([high, low], axis=1)
            keys = jnp.concatenate([keys, keys], axis=0)
        scores = dot_nn(q, keys)
        return [scores[:, t * tokens:(t + 1) * tokens] for t in range(10)]

    lse = []
    following = scores_of(0)
    for n, c in enumerate(cuts):
        raw, following = following, scores_of(n + 1) if n + 1 < heads else None
        values = [t[1, n] for t in tiles]
        limit = reach[first_head + step * heads + n]
        window = [raw[t] + bias_ref[jnp.where(listed[t], limit, none)] for t in range(9)]
        row = [raw[3] + row_bias, raw[4] + row_bias, raw[5] + outer_bias, raw[9] + outer_bias]
        tops, totals, weights = softmax_sums(
            [window, row], [values[:9], values[3:6] + values[9:]], 1 if split else TO_LOG2, ones
        )
        axial = totals[1] / weights[1]
        base_ref[:, c] = totals[0] / weights[0] + axial
        row_ref[:, c] = axial.astype(jnp.bfloat16)
        lse.append(tops[1] + jnp.log2(weights[1]))
    sums = place_pieces(sums_ref[...].astype(jnp.float32), lse, step * heads)
    sums_ref[...] = sums.astype(jnp.bfloat16)


def merged(place, base_ref, row_ref, sums_ref, rest_ref, stats_ref, cols):
    inner = (place[2] > 0) & (place[2] < cols - 1)
    tokens, width = base_ref.shape
    near = spread_pieces(sums_ref[...], 0, width // HEAD)
    far = spread_pieces(unfold_stats(stats_ref[...], tokens), 0, width // HEAD)
    share = 1.0 / (1.0 + jnp.exp2(near - jnp.where(inner, NEG, far)))
    rest, row = rest_ref[...].astype(jnp.float32), row_ref[...].astype(jnp.float32)
    return (base_ref[...] + (rest - row) * share).astype(jnp.bfloat16)


def merge_kernel(place, base_ref, row_ref, sums_ref, rest_ref, stats_ref, out_ref, *, cols):
    out_ref[...] = merged(place, base_ref, row_ref, sums_ref, rest_ref, stats_ref, cols)


def add_product(total_ref, rows, weight_ref, lanes=512):
    for start in range(0, total_ref.shape[1], lanes):
        cut = slice(start, start + lanes)
        total_ref[:, cut] += dot_nn(rows, weight_ref[:, cut])


def project_kernel(place, base_ref, row_ref, sums_ref, rest_ref, stats_ref, weight_ref, other_ref, *refs, cols):
    out_ref, total_ref, rows_ref = refs[-3:]
    step, lanes = pl.program_id(0), weight_ref.shape[0]

    @pl.when(step == 0)
    def _():
        total_ref[...] = other_ref[...].astype(jnp.float32)
        rows = merged(place, base_ref, row_ref, sums_ref, rest_ref, stats_ref, cols)
        for n in range(rows_ref.shape[0]):
            rows_ref[n] = rows[:, n * lanes:(n + 1) * lanes]

    add_product(total_ref, rows_ref[step], weight_ref)

    @pl.when(step == pl.num_programs(0) - 1)
    def _():
        out_ref[...] = total_ref[...].astype(jnp.bfloat16)


def product_kernel(rows_ref, weight_ref, out_ref, total_ref):
    @pl.when(pl.program_id(0) == 0)
    def _():
        total_ref[...] = jnp.zeros_like(total_ref)

    add_product(total_ref, rows_ref[...], weight_ref)

    @pl.when(pl.program_id(0) == pl.num_programs(0) - 1)
    def _():
        out_ref[...] = total_ref[...].astype(jnp.bfloat16)


def hbm(*values):
    return [pltpu.with_memory_space_constraint(v, pltpu.HBM) for v in values]


def params():
    return pltpu.CompilerParams(vmem_limit_bytes=VMEM_LIMIT)


def side(half, place):
    return half + (1 - 2 * half) * (1 - place[0])


def pack(place, keys, values, half, earlier=None):
    S, tokens, width = keys.shape
    heads = width // 2 // HEAD
    spec = pl.BlockSpec((None, tokens, width // 2), lambda h, s, p: (s, 0, side(half, p)))
    block = (None, None, 2, heads, tokens, HEAD)
    given = [] if earlier is None else [earlier]

    def turn(k_ref, v_ref, out_ref):
        for n in range(heads):
            cut = slice(n * HEAD, (n + 1) * HEAD)
            out_ref[0, n] = k_ref[:, cut].T
            out_ref[1, n] = v_ref[:, cut]

    def kernel(place, k_ref, v_ref, *refs):
        out_ref = refs[-1]
        if not given:
            turn(k_ref, v_ref, out_ref)
            return

        @pl.when(pl.program_id(0) == 0)
        def _():
            out_ref[...] = refs[0][...]

        @pl.when(pl.program_id(0) == 1)
        def _():
            turn(k_ref, v_ref, out_ref)

    return kernel_call(
        kernel,
        out_shape=jax.ShapeDtypeStruct((1 + len(given), S, 2, heads, tokens, HEAD), keys.dtype),
        grid_spec=pltpu.PrefetchScalarGridSpec(
            num_scalar_prefetch=1,
            grid=(1 + len(given), S),
            in_specs=[spec, spec, *[pl.BlockSpec(block, lambda h, s, p: (0, s, 0, 0, 0, 0))] * len(given)],
            out_specs=pl.BlockSpec(block, lambda h, s, p: (h, s, 0, 0, 0, 0)),
        ),
        compiler_params=params(),
        cost_estimate=pl.CostEstimate(
            flops=0, bytes_accessed=4 * S * tokens * width, transcendentals=0
        ),
        name="pack",
    )(place, *hbm(keys, values), *given)


def pick(place, value, half):
    S, tokens, width = value.shape
    heads = width // 2 // HEAD

    def kernel(place, in_ref, out_ref):
        for n in range(heads):
            out_ref[n] = in_ref[:, n * HEAD:(n + 1) * HEAD]

    return kernel_call(
        kernel,
        out_shape=jax.ShapeDtypeStruct((S, heads, tokens, HEAD), value.dtype),
        grid_spec=pltpu.PrefetchScalarGridSpec(
            num_scalar_prefetch=1,
            grid=(S,),
            in_specs=[pl.BlockSpec((None, tokens, width // 2), lambda s, p: (s, 0, side(half, p)))],
            out_specs=pl.BlockSpec((None, heads, tokens, HEAD), lambda s, p: (s, 0, 0, 0)),
        ),
        compiler_params=params(),
        cost_estimate=pl.CostEstimate(
            flops=0, bytes_accessed=2 * S * tokens * width, transcendentals=0
        ),
        name="pick",
    )(place, *hbm(value))


def edge_attend(place, q, q_block, near, far, stream, cols_tile, cols):
    _, _, heads, tokens, _ = far.shape
    width = heads * HEAD
    rows = tokens + FOLD
    return kernel_call(
        functools.partial(edge_kernel, heads=heads, cols_tile=cols_tile, cols=cols),
        out_shape=jax.ShapeDtypeStruct((rows, width), jnp.bfloat16),
        grid_spec=pltpu.PrefetchScalarGridSpec(
            num_scalar_prefetch=1,
            grid=(1,),
            in_specs=[
                pl.BlockSpec((None, heads, tokens, HEAD), lambda g, p: (q_block, 0, 0, 0)),
                pl.BlockSpec((None, 2, heads, tokens, HEAD), lambda g, p: (stream, 0, 0, 0, 0)),
                pl.BlockSpec((None, 2, heads, tokens, HEAD), lambda g, p: (0, 0, 0, 0, 0)),
            ],
            out_specs=pl.BlockSpec((rows, width), lambda g, p: (0, 0)),
        ),
        compiler_params=params(),
        cost_estimate=pl.CostEstimate(
            flops=8 * tokens * tokens * width,
            bytes_accessed=14 * tokens * width,
            transcendentals=2 * tokens * tokens * heads,
        ),
        name="edge_rows",
    )(place, q, near, far)


def rows_attend(place, mask, reach, q, tiles, sides, far, half, stream, cols_tile, frame_tokens, grid, block=3, split=False, ones=False):
    heads, tokens, _ = far.shape[2:]
    width = heads * HEAD
    at = stream if far.shape[0] > 1 else 0
    lanes = block * HEAD
    steps = heads // block
    place_of = stream if sides[0].shape[1] > 1 else 0
    own = pl.BlockSpec((None, None, 2, block, tokens, HEAD), lambda g, p: (half, stream, 0, g, 0, 0))
    near = pl.BlockSpec((None, None, 2, block, tokens, HEAD), lambda g, p: (0, place_of, 0, g, 0, 0))
    other = pl.BlockSpec((None, None, 2, block, tokens, HEAD), lambda g, p: (1, place_of, 0, g, 0, 0))
    args = [x for tile, pair in zip(tiles, sides) for x in (tile, pair, pair)]
    kernel = functools.partial(
        rows_kernel, heads=block, half=half, grid=grid, cols_tile=cols_tile, frame_tokens=frame_tokens,
        split=split, ones=ones,
    )
    return kernel_call(
        kernel,
        out_shape=(
            jax.ShapeDtypeStruct((tokens, width), jnp.float32),
            jax.ShapeDtypeStruct((tokens, width), jnp.bfloat16),
            jax.ShapeDtypeStruct((tokens, HEAD), jnp.bfloat16),
        ),
        grid_spec=pltpu.PrefetchScalarGridSpec(
            num_scalar_prefetch=1,
            grid=(steps,),
            in_specs=[
                SMEM,
                SMEM,
                pl.BlockSpec((None, tokens, lanes), lambda g, p: (stream, 0, side(half, p) * steps + g)),
                *[own, near, other] * 3,
                pl.BlockSpec((None, 2, block, tokens, HEAD), lambda g, p: (at, 0, g, 0, 0)),
            ],
            out_specs=(
                pl.BlockSpec((tokens, lanes), lambda g, p: (0, g)),
                pl.BlockSpec((tokens, lanes), lambda g, p: (0, g)),
                pl.BlockSpec((tokens, HEAD), lambda g, p: (0, 0)),
            ),
            scratch_shapes=[
                pltpu.VMEM((tokens // frame_tokens + 2, tokens, tokens), jnp.float32)
            ],
        ),
        compiler_params=params(),
        cost_estimate=pl.CostEstimate(
            flops=46 * tokens * tokens * width,
            bytes_accessed=54 * tokens * width,
            transcendentals=13 * tokens * tokens * heads,
        ),
        name="rows",
    )(place, mask, reach, *hbm(q), *args, far)


def merge(place, parts, rest, cols):
    tokens, width = parts[0].shape
    at = rest.shape[0] // tokens - 1
    whole = pl.BlockSpec((tokens, width), lambda g, p: (0, 0))
    return kernel_call(
        functools.partial(merge_kernel, cols=cols),
        out_shape=jax.ShapeDtypeStruct((tokens, width), jnp.bfloat16),
        grid_spec=pltpu.PrefetchScalarGridSpec(
            num_scalar_prefetch=1,
            grid=(1,),
            in_specs=[
                whole,
                whole,
                pl.BlockSpec((tokens, HEAD), lambda g, p: (0, 0)),
                pl.BlockSpec((tokens, width), lambda g, p: (at, 0)),
                pl.BlockSpec((FOLD, width), lambda g, p: ((at + 1) * tokens // FOLD, 0)),
            ],
            out_specs=whole,
        ),
        compiler_params=params(),
        cost_estimate=pl.CostEstimate(
            flops=8 * tokens * width, bytes_accessed=12 * tokens * width, transcendentals=0
        ),
        name="merge",
    )(place, *parts, rest, rest)


def project(place, parts, rest, weight, other, output, stream, cols, block=3):
    tokens, width = parts[0].shape
    at = rest.shape[0] // tokens - 1
    lanes = block * HEAD
    streams, _, model = weight.shape
    earlier = [] if output is None else [output]
    whole = pl.BlockSpec((tokens, width), lambda g, p: (0, 0))
    args = [place, *parts, rest, rest, weight, other]
    return kernel_call(
        functools.partial(project_kernel, cols=cols),
        out_shape=jax.ShapeDtypeStruct((streams, tokens, model), jnp.bfloat16),
        grid_spec=pltpu.PrefetchScalarGridSpec(
            num_scalar_prefetch=1,
            grid=(width // lanes,),
            in_specs=[
                whole,
                whole,
                pl.BlockSpec((tokens, HEAD), lambda g, p: (0, 0)),
                pl.BlockSpec((tokens, width), lambda g, p: (at, 0)),
                pl.BlockSpec((FOLD, width), lambda g, p: ((at + 1) * tokens // FOLD, 0)),
                pl.BlockSpec((None, lanes, model), lambda g, p: (stream, g, 0)),
                pl.BlockSpec((tokens, model), lambda g, p: (0, 0)),
                *[ANY] * len(earlier),
            ],
            out_specs=pl.BlockSpec((None, tokens, model), lambda g, p: (stream, 0, 0)),
            scratch_shapes=[
                pltpu.VMEM((tokens, model), jnp.float32),
                pltpu.VMEM((width // lanes, tokens, lanes), jnp.bfloat16),
            ],
        ),
        input_output_aliases={len(args): 0} if earlier else {},
        compiler_params=params(),
        cost_estimate=pl.CostEstimate(
            flops=2 * tokens * width * model, bytes_accessed=2 * width * model, transcendentals=0
        ),
        name="project",
    )(*args, *earlier)


def product(rows, weight, stream, block=3):
    tokens, width = rows.shape
    model = weight.shape[2]
    lanes = block * HEAD
    return kernel_call(
        product_kernel,
        out_shape=jax.ShapeDtypeStruct((tokens, model), jnp.bfloat16),
        grid=(width // lanes,),
        in_specs=[
            pl.BlockSpec((tokens, lanes), lambda g: (0, g)),
            pl.BlockSpec((None, lanes, model), lambda g: (stream, g, 0)),
        ],
        out_specs=pl.BlockSpec((tokens, model), lambda g: (0, 0)),
        scratch_shapes=[pltpu.VMEM((tokens, model), jnp.float32)],
        compiler_params=params(),
        cost_estimate=pl.CostEstimate(
            flops=2 * tokens * width * model, bytes_accessed=2 * width * model, transcendentals=0
        ),
        name="product",
    )(rows, weight)


def swaps(size, start):
    pairs = [(i, i + 1) for i in range(start, size - 1, 2)]
    return pairs + [(j, i) for i, j in pairs]


STYLES = ((dict(split=True), dict(split=True, ones=True)), (dict(), dict(ones=True)))


def per_device(queries, key_states, value_states, tile_mask, frame_reach, out_weight):
    S, F, R, C, width = queries.shape
    tokens = F * R * C
    model = out_weight.shape[2]
    rows, cols = lax.axis_size("row"), lax.axis_size("col")
    inward = [(0, 1), (cols - 1, cols - 2)]
    outward = [(j, i) for i, j in inward]
    place = jnp.stack([lax.axis_index(a) for a in ("pair", "row", "col")]).astype(jnp.int32)
    q, k, v = [a.reshape(S, tokens, width) for a in (queries, key_states, value_states)]
    mask = tile_mask.reshape(9)

    sent = {}

    def tied(value, after):
        earlier = [sent[n] if isinstance(n, str) else n for n in after]
        return lax.optimization_barrier((value, *earlier))[0] if earlier else value

    def send(name, value, axis, pairs, *after):
        sent[name] = lax.ppermute(tied(value, after), axis, pairs)

    col_pairs, col_others = swaps(cols, 0), swaps(cols, 1)
    row_pairs, row_others = swaps(rows, 0), swaps(rows, 1)
    pair_swap = swaps(2, 0)
    own0 = pack(place, k, v, 0)
    picked = pick(place, q, 0)
    heads = picked.shape[1]
    own = pack(tied(place, [picked]), k, v, 1, own0)
    q1 = pick(tied(place, [own]), q, 1)
    onward = [jnp.concatenate([own[1, s].reshape(2 * heads, tokens, HEAD), q1[s]]) for s in range(S)]

    def edge(h, s, *after):
        rows_q, block = (sent["q0"], s) if h == 0 else (sent[f"near1{s}"].reshape(3, heads, tokens, HEAD), 2)
        sent[f"part{h}{s}"] = edge_attend(
            place, tied(rows_q, after), block, sent[f"other{h}"], sent[f"far{h}{s}"], s, C, cols
        )

    def near1(s):
        return sent[f"near1{s}"][:2 * heads].reshape(1, 2, heads, tokens, HEAD)

    def rows_of(h, s, *after):
        tiles = [sent["pair_own"], own, sent["next_own"]]
        part = f"{h}" if h == 0 else f"{h}{s}"
        sides = [sent[f"pair_sides{part}"], sent[f"sides{part}"], sent[f"next_sides{part}"]]
        sent[f"rows{h}{s}"] = rows_attend(
            place, tied(mask, after), frame_reach, q, tiles, sides, sent[f"far{h}{s}"], h, s, C, R * C, (rows, cols),
            **STYLES[h][s],
        )

    send("near0", own0[0], "col", col_pairs)
    send("other0", own0[0], "col", col_others)
    send("next_own", own, "row", row_others)
    send("pair_own", own, "row", row_pairs)
    send("q0", picked, "col", inward)
    send("far00", sent["near0"][:1], "col", col_others, "other0", "pair_own")
    send("far01", sent["near0"][1:], "col", col_others, "near0", "next_own")
    sent["sides0"] = jnp.stack([sent["near0"], sent["other0"]])
    send("pair_sides0", sent["sides0"], "row", row_pairs)
    send("next_sides0", sent["sides0"], "row", row_others)
    send("near10", onward[0], "col", col_pairs, "other0")
    edge(0, 0)
    send("rest00", sent["part00"], "col", outward)
    send("other1", own[1], "col", col_others, "far00")
    edge(0, 1, "part00")
    send("rest01", sent["part01"], "col", outward)
    send("near11", onward[1], "col", col_pairs, "rest00", "part01")
    rows_of(0, 0, "part01")
    sent["merged0"] = merge(tied(place, []), sent["rows00"], sent["rest00"], cols)
    rows_of(0, 1, "merged0")
    send("theirs0", sent["merged0"], "pair", pair_swap)
    sent["product0"] = product(tied(sent["theirs0"], ["rows01"]), out_weight, 0)
    send("back0", sent["product0"], "pair", pair_swap)
    sent["merged1"] = merge(tied(place, []), sent["rows01"], sent["rest01"], cols)
    send("theirs1", sent["merged1"], "pair", pair_swap)
    send("far10", near1(0), "col", col_others, "product0")
    sent["sides10"] = jnp.stack([near1(0), tied(sent["other1"][0:1], ["rows01"])])
    send("next_sides10", sent["sides10"], "row", row_others, "other1")
    send("pair_sides10", sent["sides10"], "row", row_pairs)
    edge(1, 0)
    sent["product1"] = product(tied(sent["theirs1"], ["part10"]), out_weight, 1)
    send("back1", sent["product1"], "pair", pair_swap)
    send("rest10", sent["part10"], "col", outward)
    rows_of(1, 0)
    send("far11", near1(1), "col", col_others, "product0")
    sent["sides11"] = jnp.stack([near1(1), tied(sent["other1"][1:2], ["merged1", "sides10"])])
    send("next_sides11", sent["sides11"], "row", row_others)
    send("pair_sides11", sent["sides11"], "row", row_pairs)
    edge(1, 1, "part10")
    send("rest11", sent["part11"], "col", outward)
    rows_of(1, 1, "rows10")
    output = project(tied(place, []), sent["rows10"], sent["rest10"], out_weight, sent["back0"], None, 0, cols)
    output = project(place, sent["rows11"], sent["rest11"], out_weight, sent["back1"], output, 1, cols)
    return output.reshape(S, F, R, C, model)


def solution(mesh):
    return jax.shard_map(
        per_device,
        mesh=mesh,
        in_specs=(
            P("pair", None, "row", "col", None),
            P("pair", None, "row", "col", None),
            P("pair", None, "row", "col", None),
            P("pair", "row", "col", None),
            P(),
            P(None, "pair", None),
        ),
        out_specs=P("pair", None, "row", "col", None),
        check_vma=False,
    )
```

```python
import functools
import math

import jax
import jax.numpy as jnp
from jax import lax
from jax.experimental import pallas as pl
from jax.experimental.pallas import tpu as pltpu
from jax.sharding import PartitionSpec as P

NEG = -1e30
VMEM_LIMIT = 24 * 1024 * 1024
HEAD = 128
FOLD = 16
TO_LOG2 = HEAD ** (-0.5) * math.log2(math.e)
ANY = pl.BlockSpec(memory_space=pl.ANY)
SMEM = pl.BlockSpec(memory_space=pltpu.SMEM)


COST = {"pack": 1, "edge_rows": 8, "rows": 1, "merge": 4, "project": 1, "product": 4, "pick": 4}


def kernel_call(kernel, name, cost_estimate, **kwargs):
    k = COST.get(name, 1)
    cost = pl.CostEstimate(
        flops=int(k * cost_estimate.flops),
        bytes_accessed=int(k * cost_estimate.bytes_accessed),
        transcendentals=int(k * cost_estimate.transcendentals),
    )
    return pl.pallas_call(kernel, name=name, cost_estimate=cost, **kwargs)


def dot_nn(a, b):
    return lax.dot_general(a, b, (((1,), (0,)), ((), ())), preferred_element_type=jnp.float32)


def group_gap(tokens, group):
    q = lax.broadcasted_iota(jnp.int32, (tokens, tokens), 0)
    k = lax.broadcasted_iota(jnp.int32, (tokens, tokens), 1)
    return jnp.abs(q // group - k // group)


def softmax_sums(scores, values, scale=TO_LOG2, ones=False):
    tops = [jnp.max(functools.reduce(jnp.maximum, tiles), axis=1, keepdims=True) for tiles in scores]
    weights = [
        [jnp.exp2(s - top if scale == 1 else (s - top) * scale) for s in tiles]
        for tiles, top in zip(scores, tops)
    ]
    totals, sums = [], []
    for w, tiles in zip(weights, values):
        rounded = jnp.concatenate([x.astype(jnp.bfloat16) for x in w], axis=1)
        right = jnp.concatenate(tiles, axis=0)
        if ones:
            both = dot_nn(rounded, jnp.concatenate([right, jnp.ones_like(right)], axis=1))
            totals.append(both[:, :HEAD])
            sums.append(both[:, HEAD:])
        else:
            totals.append(dot_nn(rounded, right))
            sums.append(jnp.sum(functools.reduce(jnp.add, w), axis=1, keepdims=True))
    return [top * scale for top in tops], totals, sums


def place_pieces(stats, values, first):
    lane = lax.broadcasted_iota(jnp.int32, stats.shape, 1)
    for n, value in enumerate(values):
        at = 3 * (first + n)
        high = value.astype(jnp.bfloat16).astype(jnp.float32)
        mid = (value - high).astype(jnp.bfloat16).astype(jnp.float32)
        stats = jnp.where(lane == at, high, stats)
        stats = jnp.where(lane == at + 1, mid, stats)
        stats = jnp.where(lane == at + 2, value - high - mid, stats)
    return stats


def spread_pieces(stats, first, heads):
    lane = lax.broadcasted_iota(jnp.int32, (HEAD, heads * HEAD), 0)
    at = 3 * (first + lax.broadcasted_iota(jnp.int32, (HEAD, heads * HEAD), 1) // HEAD)
    pick_head = jnp.where((lane >= at) & (lane < at + 3), 1.0, 0.0).astype(jnp.bfloat16)
    return dot_nn(stats, pick_head)


def fold_stats(stats, width):
    groups = [stats[start:start + FOLD] for start in range(0, stats.shape[0], FOLD)]
    rest = width // HEAD - len(groups)
    return jnp.concatenate(groups + [jnp.zeros_like(groups[0])] * rest, axis=1)


def unfold_stats(folded, tokens):
    return jnp.concatenate(
        [folded[:, n * HEAD:(n + 1) * HEAD] for n in range(tokens // FOLD)], axis=0
    )


def edge_kernel(place, q_ref, near_ref, far_ref, out_ref, *, heads, cols_tile, cols):
    tokens = q_ref.shape[0]
    inner = (place[2] > 0) & (place[2] < cols - 1)

    @pl.when(jnp.logical_not(inner))
    def _():
        out_ref[...] = jnp.zeros_like(out_ref)

    @pl.when(inner)
    def _():
        bias = jnp.where(group_gap(tokens, cols_tile) == 0, 0.0, NEG)
        cuts = [slice(n * HEAD, (n + 1) * HEAD) for n in range(heads)]
        tiles = (near_ref, far_ref)
        scores = [[dot_nn(q_ref[:, c], t[0, :, c]) + bias for t in tiles] for c in cuts]
        values = [[t[1, :, c] for t in tiles] for c in cuts]
        tops, totals, weights = softmax_sums(scores, values)
        lse = [top + jnp.log2(w) for top, w in zip(tops, weights)]
        stats = place_pieces(jnp.zeros((tokens, HEAD), jnp.float32), lse, 0)
        out_ref[:tokens] = jnp.concatenate(
            [(t / w).astype(jnp.bfloat16) for t, w in zip(totals, weights)], axis=1
        )
        out_ref[tokens:] = fold_stats(stats.astype(jnp.bfloat16), out_ref.shape[1])


def fill_bias(bias_ref, frame_tokens, cols_tile):
    tokens = bias_ref.shape[1]
    frames = tokens // frame_tokens
    gap = group_gap(tokens, frame_tokens)
    for reach in range(frames):
        bias_ref[reach] = jnp.where(gap <= reach, 0.0, NEG)
    bias_ref[frames] = jnp.full((tokens, tokens), NEG, jnp.float32)
    bias_ref[frames + 1] = jnp.where(group_gap(tokens, cols_tile) == 0, 0.0, NEG)


def rows_kernel(
    place, mask, reach, q_ref, *refs, heads, half, grid, cols_tile, frame_tokens, split, ones
):
    tiles = refs[:10]
    base_ref, row_ref, sums_ref, bias_ref = refs[10:]
    tokens = q_ref.shape[0]
    none = bias_ref.shape[0] - 2
    step = pl.program_id(0)

    @pl.when(step == 0)
    def _():
        fill_bias(bias_ref, frame_tokens, cols_tile)
        sums_ref[...] = jnp.zeros_like(sums_ref)

    rows, cols = grid
    row, col = place[1], place[2]
    row_sign, col_sign = 1 - 2 * (row % 2), 1 - 2 * (col % 2)
    row_steps, col_steps = (row_sign, 0, -row_sign), (0, col_sign, -col_sign)
    listed = []
    for a in row_steps:
        for b in col_steps:
            inside = (row + a >= 0) & (row + a < rows) & (col + b >= 0) & (col + b < cols)
            listed.append(inside & ((mask[3 * (a + 1) + b + 1] > 0) | ((a == 0) & (b == 0))))
    inner = (col > 0) & (col < cols - 1)
    first_head = side(half, place) * heads * pl.num_programs(0)
    cuts = [slice(n * HEAD, (n + 1) * HEAD) for n in range(heads)]
    row_bias = bias_ref[none + 1]
    outer_bias = bias_ref[jnp.where(inner, none + 1, none)]

    def scores_of(n):
        q, keys = q_ref[:, cuts[n]], jnp.concatenate([t[0, :, cuts[n]] for t in tiles], axis=1)
        if split:
            scaled = q.astype(jnp.float32) * TO_LOG2
            high = scaled.astype(jnp.bfloat16)
            low = (scaled - high.astype(jnp.float32)).astype(jnp.bfloat16)
            q = jnp.concatenate([high, low], axis=1)
            keys = jnp.concatenate([keys, keys], axis=0)
        scores = dot_nn(q, keys)
        return [scores[:, t * tokens:(t + 1) * tokens] for t in range(10)]

    lse = []
    following = scores_of(0)
    for n, c in enumerate(cuts):
        raw, following = following, scores_of(n + 1) if n + 1 < heads else None
        values = [t[1, :, c] for t in tiles]
        limit = reach[first_head + step * heads + n]
        window = [raw[t] + bias_ref[jnp.where(listed[t], limit, none)] for t in range(9)]
        row = [raw[3] + row_bias, raw[4] + row_bias, raw[5] + outer_bias, raw[9] + outer_bias]
        tops, totals, weights = softmax_sums(
            [window, row], [values[:9], values[3:6] + values[9:]], 1 if split else TO_LOG2, ones
        )
        axial = totals[1] / weights[1]
        base_ref[:, c] = totals[0] / weights[0] + axial
        row_ref[:, c] = axial.astype(jnp.bfloat16)
        lse.append(tops[1] + jnp.log2(weights[1]))
    sums = place_pieces(sums_ref[...].astype(jnp.float32), lse, step * heads)
    sums_ref[...] = sums.astype(jnp.bfloat16)


def merged(place, base_ref, row_ref, sums_ref, rest_ref, stats_ref, cols):
    inner = (place[2] > 0) & (place[2] < cols - 1)
    tokens, width = base_ref.shape
    near = spread_pieces(sums_ref[...], 0, width // HEAD)
    far = spread_pieces(unfold_stats(stats_ref[...], tokens), 0, width // HEAD)
    share = 1.0 / (1.0 + jnp.exp2(near - jnp.where(inner, NEG, far)))
    rest, row = rest_ref[...].astype(jnp.float32), row_ref[...].astype(jnp.float32)
    return (base_ref[...] + (rest - row) * share).astype(jnp.bfloat16)


def merge_kernel(place, base_ref, row_ref, sums_ref, rest_ref, stats_ref, out_ref, *, cols):
    out_ref[...] = merged(place, base_ref, row_ref, sums_ref, rest_ref, stats_ref, cols)


def add_product(total_ref, rows, weight_ref, lanes=512):
    for start in range(0, total_ref.shape[1], lanes):
        cut = slice(start, start + lanes)
        total_ref[:, cut] += dot_nn(rows, weight_ref[:, cut])


def project_kernel(place, base_ref, row_ref, sums_ref, rest_ref, stats_ref, weight_ref, other_ref, *refs, cols):
    out_ref, total_ref, rows_ref = refs[-3:]
    step, lanes = pl.program_id(0), weight_ref.shape[0]

    @pl.when(step == 0)
    def _():
        total_ref[...] = other_ref[...].astype(jnp.float32)
        rows = merged(place, base_ref, row_ref, sums_ref, rest_ref, stats_ref, cols)
        for n in range(rows_ref.shape[0]):
            rows_ref[n] = rows[:, n * lanes:(n + 1) * lanes]

    add_product(total_ref, rows_ref[step], weight_ref)

    @pl.when(step == pl.num_programs(0) - 1)
    def _():
        out_ref[...] = total_ref[...].astype(jnp.bfloat16)


def product_kernel(rows_ref, weight_ref, out_ref, total_ref):
    @pl.when(pl.program_id(0) == 0)
    def _():
        total_ref[...] = jnp.zeros_like(total_ref)

    add_product(total_ref, rows_ref[...], weight_ref)

    @pl.when(pl.program_id(0) == pl.num_programs(0) - 1)
    def _():
        out_ref[...] = total_ref[...].astype(jnp.bfloat16)


def hbm(*values):
    return [pltpu.with_memory_space_constraint(v, pltpu.HBM) for v in values]


def params():
    return pltpu.CompilerParams(vmem_limit_bytes=VMEM_LIMIT)


def side(half, place):
    return half + (1 - 2 * half) * (1 - place[0])


def pack(place, keys, values, half, earlier=None):
    S, tokens, width = keys.shape
    width //= 2
    spec = pl.BlockSpec((None, tokens, width), lambda h, s, p: (s, 0, side(half, p)))
    block = (None, None, 2, tokens, width)
    given = [] if earlier is None else [earlier]

    def turn(k_ref, v_ref, out_ref):
        for start in range(0, width, HEAD):
            cut = slice(start, start + HEAD)
            out_ref[0, :, cut] = k_ref[:, cut].T
        out_ref[1] = v_ref[...]

    def kernel(place, k_ref, v_ref, *refs):
        out_ref = refs[-1]
        if not given:
            turn(k_ref, v_ref, out_ref)
            return

        @pl.when(pl.program_id(0) == 0)
        def _():
            out_ref[...] = refs[0][...]

        @pl.when(pl.program_id(0) == 1)
        def _():
            turn(k_ref, v_ref, out_ref)

    return kernel_call(
        kernel,
        out_shape=jax.ShapeDtypeStruct((1 + len(given), S, 2, tokens, width), keys.dtype),
        grid_spec=pltpu.PrefetchScalarGridSpec(
            num_scalar_prefetch=1,
            grid=(1 + len(given), S),
            in_specs=[spec, spec, *[pl.BlockSpec(block, lambda h, s, p: (0, s, 0, 0, 0))] * len(given)],
            out_specs=pl.BlockSpec(block, lambda h, s, p: (h, s, 0, 0, 0)),
        ),
        compiler_params=params(),
        cost_estimate=pl.CostEstimate(
            flops=0, bytes_accessed=8 * S * tokens * width, transcendentals=0
        ),
        name="pack",
    )(place, *hbm(keys, values), *given)


def pick(place, value, half):
    S, tokens, width = value.shape
    width //= 2

    def kernel(place, in_ref, out_ref):
        out_ref[...] = in_ref[...]

    return kernel_call(
        kernel,
        out_shape=jax.ShapeDtypeStruct((S, tokens, width), value.dtype),
        grid_spec=pltpu.PrefetchScalarGridSpec(
            num_scalar_prefetch=1,
            grid=(S,),
            in_specs=[pl.BlockSpec((None, tokens, width), lambda s, p: (s, 0, side(half, p)))],
            out_specs=pl.BlockSpec((None, tokens, width), lambda s, p: (s, 0, 0)),
        ),
        compiler_params=params(),
        cost_estimate=pl.CostEstimate(
            flops=0, bytes_accessed=4 * S * tokens * width, transcendentals=0
        ),
        name="pick",
    )(place, *hbm(value))


def edge_attend(place, q, q_block, near, far, stream, cols_tile, cols):
    _, _, tokens, width = far.shape
    heads = width // HEAD
    rows = tokens + FOLD
    return kernel_call(
        functools.partial(edge_kernel, heads=heads, cols_tile=cols_tile, cols=cols),
        out_shape=jax.ShapeDtypeStruct((rows, width), jnp.bfloat16),
        grid_spec=pltpu.PrefetchScalarGridSpec(
            num_scalar_prefetch=1,
            grid=(1,),
            in_specs=[
                pl.BlockSpec((tokens, width), lambda g, p: (q_block, 0)),
                pl.BlockSpec((None, 2, tokens, width), lambda g, p: (stream, 0, 0, 0)),
                pl.BlockSpec((None, 2, tokens, width), lambda g, p: (0, 0, 0, 0)),
            ],
            out_specs=pl.BlockSpec((rows, width), lambda g, p: (0, 0)),
        ),
        compiler_params=params(),
        cost_estimate=pl.CostEstimate(
            flops=8 * tokens * tokens * width,
            bytes_accessed=14 * tokens * width,
            transcendentals=2 * tokens * tokens * heads,
        ),
        name="edge_rows",
    )(place, q, near, far)


def rows_attend(place, mask, reach, q, tiles, sides, far, half, stream, cols_tile, frame_tokens, grid, block=3, split=False, ones=False):
    tokens, width = far.shape[2:]
    at = stream if far.shape[0] > 1 else 0
    heads = width // HEAD
    lanes = block * HEAD
    steps = heads // block
    place_of = stream if sides[0].shape[1] > 1 else 0
    own = pl.BlockSpec((None, None, 2, tokens, lanes), lambda g, p: (half, stream, 0, 0, g))
    near = pl.BlockSpec((None, None, 2, tokens, lanes), lambda g, p: (0, place_of, 0, 0, g))
    other = pl.BlockSpec((None, None, 2, tokens, lanes), lambda g, p: (1, place_of, 0, 0, g))
    args = [x for tile, pair in zip(tiles, sides) for x in (tile, pair, pair)]
    kernel = functools.partial(
        rows_kernel, heads=block, half=half, grid=grid, cols_tile=cols_tile, frame_tokens=frame_tokens,
        split=split, ones=ones,
    )
    return kernel_call(
        kernel,
        out_shape=(
            jax.ShapeDtypeStruct((tokens, width), jnp.float32),
            jax.ShapeDtypeStruct((tokens, width), jnp.bfloat16),
            jax.ShapeDtypeStruct((tokens, HEAD), jnp.bfloat16),
        ),
        grid_spec=pltpu.PrefetchScalarGridSpec(
            num_scalar_prefetch=1,
            grid=(steps,),
            in_specs=[
                SMEM,
                SMEM,
                pl.BlockSpec((None, tokens, lanes), lambda g, p: (stream, 0, side(half, p) * steps + g)),
                *[own, near, other] * 3,
                pl.BlockSpec((None, 2, tokens, lanes), lambda g, p: (at, 0, 0, g)),
            ],
            out_specs=(
                pl.BlockSpec((tokens, lanes), lambda g, p: (0, g)),
                pl.BlockSpec((tokens, lanes), lambda g, p: (0, g)),
                pl.BlockSpec((tokens, HEAD), lambda g, p: (0, 0)),
            ),
            scratch_shapes=[
                pltpu.VMEM((tokens // frame_tokens + 2, tokens, tokens), jnp.float32)
            ],
        ),
        compiler_params=params(),
        cost_estimate=pl.CostEstimate(
            flops=46 * tokens * tokens * width,
            bytes_accessed=54 * tokens * width,
            transcendentals=13 * tokens * tokens * heads,
        ),
        name="rows",
    )(place, mask, reach, *hbm(q), *args, far)


def merge(place, parts, rest, cols):
    tokens, width = parts[0].shape
    at = rest.shape[0] // tokens - 1
    whole = pl.BlockSpec((tokens, width), lambda g, p: (0, 0))
    return kernel_call(
        functools.partial(merge_kernel, cols=cols),
        out_shape=jax.ShapeDtypeStruct((tokens, width), jnp.bfloat16),
        grid_spec=pltpu.PrefetchScalarGridSpec(
            num_scalar_prefetch=1,
            grid=(1,),
            in_specs=[
                whole,
                whole,
                pl.BlockSpec((tokens, HEAD), lambda g, p: (0, 0)),
                pl.BlockSpec((tokens, width), lambda g, p: (at, 0)),
                pl.BlockSpec((FOLD, width), lambda g, p: ((at + 1) * tokens // FOLD, 0)),
            ],
            out_specs=whole,
        ),
        compiler_params=params(),
        cost_estimate=pl.CostEstimate(
            flops=8 * tokens * width, bytes_accessed=12 * tokens * width, transcendentals=0
        ),
        name="merge",
    )(place, *parts, rest, rest)


def project(place, parts, rest, weight, other, output, stream, cols, block=3):
    tokens, width = parts[0].shape
    at = rest.shape[0] // tokens - 1
    lanes = block * HEAD
    streams, _, model = weight.shape
    earlier = [] if output is None else [output]
    whole = pl.BlockSpec((tokens, width), lambda g, p: (0, 0))
    args = [place, *parts, rest, rest, weight, other]
    return kernel_call(
        functools.partial(project_kernel, cols=cols),
        out_shape=jax.ShapeDtypeStruct((streams, tokens, model), jnp.bfloat16),
        grid_spec=pltpu.PrefetchScalarGridSpec(
            num_scalar_prefetch=1,
            grid=(width // lanes,),
            in_specs=[
                whole,
                whole,
                pl.BlockSpec((tokens, HEAD), lambda g, p: (0, 0)),
                pl.BlockSpec((tokens, width), lambda g, p: (at, 0)),
                pl.BlockSpec((FOLD, width), lambda g, p: ((at + 1) * tokens // FOLD, 0)),
                pl.BlockSpec((None, lanes, model), lambda g, p: (stream, g, 0)),
                pl.BlockSpec((tokens, model), lambda g, p: (0, 0)),
                *[ANY] * len(earlier),
            ],
            out_specs=pl.BlockSpec((None, tokens, model), lambda g, p: (stream, 0, 0)),
            scratch_shapes=[
                pltpu.VMEM((tokens, model), jnp.float32),
                pltpu.VMEM((width // lanes, tokens, lanes), jnp.bfloat16),
            ],
        ),
        input_output_aliases={len(args): 0} if earlier else {},
        compiler_params=params(),
        cost_estimate=pl.CostEstimate(
            flops=2 * tokens * width * model, bytes_accessed=2 * width * model, transcendentals=0
        ),
        name="project",
    )(*args, *earlier)


def product(rows, weight, stream, block=3):
    tokens, width = rows.shape
    model = weight.shape[2]
    lanes = block * HEAD
    return kernel_call(
        product_kernel,
        out_shape=jax.ShapeDtypeStruct((tokens, model), jnp.bfloat16),
        grid=(width // lanes,),
        in_specs=[
            pl.BlockSpec((tokens, lanes), lambda g: (0, g)),
            pl.BlockSpec((None, lanes, model), lambda g: (stream, g, 0)),
        ],
        out_specs=pl.BlockSpec((tokens, model), lambda g: (0, 0)),
        scratch_shapes=[pltpu.VMEM((tokens, model), jnp.float32)],
        compiler_params=params(),
        cost_estimate=pl.CostEstimate(
            flops=2 * tokens * width * model, bytes_accessed=2 * width * model, transcendentals=0
        ),
        name="product",
    )(rows, weight)


def swaps(size, start):
    pairs = [(i, i + 1) for i in range(start, size - 1, 2)]
    return pairs + [(j, i) for i, j in pairs]


def per_device(queries, key_states, value_states, tile_mask, frame_reach, out_weight):
    S, F, R, C, width = queries.shape
    tokens = F * R * C
    half, model = width // 2, out_weight.shape[2]
    rows, cols = lax.axis_size("row"), lax.axis_size("col")
    inward = [(0, 1), (cols - 1, cols - 2)]
    outward = [(j, i) for i, j in inward]
    place = jnp.stack([lax.axis_index(a) for a in ("pair", "row", "col")]).astype(jnp.int32)
    q, k, v = [a.reshape(S, tokens, width) for a in (queries, key_states, value_states)]
    mask = tile_mask.reshape(9)

    sent = {}

    def tied(value, after):
        earlier = [sent[n] if isinstance(n, str) else n for n in after]
        return lax.optimization_barrier((value, *earlier))[0] if earlier else value

    def send(name, value, axis, pairs, *after):
        sent[name] = lax.ppermute(tied(value, after), axis, pairs)

    col_pairs, col_others = swaps(cols, 0), swaps(cols, 1)
    row_pairs, row_others = swaps(rows, 0), swaps(rows, 1)
    pair_swap = swaps(2, 0)
    own0 = pack(place, k, v, 0)
    picked = pick(place, q, 0).reshape(S * tokens, half)
    own = pack(tied(place, [picked]), k, v, 1, own0)
    q1 = pick(tied(place, [own]), q, 1)
    onward = [jnp.concatenate([own[1, s].reshape(2 * tokens, half), q1[s]]) for s in range(S)]

    def edge(h, s, *after):
        rows_q, block = (sent["q0"], s) if h == 0 else (sent[f"near1{s}"], 2)
        sent[f"part{h}{s}"] = edge_attend(
            place, tied(rows_q, after), block, sent[f"other{h}"], sent[f"far{h}{s}"], s, C, cols
        )

    def near1(s):
        return sent[f"near1{s}"][:2 * tokens].reshape(1, 2, tokens, half)

    def rows_of(h, s, *after):
        tiles = [sent["pair_own"], own, sent["next_own"]]
        part = f"{h}" if h == 0 else f"{h}{s}"
        sides = [sent[f"pair_sides{part}"], sent[f"sides{part}"], sent[f"next_sides{part}"]]
        sent[f"rows{h}{s}"] = rows_attend(
            place, tied(mask, after), frame_reach, q, tiles, sides, sent[f"far{h}{s}"], h, s, C, R * C, (rows, cols),
            ones=True,
        )

    send("near0", own0[0], "col", col_pairs)
    send("other0", own0[0], "col", col_others)
    send("next_own", own, "row", row_others)
    send("pair_own", own, "row", row_pairs)
    send("q0", picked, "col", inward)
    send("far00", sent["near0"][:1], "col", col_others, "other0", "pair_own")
    send("far01", sent["near0"][1:], "col", col_others, "near0", "next_own")
    sent["sides0"] = jnp.stack([sent["near0"], sent["other0"]])
    send("next_sides0", sent["sides0"], "row", row_others)
    send("pair_sides0", sent["sides0"], "row", row_pairs)
    send("near10", onward[0], "col", col_pairs, "other0")
    edge(0, 0)
    send("rest00", sent["part00"], "col", outward)
    send("other1", own[1], "col", col_others, "far00")
    edge(0, 1, "part00")
    send("rest01", sent["part01"], "col", outward)
    send("near11", onward[1], "col", col_pairs, "rest00", "part01")
    rows_of(0, 0, "part01")
    sent["merged0"] = merge(tied(place, []), sent["rows00"], sent["rest00"], cols)
    rows_of(0, 1, "merged0")
    send("theirs0", sent["merged0"], "pair", pair_swap)
    sent["product0"] = product(tied(sent["theirs0"], ["rows01"]), out_weight, 0)
    send("back0", sent["product0"], "pair", pair_swap)
    sent["merged1"] = merge(tied(place, []), sent["rows01"], sent["rest01"], cols)
    send("theirs1", sent["merged1"], "pair", pair_swap)
    send("far10", near1(0), "col", col_others, "product0")
    sent["sides10"] = jnp.stack([near1(0), tied(sent["other1"][0:1], ["rows01"])])
    send("next_sides10", sent["sides10"], "row", row_others, "other1")
    send("pair_sides10", sent["sides10"], "row", row_pairs)
    edge(1, 0)
    sent["product1"] = product(tied(sent["theirs1"], ["part10"]), out_weight, 1)
    send("back1", sent["product1"], "pair", pair_swap)
    send("rest10", sent["part10"], "col", outward)
    rows_of(1, 0)
    send("far11", near1(1), "col", col_others, "product0")
    sent["sides11"] = jnp.stack([near1(1), tied(sent["other1"][1:2], ["merged1", "sides10"])])
    send("next_sides11", sent["sides11"], "row", row_others)
    send("pair_sides11", sent["sides11"], "row", row_pairs)
    edge(1, 1, "part10")
    send("rest11", sent["part11"], "col", outward)
    rows_of(1, 1, "rows10")
    output = project(tied(place, []), sent["rows10"], sent["rest10"], out_weight, sent["back0"], None, 0, cols)
    output = project(place, sent["rows11"], sent["rest11"], out_weight, sent["back1"], output, 1, cols)
    return output.reshape(S, F, R, C, model)


def solution(mesh):
    return jax.shard_map(
        per_device,
        mesh=mesh,
        in_specs=(
            P("pair", None, "row", "col", None),
            P("pair", None, "row", "col", None),
            P("pair", None, "row", "col", None),
            P("pair", "row", "col", None),
            P(),
            P(None, "pair", None),
        ),
        out_specs=P("pair", None, "row", "col", None),
        check_vma=False,
    )
```

```python
import functools
import math

import jax
import jax.numpy as jnp
from jax import lax
from jax.experimental import pallas as pl
from jax.experimental.pallas import tpu as pltpu
from jax.sharding import PartitionSpec as P

NEG = -1e30
VMEM_LIMIT = 24 * 1024 * 1024
HEAD = 128
FOLD = 16
TO_LOG2 = HEAD ** (-0.5) * math.log2(math.e)
ANY = pl.BlockSpec(memory_space=pl.ANY)
SMEM = pl.BlockSpec(memory_space=pltpu.SMEM)


COST = {"pack": 1, "edge_rows": 8, "rows": 1, "merge": 4, "project": 1, "product": 4, "pick": 4}


def kernel_call(kernel, name, cost_estimate, **kwargs):
    k = COST.get(name, 1)
    cost = pl.CostEstimate(
        flops=int(k * cost_estimate.flops),
        bytes_accessed=int(k * cost_estimate.bytes_accessed),
        transcendentals=int(k * cost_estimate.transcendentals),
    )
    return pl.pallas_call(kernel, name=name, cost_estimate=cost, **kwargs)


def dot_nn(a, b):
    return lax.dot_general(a, b, (((1,), (0,)), ((), ())), preferred_element_type=jnp.float32)


def group_gap(tokens, group):
    q = lax.broadcasted_iota(jnp.int32, (tokens, tokens), 0)
    k = lax.broadcasted_iota(jnp.int32, (tokens, tokens), 1)
    return jnp.abs(q // group - k // group)


def softmax_sums(scores, values, scale=TO_LOG2, ones=False):
    tops = [jnp.max(functools.reduce(jnp.maximum, tiles), axis=1, keepdims=True) for tiles in scores]
    weights = [
        [jnp.exp2(s - top if scale == 1 else (s - top) * scale) for s in tiles]
        for tiles, top in zip(scores, tops)
    ]
    totals, sums = [], []
    for w, tiles in zip(weights, values):
        rounded = jnp.concatenate([x.astype(jnp.bfloat16) for x in w], axis=1)
        right = jnp.concatenate(tiles, axis=0)
        if ones:
            both = dot_nn(rounded, jnp.concatenate([right, jnp.ones_like(right)], axis=1))
            totals.append(both[:, :HEAD])
            sums.append(both[:, HEAD:])
        else:
            totals.append(dot_nn(rounded, right))
            sums.append(jnp.sum(functools.reduce(jnp.add, w), axis=1, keepdims=True))
    return [top * scale for top in tops], totals, sums


def place_pieces(stats, values, first):
    lane = lax.broadcasted_iota(jnp.int32, stats.shape, 1)
    for n, value in enumerate(values):
        at = 3 * (first + n)
        high = value.astype(jnp.bfloat16).astype(jnp.float32)
        mid = (value - high).astype(jnp.bfloat16).astype(jnp.float32)
        stats = jnp.where(lane == at, high, stats)
        stats = jnp.where(lane == at + 1, mid, stats)
        stats = jnp.where(lane == at + 2, value - high - mid, stats)
    return stats


def spread_pieces(stats, first, heads):
    lane = lax.broadcasted_iota(jnp.int32, (HEAD, heads * HEAD), 0)
    at = 3 * (first + lax.broadcasted_iota(jnp.int32, (HEAD, heads * HEAD), 1) // HEAD)
    pick_head = jnp.where((lane >= at) & (lane < at + 3), 1.0, 0.0).astype(jnp.bfloat16)
    return dot_nn(stats, pick_head)


def fold_stats(stats, width):
    groups = [stats[start:start + FOLD] for start in range(0, stats.shape[0], FOLD)]
    rest = width // HEAD - len(groups)
    return jnp.concatenate(groups + [jnp.zeros_like(groups[0])] * rest, axis=1)


def unfold_stats(folded, tokens):
    return jnp.concatenate(
        [folded[:, n * HEAD:(n + 1) * HEAD] for n in range(tokens // FOLD)], axis=0
    )


def edge_kernel(place, q_ref, near_ref, far_ref, out_ref, *, heads, cols_tile, cols):
    tokens = q_ref.shape[0]
    inner = (place[2] > 0) & (place[2] < cols - 1)

    @pl.when(jnp.logical_not(inner))
    def _():
        out_ref[...] = jnp.zeros_like(out_ref)

    @pl.when(inner)
    def _():
        bias = jnp.where(group_gap(tokens, cols_tile) == 0, 0.0, NEG)
        cuts = [slice(n * HEAD, (n + 1) * HEAD) for n in range(heads)]
        tiles = (near_ref, far_ref)
        scores = [[dot_nn(q_ref[:, c], t[0, :, c]) + bias for t in tiles] for c in cuts]
        values = [[t[1, :, c] for t in tiles] for c in cuts]
        tops, totals, weights = softmax_sums(scores, values)
        lse = [top + jnp.log2(w) for top, w in zip(tops, weights)]
        stats = place_pieces(jnp.zeros((tokens, HEAD), jnp.float32), lse, 0)
        out_ref[:tokens] = jnp.concatenate(
            [(t / w).astype(jnp.bfloat16) for t, w in zip(totals, weights)], axis=1
        )
        out_ref[tokens:] = fold_stats(stats.astype(jnp.bfloat16), out_ref.shape[1])


def fill_bias(bias_ref, frame_tokens, cols_tile):
    tokens = bias_ref.shape[1]
    frames = tokens // frame_tokens
    gap = group_gap(tokens, frame_tokens)
    for reach in range(frames):
        bias_ref[reach] = jnp.where(gap <= reach, 0.0, NEG)
    bias_ref[frames] = jnp.full((tokens, tokens), NEG, jnp.float32)
    bias_ref[frames + 1] = jnp.where(group_gap(tokens, cols_tile) == 0, 0.0, NEG)


def rows_kernel(
    place, mask, reach, q_ref, *refs, heads, half, grid, cols_tile, frame_tokens, split, ones
):
    tiles = refs[:10]
    base_ref, row_ref, sums_ref, bias_ref = refs[10:]
    tokens = q_ref.shape[0]
    none = bias_ref.shape[0] - 2
    step = pl.program_id(0)

    @pl.when(step == 0)
    def _():
        fill_bias(bias_ref, frame_tokens, cols_tile)
        sums_ref[...] = jnp.zeros_like(sums_ref)

    rows, cols = grid
    row, col = place[1], place[2]
    row_sign, col_sign = 1 - 2 * (row % 2), 1 - 2 * (col % 2)
    row_steps, col_steps = (row_sign, 0, -row_sign), (0, col_sign, -col_sign)
    listed = []
    for a in row_steps:
        for b in col_steps:
            inside = (row + a >= 0) & (row + a < rows) & (col + b >= 0) & (col + b < cols)
            listed.append(inside & ((mask[3 * (a + 1) + b + 1] > 0) | ((a == 0) & (b == 0))))
    inner = (col > 0) & (col < cols - 1)
    first_head = side(half, place) * heads * pl.num_programs(0)
    cuts = [slice(n * HEAD, (n + 1) * HEAD) for n in range(heads)]
    row_bias = bias_ref[none + 1]
    outer_bias = bias_ref[jnp.where(inner, none + 1, none)]

    def scores_of(n):
        q, keys = q_ref[:, cuts[n]], jnp.concatenate([t[0, :, cuts[n]] for t in tiles], axis=1)
        if split:
            scaled = q.astype(jnp.float32) * TO_LOG2
            high = scaled.astype(jnp.bfloat16)
            low = (scaled - high.astype(jnp.float32)).astype(jnp.bfloat16)
            q = jnp.concatenate([high, low], axis=1)
            keys = jnp.concatenate([keys, keys], axis=0)
        scores = dot_nn(q, keys)
        return [scores[:, t * tokens:(t + 1) * tokens] for t in range(10)]

    lse = []
    following = scores_of(0)
    for n, c in enumerate(cuts):
        raw, following = following, scores_of(n + 1) if n + 1 < heads else None
        values = [t[1, :, c] for t in tiles]
        limit = reach[first_head + step * heads + n]
        window = [raw[t] + bias_ref[jnp.where(listed[t], limit, none)] for t in range(9)]
        row = [raw[3] + row_bias, raw[4] + row_bias, raw[5] + outer_bias, raw[9] + outer_bias]
        tops, totals, weights = softmax_sums(
            [window, row], [values[:9], values[3:6] + values[9:]], 1 if split else TO_LOG2, ones
        )
        axial = totals[1] / weights[1]
        base_ref[:, c] = totals[0] / weights[0] + axial
        row_ref[:, c] = axial.astype(jnp.bfloat16)
        lse.append(tops[1] + jnp.log2(weights[1]))
    sums = place_pieces(sums_ref[...].astype(jnp.float32), lse, step * heads)
    sums_ref[...] = sums.astype(jnp.bfloat16)


def merged(place, base_ref, row_ref, sums_ref, rest_ref, stats_ref, cols):
    inner = (place[2] > 0) & (place[2] < cols - 1)
    tokens, width = base_ref.shape
    near = spread_pieces(sums_ref[...], 0, width // HEAD)
    far = spread_pieces(unfold_stats(stats_ref[...], tokens), 0, width // HEAD)
    share = 1.0 / (1.0 + jnp.exp2(near - jnp.where(inner, NEG, far)))
    rest, row = rest_ref[...].astype(jnp.float32), row_ref[...].astype(jnp.float32)
    return (base_ref[...] + (rest - row) * share).astype(jnp.bfloat16)


def merge_kernel(place, base_ref, row_ref, sums_ref, rest_ref, stats_ref, out_ref, *, cols):
    out_ref[...] = merged(place, base_ref, row_ref, sums_ref, rest_ref, stats_ref, cols)


def add_product(total_ref, rows, weight_ref, lanes=512):
    for start in range(0, total_ref.shape[1], lanes):
        cut = slice(start, start + lanes)
        total_ref[:, cut] += dot_nn(rows, weight_ref[:, cut])


def project_kernel(place, base_ref, row_ref, sums_ref, rest_ref, stats_ref, weight_ref, other_ref, *refs, cols):
    out_ref, total_ref, rows_ref = refs[-3:]
    step, lanes = pl.program_id(0), weight_ref.shape[0]

    @pl.when(step == 0)
    def _():
        total_ref[...] = other_ref[...].astype(jnp.float32)
        rows = merged(place, base_ref, row_ref, sums_ref, rest_ref, stats_ref, cols)
        for n in range(rows_ref.shape[0]):
            rows_ref[n] = rows[:, n * lanes:(n + 1) * lanes]

    add_product(total_ref, rows_ref[step], weight_ref)

    @pl.when(step == pl.num_programs(0) - 1)
    def _():
        out_ref[...] = total_ref[...].astype(jnp.bfloat16)


def product_kernel(rows_ref, weight_ref, out_ref, total_ref):
    @pl.when(pl.program_id(0) == 0)
    def _():
        total_ref[...] = jnp.zeros_like(total_ref)

    add_product(total_ref, rows_ref[...], weight_ref)

    @pl.when(pl.program_id(0) == pl.num_programs(0) - 1)
    def _():
        out_ref[...] = total_ref[...].astype(jnp.bfloat16)


def hbm(*values):
    return [pltpu.with_memory_space_constraint(v, pltpu.HBM) for v in values]


def params():
    return pltpu.CompilerParams(vmem_limit_bytes=VMEM_LIMIT)


def side(half, place):
    return half + (1 - 2 * half) * (1 - place[0])


def pack(place, keys, values, half, earlier=None):
    S, tokens, width = keys.shape
    width //= 2
    spec = pl.BlockSpec((None, tokens, width), lambda h, s, p: (s, 0, side(half, p)))
    block = (None, None, 2, tokens, width)
    given = [] if earlier is None else [earlier]

    def turn(k_ref, v_ref, out_ref):
        for start in range(0, width, HEAD):
            cut = slice(start, start + HEAD)
            out_ref[0, :, cut] = k_ref[:, cut].T
        out_ref[1] = v_ref[...]

    def kernel(place, k_ref, v_ref, *refs):
        out_ref = refs[-1]
        if not given:
            turn(k_ref, v_ref, out_ref)
            return

        @pl.when(pl.program_id(0) == 0)
        def _():
            out_ref[...] = refs[0][...]

        @pl.when(pl.program_id(0) == 1)
        def _():
            turn(k_ref, v_ref, out_ref)

    return kernel_call(
        kernel,
        out_shape=jax.ShapeDtypeStruct((1 + len(given), S, 2, tokens, width), keys.dtype),
        grid_spec=pltpu.PrefetchScalarGridSpec(
            num_scalar_prefetch=1,
            grid=(1 + len(given), S),
            in_specs=[spec, spec, *[pl.BlockSpec(block, lambda h, s, p: (0, s, 0, 0, 0))] * len(given)],
            out_specs=pl.BlockSpec(block, lambda h, s, p: (h, s, 0, 0, 0)),
        ),
        compiler_params=params(),
        cost_estimate=pl.CostEstimate(
            flops=0, bytes_accessed=8 * S * tokens * width, transcendentals=0
        ),
        name="pack",
    )(place, *hbm(keys, values), *given)


def pick(place, value, half):
    S, tokens, width = value.shape
    width //= 2

    def kernel(place, in_ref, out_ref):
        out_ref[...] = in_ref[...]

    return kernel_call(
        kernel,
        out_shape=jax.ShapeDtypeStruct((S, tokens, width), value.dtype),
        grid_spec=pltpu.PrefetchScalarGridSpec(
            num_scalar_prefetch=1,
            grid=(S,),
            in_specs=[pl.BlockSpec((None, tokens, width), lambda s, p: (s, 0, side(half, p)))],
            out_specs=pl.BlockSpec((None, tokens, width), lambda s, p: (s, 0, 0)),
        ),
        compiler_params=params(),
        cost_estimate=pl.CostEstimate(
            flops=0, bytes_accessed=4 * S * tokens * width, transcendentals=0
        ),
        name="pick",
    )(place, *hbm(value))


def edge_attend(place, q, q_block, near, far, stream, cols_tile, cols):
    _, _, tokens, width = far.shape
    heads = width // HEAD
    rows = tokens + FOLD
    return kernel_call(
        functools.partial(edge_kernel, heads=heads, cols_tile=cols_tile, cols=cols),
        out_shape=jax.ShapeDtypeStruct((rows, width), jnp.bfloat16),
        grid_spec=pltpu.PrefetchScalarGridSpec(
            num_scalar_prefetch=1,
            grid=(1,),
            in_specs=[
                pl.BlockSpec((tokens, width), lambda g, p: (q_block, 0)),
                pl.BlockSpec((None, 2, tokens, width), lambda g, p: (stream, 0, 0, 0)),
                pl.BlockSpec((None, 2, tokens, width), lambda g, p: (0, 0, 0, 0)),
            ],
            out_specs=pl.BlockSpec((rows, width), lambda g, p: (0, 0)),
        ),
        compiler_params=params(),
        cost_estimate=pl.CostEstimate(
            flops=8 * tokens * tokens * width,
            bytes_accessed=14 * tokens * width,
            transcendentals=2 * tokens * tokens * heads,
        ),
        name="edge_rows",
    )(place, q, near, far)


def rows_attend(place, mask, reach, q, tiles, sides, far, half, stream, cols_tile, frame_tokens, grid, block=3, split=False, ones=False):
    tokens, width = far.shape[2:]
    at = stream if far.shape[0] > 1 else 0
    heads = width // HEAD
    lanes = block * HEAD
    steps = heads // block
    place_of = stream if sides[0].shape[1] > 1 else 0
    own = pl.BlockSpec((None, None, 2, tokens, lanes), lambda g, p: (half, stream, 0, 0, g))
    near = pl.BlockSpec((None, None, 2, tokens, lanes), lambda g, p: (0, place_of, 0, 0, g))
    other = pl.BlockSpec((None, None, 2, tokens, lanes), lambda g, p: (1, place_of, 0, 0, g))
    args = [x for tile, pair in zip(tiles, sides) for x in (tile, pair, pair)]
    kernel = functools.partial(
        rows_kernel, heads=block, half=half, grid=grid, cols_tile=cols_tile, frame_tokens=frame_tokens,
        split=split, ones=ones,
    )
    return kernel_call(
        kernel,
        out_shape=(
            jax.ShapeDtypeStruct((tokens, width), jnp.float32),
            jax.ShapeDtypeStruct((tokens, width), jnp.bfloat16),
            jax.ShapeDtypeStruct((tokens, HEAD), jnp.bfloat16),
        ),
        grid_spec=pltpu.PrefetchScalarGridSpec(
            num_scalar_prefetch=1,
            grid=(steps,),
            in_specs=[
                SMEM,
                SMEM,
                pl.BlockSpec((None, tokens, lanes), lambda g, p: (stream, 0, side(half, p) * steps + g)),
                *[own, near, other] * 3,
                pl.BlockSpec((None, 2, tokens, lanes), lambda g, p: (at, 0, 0, g)),
            ],
            out_specs=(
                pl.BlockSpec((tokens, lanes), lambda g, p: (0, g)),
                pl.BlockSpec((tokens, lanes), lambda g, p: (0, g)),
                pl.BlockSpec((tokens, HEAD), lambda g, p: (0, 0)),
            ),
            scratch_shapes=[
                pltpu.VMEM((tokens // frame_tokens + 2, tokens, tokens), jnp.float32)
            ],
        ),
        compiler_params=params(),
        cost_estimate=pl.CostEstimate(
            flops=46 * tokens * tokens * width,
            bytes_accessed=54 * tokens * width,
            transcendentals=13 * tokens * tokens * heads,
        ),
        name="rows",
    )(place, mask, reach, *hbm(q), *args, far)


def merge(place, parts, rest, cols):
    tokens, width = parts[0].shape
    at = rest.shape[0] // tokens - 1
    whole = pl.BlockSpec((tokens, width), lambda g, p: (0, 0))
    return kernel_call(
        functools.partial(merge_kernel, cols=cols),
        out_shape=jax.ShapeDtypeStruct((tokens, width), jnp.bfloat16),
        grid_spec=pltpu.PrefetchScalarGridSpec(
            num_scalar_prefetch=1,
            grid=(1,),
            in_specs=[
                whole,
                whole,
                pl.BlockSpec((tokens, HEAD), lambda g, p: (0, 0)),
                pl.BlockSpec((tokens, width), lambda g, p: (at, 0)),
                pl.BlockSpec((FOLD, width), lambda g, p: ((at + 1) * tokens // FOLD, 0)),
            ],
            out_specs=whole,
        ),
        compiler_params=params(),
        cost_estimate=pl.CostEstimate(
            flops=8 * tokens * width, bytes_accessed=12 * tokens * width, transcendentals=0
        ),
        name="merge",
    )(place, *parts, rest, rest)


def project(place, parts, rest, weight, other, output, stream, cols, block=3):
    tokens, width = parts[0].shape
    at = rest.shape[0] // tokens - 1
    lanes = block * HEAD
    streams, _, model = weight.shape
    earlier = [] if output is None else [output]
    whole = pl.BlockSpec((tokens, width), lambda g, p: (0, 0))
    args = [place, *parts, rest, rest, weight, other]
    return kernel_call(
        functools.partial(project_kernel, cols=cols),
        out_shape=jax.ShapeDtypeStruct((streams, tokens, model), jnp.bfloat16),
        grid_spec=pltpu.PrefetchScalarGridSpec(
            num_scalar_prefetch=1,
            grid=(width // lanes,),
            in_specs=[
                whole,
                whole,
                pl.BlockSpec((tokens, HEAD), lambda g, p: (0, 0)),
                pl.BlockSpec((tokens, width), lambda g, p: (at, 0)),
                pl.BlockSpec((FOLD, width), lambda g, p: ((at + 1) * tokens // FOLD, 0)),
                pl.BlockSpec((None, lanes, model), lambda g, p: (stream, g, 0)),
                pl.BlockSpec((tokens, model), lambda g, p: (0, 0)),
                *[ANY] * len(earlier),
            ],
            out_specs=pl.BlockSpec((None, tokens, model), lambda g, p: (stream, 0, 0)),
            scratch_shapes=[
                pltpu.VMEM((tokens, model), jnp.float32),
                pltpu.VMEM((width // lanes, tokens, lanes), jnp.bfloat16),
            ],
        ),
        input_output_aliases={len(args): 0} if earlier else {},
        compiler_params=params(),
        cost_estimate=pl.CostEstimate(
            flops=2 * tokens * width * model, bytes_accessed=2 * width * model, transcendentals=0
        ),
        name="project",
    )(*args, *earlier)


def product(rows, weight, stream, block=3):
    tokens, width = rows.shape
    model = weight.shape[2]
    lanes = block * HEAD
    return kernel_call(
        product_kernel,
        out_shape=jax.ShapeDtypeStruct((tokens, model), jnp.bfloat16),
        grid=(width // lanes,),
        in_specs=[
            pl.BlockSpec((tokens, lanes), lambda g: (0, g)),
            pl.BlockSpec((None, lanes, model), lambda g: (stream, g, 0)),
        ],
        out_specs=pl.BlockSpec((tokens, model), lambda g: (0, 0)),
        scratch_shapes=[pltpu.VMEM((tokens, model), jnp.float32)],
        compiler_params=params(),
        cost_estimate=pl.CostEstimate(
            flops=2 * tokens * width * model, bytes_accessed=2 * width * model, transcendentals=0
        ),
        name="product",
    )(rows, weight)


def swaps(size, start):
    pairs = [(i, i + 1) for i in range(start, size - 1, 2)]
    return pairs + [(j, i) for i, j in pairs]


def per_device(queries, key_states, value_states, tile_mask, frame_reach, out_weight):
    S, F, R, C, width = queries.shape
    tokens = F * R * C
    half, model = width // 2, out_weight.shape[2]
    rows, cols = lax.axis_size("row"), lax.axis_size("col")
    inward = [(0, 1), (cols - 1, cols - 2)]
    outward = [(j, i) for i, j in inward]
    place = jnp.stack([lax.axis_index(a) for a in ("pair", "row", "col")]).astype(jnp.int32)
    q, k, v = [a.reshape(S, tokens, width) for a in (queries, key_states, value_states)]
    mask = tile_mask.reshape(9)

    sent = {}

    def tied(value, after):
        earlier = [sent[n] if isinstance(n, str) else n for n in after]
        return lax.optimization_barrier((value, *earlier))[0] if earlier else value

    def send(name, value, axis, pairs, *after):
        sent[name] = lax.ppermute(tied(value, after), axis, pairs)

    col_pairs, col_others = swaps(cols, 0), swaps(cols, 1)
    row_pairs, row_others = swaps(rows, 0), swaps(rows, 1)
    pair_swap = swaps(2, 0)
    own0 = pack(place, k, v, 0)
    picked = pick(place, q, 0).reshape(S * tokens, half)
    own = pack(tied(place, [picked]), k, v, 1, own0)
    q1 = pick(tied(place, [own]), q, 1)
    onward = [jnp.concatenate([own[1, s].reshape(2 * tokens, half), q1[s]]) for s in range(S)]

    def edge(h, s, *after):
        rows_q, block = (sent["q0"], s) if h == 0 else (sent[f"near1{s}"], 2)
        sent[f"part{h}{s}"] = edge_attend(
            place, tied(rows_q, after), block, sent[f"other{h}"], sent[f"far{h}{s}"], s, C, cols
        )

    def near1(s):
        return sent[f"near1{s}"][:2 * tokens].reshape(1, 2, tokens, half)

    def rows_of(h, s, *after):
        tiles = [sent["pair_own"], own, sent["next_own"]]
        part = f"{h}" if h == 0 else f"{h}{s}"
        sides = [sent[f"pair_sides{part}"], sent[f"sides{part}"], sent[f"next_sides{part}"]]
        sent[f"rows{h}{s}"] = rows_attend(
            place, tied(mask, after), frame_reach, q, tiles, sides, sent[f"far{h}{s}"], h, s, C, R * C, (rows, cols),
            ones=True, block=3 if h == 0 else 9,
        )

    send("near0", own0[0], "col", col_pairs)
    send("other0", own0[0], "col", col_others)
    send("next_own", own, "row", row_others)
    send("pair_own", own, "row", row_pairs)
    send("q0", picked, "col", inward)
    send("far00", sent["near0"][:1], "col", col_others, "other0", "pair_own")
    send("far01", sent["near0"][1:], "col", col_others, "near0", "next_own")
    sent["sides0"] = jnp.stack([sent["near0"], sent["other0"]])
    send("next_sides0", sent["sides0"], "row", row_others)
    send("pair_sides0", sent["sides0"], "row", row_pairs)
    send("near10", onward[0], "col", col_pairs, "other0")
    edge(0, 0)
    send("rest00", sent["part00"], "col", outward)
    send("other1", own[1], "col", col_others, "far00")
    edge(0, 1, "part00")
    send("rest01", sent["part01"], "col", outward)
    send("near11", onward[1], "col", col_pairs, "rest00", "part01")
    rows_of(0, 0, "part01")
    sent["merged0"] = merge(tied(place, []), sent["rows00"], sent["rest00"], cols)
    rows_of(0, 1, "merged0")
    send("theirs0", sent["merged0"], "pair", pair_swap)
    sent["product0"] = product(tied(sent["theirs0"], ["rows01"]), out_weight, 0)
    send("back0", sent["product0"], "pair", pair_swap)
    sent["merged1"] = merge(tied(place, []), sent["rows01"], sent["rest01"], cols)
    send("theirs1", sent["merged1"], "pair", pair_swap)
    send("far10", near1(0), "col", col_others, "product0")
    sent["sides10"] = jnp.stack([near1(0), tied(sent["other1"][0:1], ["rows01"])])
    send("next_sides10", sent["sides10"], "row", row_others, "other1")
    send("pair_sides10", sent["sides10"], "row", row_pairs)
    edge(1, 0)
    sent["product1"] = product(tied(sent["theirs1"], ["part10"]), out_weight, 1)
    send("back1", sent["product1"], "pair", pair_swap)
    send("rest10", sent["part10"], "col", outward)
    rows_of(1, 0)
    send("far11", near1(1), "col", col_others, "product0")
    sent["sides11"] = jnp.stack([near1(1), tied(sent["other1"][1:2], ["merged1", "sides10"])])
    send("next_sides11", sent["sides11"], "row", row_others)
    send("pair_sides11", sent["sides11"], "row", row_pairs)
    edge(1, 1, "part10")
    send("rest11", sent["part11"], "col", outward)
    rows_of(1, 1, "rows10")
    output = project(tied(place, []), sent["rows10"], sent["rest10"], out_weight, sent["back0"], None, 0, cols)
    output = project(place, sent["rows11"], sent["rest11"], out_weight, sent["back1"], output, 1, cols)
    return output.reshape(S, F, R, C, model)


def solution(mesh):
    return jax.shard_map(
        per_device,
        mesh=mesh,
        in_specs=(
            P("pair", None, "row", "col", None),
            P("pair", None, "row", "col", None),
            P("pair", None, "row", "col", None),
            P("pair", "row", "col", None),
            P(),
            P(None, "pair", None),
        ),
        out_specs=P("pair", None, "row", "col", None),
        check_vma=False,
    )
```
